256 devices in a mesh: batch: 16 (over z_lo, x, core), seq: 16 (over y, z_hi).
Axes of the slice: x: 4, y: 4, z: 8 (z_hi: 4, z_lo: 2; z = z_hi * 2 + z_lo), core: 2. Of those that a mesh axis runs over, the one named last changes fastest.
Arguments:
- residual: bfloat16 [32768, 4096], P(('batch', 'seq')), may hold values from -25 to 25
- query_proj: bfloat16 [32768, 4096], P(('batch', 'seq')), may hold values from -68 to 68
- key_proj: bfloat16 [32768, 1024], P(('batch', 'seq')), may hold values from -6 to 6
- value_proj: bfloat16 [32768, 1024], P(('batch', 'seq')), may hold values from -6 to 6
- norm_gain: float32 [4096], replicated, may hold values from 0.1 to 1.9
- lengths: int32 [16], P('batch'), may hold values from 512 to 2048, as said below
- positives: int32 [16], replicated, may hold values from 0 to 15, as said below
Outputs:
- batch_loss: float32 [], replicated
- grad_residual: bfloat16 [32768, 4096], P(('batch', 'seq'))
- grad_queries: bfloat16 [32768, 4096], P(('batch', 'seq'))
- grad_keys: bfloat16 [32768, 1024], P(('batch', 'seq'))
- grad_values: bfloat16 [32768, 1024], P(('batch', 'seq'))
The draws below stay inside these ranges and needn't reach their ends.
Inputs may be any that keep to these rules, and one draw needn't show every extreme that they name: `lengths`: in every draw some document has all 2048 slots valid. `positives`: never the document itself.
All inputs are finite; a program needn't handle non-finite values.
Results may differ from the reference program's by a relative error of at most 0.012.
Values may be sent and summed in bfloat16 or wider, within the bound.
A program may use at most 128 MiB of HBM per device.

```python
import math
import jax
import jax.numpy as jnp
from jax import lax

D = 4096
HEADS = 32
KV_HEADS = 8
HEAD_DIM = 128
DOC_LEN = 2048
KVW = 1024
TOKENS = 32768
DOCS = 16
GRAD_SCALE = 32768
N_SEQ = 16


def shared_keys(key):
    normal_part = jax.random.normal(key, (TOKENS, KVW), jnp.float32)
    return 1.4 * jnp.clip(normal_part, -4.0, 4.0)


def log_scales(key, shape):
    return jnp.exp(jax.random.uniform(key, shape, jnp.float32) * jnp.log(10.0))


def draw_key_proj(key, part):
    key_rows = shared_keys(key)
    return key_rows.astype(jnp.bfloat16)


def draw_query_proj(key, part):
    key = jax.random.fold_in(key, 5)
    normal_part = 1.4 * jnp.clip(jax.random.normal(key, (TOKENS, D), jnp.float32), -4.0, 4.0)
    return normal_part.astype(jnp.bfloat16)


def draw_residual(key, part):
    key = jax.random.fold_in(key, 7)
    noise_key, row_key, col_key = jax.random.split(key, 3)
    row_scale = log_scales(row_key, (TOKENS, 1))
    col_scale = log_scales(col_key, (1, D))
    noise_part = jnp.clip(jax.random.normal(noise_key, (TOKENS, D), jnp.float32), -4.0, 4.0)
    return (0.06 * row_scale * col_scale * noise_part).astype(jnp.bfloat16)


def draw_lengths(key, part):
    key = jax.random.fold_in(key, 11)
    length_key, full_key = jax.random.split(key, 2)
    drawn = jax.random.randint(length_key, (DOCS,), DOC_LEN // 4, DOC_LEN + 1, jnp.int32)
    full_doc = jax.random.randint(full_key, (), 0, DOCS, jnp.int32)
    return jnp.where(jnp.arange(DOCS, dtype=jnp.int32) == full_doc, DOC_LEN, drawn).astype(jnp.int32)


def draw_positives(key, part):
    key = jax.random.fold_in(key, 13)
    offset = jax.random.randint(key, (DOCS,), 1, DOCS, jnp.int32)
    doc_ids = jnp.arange(DOCS, dtype=jnp.int32)
    drawn = (doc_ids + offset) % DOCS
    drawn = jnp.where(doc_ids == 0, DOCS - 1, drawn)
    drawn = jnp.where(doc_ids == DOCS - 1, 0, drawn)
    return drawn.astype(jnp.int32)


def steps_of(key, extent, pieces, smallest, high):
    def one(dim, shards_of):
        steps = jax.random.uniform(jax.random.fold_in(jax.random.fold_in(key, 6), dim), (shards_of,), jnp.float32, smallest / len(pieces), high / len(pieces))
        return jnp.repeat(jnp.exp(steps), extent[dim] // shards_of).reshape((-1,) + (1,) * (len(extent) - dim - 1))

    factor_of = one(*pieces[0])
    for cut in pieces[1:]:
        factor_of = factor_of * one(*cut)
    return factor_of


def noise(rng, dims, width, reach, shards=(), kind=jnp.bfloat16):
    values = jax.random.normal(rng, dims, jnp.float32) * width
    if len(shards) > 0:
        values = steps_of(rng, dims, shards, -0.22, 0.18) * values
    return jnp.clip(values, min=-reach, max=reach).astype(kind)


def setup_inputs(seed: int = 0) -> dict:
    seeds = jax.random.split(jax.random.key(seed), 8)
    return {
        "residual": draw_residual(jax.random.fold_in(seeds[7], 71), 0),
        "query_proj": draw_query_proj(jax.random.fold_in(seeds[7], 71), 0),
        "key_proj": draw_key_proj(jax.random.fold_in(seeds[7], 71), 0),
        "value_proj": noise(seeds[3], (TOKENS, KVW), 1.0, 6.0, ((0, 256),)),
        "norm_gain": jnp.clip(1.0 + 0.18 * jax.random.normal(seeds[4], (D,), jnp.float32), 0.1, 1.9),
        "lengths": draw_lengths(jax.random.fold_in(seeds[7], 71), 0),
        "positives": draw_positives(jax.random.fold_in(seeds[7], 71), 0),
    }


TEMP_FACTOR = 10.0
BIAS_SHIFT = -2.0
EPSILON = 1e-06

def siglip_loss(embedding, positives):
    squares = lax.optimization_barrier(jnp.sum(embedding * embedding, axis=-1, keepdims=True))
    unit_rows = embedding * lax.rsqrt(squares + EPSILON)
    similar = jnp.dot(unit_rows, unit_rows.T, precision=lax.Precision.HIGHEST, preferred_element_type=jnp.float32)
    logits = TEMP_FACTOR * similar + BIAS_SHIFT
    doc_count = embedding.shape[0]
    labels = jnp.arange(doc_count, dtype=jnp.int32)
    label_signs = jnp.where(labels[None, :] == positives[:, None], 1.0, -1.0).astype(jnp.float32)
    others = labels[None, :] != labels[:, None]
    pair_terms = jnp.where(others, jax.nn.softplus(-label_signs * logits), 0.0)
    return jnp.sum(pair_terms) / doc_count

def head_probs(query_rows, key_rows, valid_mask, factor):
    scores = jnp.einsum('qhd,khd->hqk', query_rows, key_rows, precision=lax.Precision.HIGHEST) * factor
    masked = jnp.where(valid_mask[None, None, :], scores, -jnp.inf)
    row_peak = lax.optimization_barrier(jnp.max(masked, axis=-1, keepdims=True))
    raw_weights = jnp.where(valid_mask[None, None, :], jnp.exp(scores - row_peak), 0.0)
    return (raw_weights / lax.optimization_barrier(jnp.sum(raw_weights, axis=-1, keepdims=True))).astype(jnp.bfloat16)

def reference(residual, query_proj, key_proj, value_proj, norm_gain, lengths, positives):
    group_size = HEADS // KV_HEADS
    copies = N_SEQ // KV_HEADS
    local_heads = HEADS // N_SEQ
    factor = 1.0 / math.sqrt(HEAD_DIM)
    doc_count = lengths.shape[0]
    query_docs = query_proj.reshape(doc_count, DOC_LEN, HEADS, HEAD_DIM)
    key_docs = key_proj.reshape(doc_count, DOC_LEN, KV_HEADS, HEAD_DIM)
    value_docs = value_proj.reshape(doc_count, DOC_LEN, KV_HEADS, HEAD_DIM)
    positions = jnp.arange(DOC_LEN, dtype=jnp.int32)
    valid_docs = positions[None, :] < lengths[:, None]

    def widen_heads(block):
        return jnp.repeat(block.astype(jnp.float32), group_size, axis=1)

    def forward_doc(inputs):
        query_rows, key_rows, value_rows, valid_mask = inputs
        weights = head_probs(query_rows.astype(jnp.float32), widen_heads(key_rows), valid_mask, factor)
        attended = jnp.einsum('hqk,khd->qhd', weights.astype(jnp.float32), widen_heads(value_rows), precision=lax.Precision.HIGHEST)
        return attended.astype(jnp.bfloat16)
    attended = lax.map(forward_doc, (query_docs, key_docs, value_docs, valid_docs)).reshape(-1, D)
    summed = residual.astype(jnp.float32) + attended.astype(jnp.float32)
    inv_rms = lax.rsqrt(lax.optimization_barrier(jnp.mean(summed * summed, axis=-1, keepdims=True)) + EPSILON)
    scaled_rows = summed * inv_rms
    normed = scaled_rows * norm_gain
    valid_flat = valid_docs.reshape(-1, 1)
    len_float = lengths.astype(jnp.float32)
    pooled_sum = lax.optimization_barrier(jnp.sum(jnp.where(valid_flat, normed, 0.0).reshape(doc_count, DOC_LEN, D), axis=1))
    embedding = pooled_sum / len_float[:, None]
    batch_loss, pullback = jax.vjp(lambda emb_rows: siglip_loss(emb_rows, positives), embedding)
    grad_embedding, = pullback(jnp.ones((), jnp.float32) * GRAD_SCALE)
    grad_normed = jnp.where(valid_flat, jnp.repeat(grad_embedding / len_float[:, None], DOC_LEN, axis=0), 0.0)
    gained = grad_normed * norm_gain
    grad_summed = inv_rms * (gained - scaled_rows * lax.optimization_barrier(jnp.mean(gained * scaled_rows, axis=-1, keepdims=True)))
    grad_residual = grad_summed.astype(jnp.bfloat16)
    grad_docs = grad_residual.reshape(doc_count, DOC_LEN, HEADS, HEAD_DIM)

    def fold_parts(per_head):
        parts = per_head.reshape(DOC_LEN, KV_HEADS, copies, local_heads, HEAD_DIM).sum(axis=3).astype(jnp.bfloat16)
        return parts.astype(jnp.float32).sum(axis=2).astype(jnp.bfloat16)

    def backward_doc(inputs):
        query_rows, key_rows, value_rows, valid_mask, grad_rows = inputs
        query_float = query_rows.astype(jnp.float32)
        key_wide = widen_heads(key_rows)
        value_wide = widen_heads(value_rows)
        weights = head_probs(query_float, key_wide, valid_mask, factor)
        weight_float = weights.astype(jnp.float32)
        grad_float = grad_rows.astype(jnp.float32)
        grad_weights = jnp.einsum('qhd,khd->hqk', grad_float, value_wide, precision=lax.Precision.HIGHEST)
        row_dot = lax.optimization_barrier(jnp.sum(weight_float * grad_weights, axis=-1, keepdims=True))
        grad_scores = (weight_float * (grad_weights - row_dot) * factor).astype(jnp.bfloat16)
        score_float = grad_scores.astype(jnp.float32)
        grad_query = jnp.einsum('hqk,khd->qhd', score_float, key_wide, precision=lax.Precision.HIGHEST).astype(jnp.bfloat16)
        key_heads = jnp.einsum('hqk,qhd->khd', score_float, query_float, precision=lax.Precision.HIGHEST)
        value_heads = jnp.einsum('hqk,qhd->khd', weight_float, grad_float, precision=lax.Precision.HIGHEST)
        return (grad_query, fold_parts(key_heads), fold_parts(value_heads))
    grad_query, grad_key, grad_value = lax.map(backward_doc, (query_docs, key_docs, value_docs, valid_docs, grad_docs))
    return (batch_loss, grad_residual, grad_query.reshape(-1, D), grad_key.reshape(-1, KVW), grad_value.reshape(-1, KVW))
```

```python
import functools
import math

import jax
import jax.numpy as jnp
from jax import lax
from jax.experimental import pallas as pl
from jax.experimental.pallas import tpu as pltpu
from jax.sharding import PartitionSpec as P

MESH = pl.DeviceIdType.MESH
HD = 128
NY = 4
NZ = 4
H = 2
G = 4
GW = G * HD
EPS = 1e-6
F32 = jnp.float32
BF16 = jnp.bfloat16
FACTOR = 1.0 / math.sqrt(HD)
LOG2E_FACTOR = FACTOR * math.log2(math.e)


def dot(a, b, dims=((1,), (0,))):
    return lax.dot_general(a, b, (dims, ((), ())), preferred_element_type=F32)


def kernel(
    nb, t_rows,
    len_ref, pos_ref, res_hbm, q_hbm, k_hbm, v_hbm, gain_ref,
    loss_ref, out_gr, out_gq, out_gk, out_gv,
    kvb, kfx, kzt, vta, qin, qs, qt, est, mb, mrun, linv, acc, ato, ati, res, sm,
    pp, ppa, emba, gref, gro, doi, dot_t, dqa, gqo, dka, dva, dkvo, own, rs1, rs2, fin,
    kvs, kvr, kvl, qss, qsr, qsl, z1s, z1r, z2s, z2r, ats, atr, atl, resl,
    p1s, p1r, p2s, p2r, grs, grr, grl, gol, r1s, r1r, r2s, r2r, gqs, gqr, gql, gks, gkr, gkl,
):
    T = t_rows
    BK = NY * T
    ns = NY * NZ
    b = lax.axis_index("batch")
    s = lax.axis_index("seq")
    y = lax.div(s, NZ)
    zh = lax.rem(s, NZ)
    zr = lax.rem(zh + 1, NZ)
    zl = lax.rem(zh + NZ - 1, NZ)
    right = (b, y * NZ + zr)
    left = (b, y * NZ + zl)

    def yo(k):
        return lax.rem(y + k, NY)

    def ydev(yy):
        return (b, yy * NZ + zh)

    def col(index, width):
        return pl.ds(pl.multiple_of(index * width, width), width)

    def rcopy(src, dst, ssem, rsem, dev):
        return pltpu.make_async_remote_copy(
            src_ref=src, dst_ref=dst, send_sem=ssem, recv_sem=rsem, device_id=dev, device_id_type=MESH
        )

    def lcopy(src, dst, sem):
        return pltpu.make_async_copy(src, dst, sem)

    def await_ref(ref, sem):
        pltpu.make_async_copy(ref, ref, sem).wait()

    sends = []

    def send(src, dst, ssem, rsem, dev):
        copy = rcopy(src, dst, ssem, rsem, dev)
        copy.start()
        sends.append(copy)

    length = len_ref[0]
    lenf = length.astype(F32)

    res_copy = lcopy(res_hbm, res, resl)
    res_copy.start()
    for h in range(H):
        for c, src in ((0, k_hbm), (1, v_hbm)):
            lcopy(src.at[:, col(2 * y + h, HD)], kvb.at[h, 0, c, y], kvl.at[h, c]).start()
        lcopy(q_hbm.at[:, col(2 * y + h, GW)], qin.at[h, y], qsl.at[h]).start()

    barrier = pltpu.get_barrier_semaphore()
    for k in range(1, ns):
        pl.semaphore_signal(barrier, inc=1, device_id=(b, lax.rem(s + k, ns)), device_id_type=MESH)
    for k in range(1, nb):
        pl.semaphore_signal(barrier, inc=1, device_id=(lax.rem(b + k, nb), s), device_id_type=MESH)
    pl.semaphore_wait(barrier, ns - 1 + nb - 1)

    for h in range(H):
        for k in (1, 3, 2):
            yy = yo(k)
            for c, src in ((0, k_hbm), (1, v_hbm)):
                send(src.at[:, col(2 * yy + h, HD)], kvb.at[h, 0, c, y], kvs.at[h, c, k - 1], kvr.at[h, c, k - 1], ydev(yy))
    for h in range(H):
        for k in (1, 3, 2):
            yy = yo(k)
            send(q_hbm.at[:, col(2 * yy + h, GW)], qin.at[h, y], qss.at[h, k - 1], qsr.at[h, k - 1], ydev(yy))

    for h in range(H):
        for k in (0, 1, 3, 2):
            p = yo(NY - k)
            for c, src in ((0, k_hbm), (1, v_hbm)):
                if k == 0:
                    lcopy(src.at[:, col(2 * y + h, HD)], kvb.at[h, 0, c, y], kvl.at[h, c]).wait()
                else:
                    await_ref(kvb.at[h, 0, c, p], kvr.at[h, c, k - 1])
            send(kvb.at[h, 0, :, p], kvb.at[h, 1, :, p], z1s.at[h, 0, k], z1r.at[h, 0, k], right)
            send(kvb.at[h, 0, :, p], kvb.at[h, 2, :, p], z1s.at[h, 1, k], z1r.at[h, 1, k], left)

    def hop2(h, way):
        src, dev, piece = (1, right, 0) if way == 0 else (2, left, 2)
        return rcopy(
            kvb.at[h, src, :, pl.ds(piece, 2)], kvb.at[h, 3, :, pl.ds(piece, 2)], z2s.at[h, way], z2r.at[h, way], dev
        )

    def att_send(h, kk):
        yy = yo(kk)
        return rcopy(ato.at[h, yy], ati.at[h, y], ats.at[h, kk - 1], atr.at[h, kk - 1], ydev(yy))

    def fwd_step(step, carry):
        rel = lax.div(step, H)
        h = lax.rem(step, H)

        @pl.when(rel == 0)
        def _():
            for k in range(NY):
                if k == 0:
                    lcopy(q_hbm.at[:, col(2 * y + h, GW)], qin.at[h, y], qsl.at[h]).wait()
                else:
                    await_ref(qin.at[h, yo(NY - k)], qsr.at[h, k - 1])

            def prep_q(yy, carry):
                for j in range(G):
                    head = qin[h, yy, :, j * HD : (j + 1) * HD]
                    qs[h, yy, j * T : (j + 1) * T, :] = head
                    qt[h, yy, :, j * T : (j + 1) * T] = head.astype(F32).T.astype(BF16)
                mrun[h, yy] = jnp.full((1, G * T), -3e38, F32)
                acc[h, yy] = jnp.zeros((HD + 16, G * T), F32)
                return carry

            lax.fori_loop(0, NY, prep_q, 0)

        @pl.when(rel == 1)
        def _():
            for k in range(NY):
                await_ref(kvb.at[h, 1, :, yo(NY - k)], z1r.at[h, 0, k])
            hop2(h, 0).start()

        @pl.when(rel == 2)
        def _():
            for k in range(NY):
                await_ref(kvb.at[h, 2, :, yo(NY - k)], z1r.at[h, 1, k])
            hop2(h, 1).start()

        @pl.when(rel == 3)
        def _():
            await_ref(kvb.at[h, 3, :, pl.ds(0, 2)], z2r.at[h, 0])
            await_ref(kvb.at[h, 3, :, pl.ds(2, 2)], z2r.at[h, 1])

        zb = lax.rem(zh + jnp.where(rel == 0, 0, jnp.where(rel == 1, 3, jnp.where(rel == 2, 1, 2))), NZ)
        first_key = kvb[h, rel, 0, 0, 0:1, :].astype(F32)
        for yy in range(NY):
            base = (yy * NZ + zb) * T
            valid = lax.broadcasted_iota(jnp.int32, (T, HD), 0) + base < length
            rows = slice(yy * T, (yy + 1) * T)
            kp = kvb[h, rel, 0, yy].astype(F32)
            vp = kvb[h, rel, 1, yy].astype(F32)
            kfx[h, rel, rows, :] = jnp.where(valid, kp, first_key).astype(BF16)
            kzt[h, rel, :, rows] = jnp.where(valid, kp, 0.0).T.astype(BF16)
            vta[h, rel, 0:HD, rows] = jnp.where(valid, vp, 0.0).T.astype(BF16)
            lanes = lax.broadcasted_iota(jnp.int32, (16, T), 1) + base < length
            vta[h, rel, HD : HD + 16, rows] = jnp.where(lanes, 1.0, 0.0).astype(BF16)

        def chunk(t, carry):
            kk = lax.rem(t + 1, NY)
            yy = yo(kk)
            half = G * T // 2
            for part in range(2):
                lanes = slice(part * half, (part + 1) * half)
                sc = dot(kfx[h, rel], qt[h, yy, :, lanes])
                m = jnp.max(sc, axis=0, keepdims=True)
                e = jnp.exp2((sc - m) * LOG2E_FACTOR).astype(BF16)
                est[h, rel, yy, :, lanes] = e
                mb[h, rel, yy, :, lanes] = m
                o = dot(vta[h, rel], e)
                mo = mrun[h, yy, :, lanes]
                mn = jnp.maximum(mo, m)
                keep = jnp.exp2((mo - mn) * LOG2E_FACTOR)
                add = jnp.exp2((m - mn) * LOG2E_FACTOR)
                acc[h, yy, :, lanes] = acc[h, yy, :, lanes] * keep + o * add
                mrun[h, yy, :, lanes] = mn

            @pl.when(rel == 3)
            def _():
                li = 1.0 / acc[h, yy, HD : HD + 1, :]
                linv[h, yy] = li
                o = acc[h, yy, 0:HD, :] * li
                acc[h, yy, 0:HD, :] = o
                for j in range(G):
                    ato[h, yy, :, j * HD : (j + 1) * HD] = o[:, j * T : (j + 1) * T].T.astype(BF16)

                @pl.when(kk > 0)
                def _():
                    att_send(h, kk).start()

                @pl.when(kk == 0)
                def _():
                    lcopy(ato.at[h, y], ati.at[h, y], atl.at[h]).start()

            return carry

        lax.fori_loop(0, NY, chunk, 0)
        return carry

    lax.fori_loop(0, NZ * H, fwd_step, 0)

    res_copy.wait()
    for h in range(H):
        lcopy(ato.at[h, y], ati.at[h, y], atl.at[h]).wait()
        for k in range(1, NY):
            await_ref(ati.at[h, yo(NY - k)], atr.at[h, k - 1])
    square = jnp.zeros((T, HD), F32)
    for g in range(NY * H):
        x = res[:, g * GW : (g + 1) * GW].astype(F32) + ati[g % H, g // H].astype(F32)
        sm[g] = x
        x = x * x
        for j in range(G):
            square = square + x[:, j * HD : (j + 1) * HD]
    inv = lax.rsqrt(jnp.sum(square, axis=1, keepdims=True) * (1.0 / (NY * H * GW)) + EPS)
    valid_row = lax.broadcasted_iota(jnp.int32, (T, GW), 0) + s * T < length
    for g in range(NY * H):
        scaled = sm[g] * inv
        sm[g] = scaled
        normed = scaled * gain_ref[0:1, g * GW : (g + 1) * GW]
        pp[g : g + 1, :] = jnp.sum(jnp.where(valid_row, normed, 0.0), axis=0, keepdims=True) / lenf

    for k in range(1, ns):
        send(pp, ppa.at[s], p1s.at[k - 1], p1r.at[k - 1], (b, lax.rem(s + k, ns)))
    ppa[s] = pp[...]
    for k in range(1, ns):
        await_ref(ppa.at[lax.rem(s + ns - k, ns)], p1r.at[k - 1])
    mine = ppa[0]
    for i in range(1, ns):
        mine = mine + ppa[i]
    emba[b] = mine
    for k in range(1, nb):
        send(emba.at[b], emba.at[b], p2s.at[k - 1], p2r.at[k - 1], (lax.rem(b + k, nb), s))
    for k in range(1, nb):
        await_ref(emba.at[lax.rem(b + nb - k, nb)], p2r.at[k - 1])

    doc_ids = lax.broadcasted_iota(jnp.int32, (nb, HD), 0)

    def fold(x):
        return x[:, 0:HD] + x[:, HD : 2 * HD] + x[:, 2 * HD : 3 * HD] + x[:, 3 * HD :]

    def dots(row):
        out = jnp.zeros((nb, HD), F32)
        for j in range(nb):
            prod = jnp.sum(fold(emba[j] * (emba[j] if row is None else row)), axis=0, keepdims=True)
            out = jnp.where(doc_ids == j, prod, out)
        return jnp.broadcast_to(jnp.sum(out, axis=1, keepdims=True), (nb, HD))

    posv = jnp.zeros((nb, HD), jnp.int32)
    for j in range(nb):
        posv = jnp.where(doc_ids == j, pos_ref[j], posv)
    rho = lax.rsqrt(dots(None) + EPS)

    def own_rho(row):
        total = jnp.sum(jnp.sum(fold(row * row), axis=0, keepdims=True), axis=1, keepdims=True)
        return jnp.broadcast_to(lax.rsqrt(total + EPS), (nb, HD))

    row_rho = own_rho(mine)
    sims = dots(mine) * rho * row_rho
    logits = 10.0 * sims - 2.0

    def pull(sign):
        return -10.0 / nb * sign / (1.0 + jnp.exp(sign * logits))

    pair = pull(jnp.where(doc_ids == pos_ref[b], 1.0, -1.0)) + pull(jnp.where(posv == b, 1.0, -1.0))
    pair = jnp.where(doc_ids == b, 0.0, pair) * (16.0 * ns * T)
    coef = pair * rho * row_rho
    self_coef = row_rho * row_rho * jnp.broadcast_to(jnp.sum(pair * sims, axis=0, keepdims=True), (nb, HD))
    grad = -self_coef[0:1, 0:1] * mine
    for j in range(nb):
        grad = grad + coef[j : j + 1, 0:1] * emba[j]
    gref[...] = grad / lenf

    total = jnp.zeros((T, HD), F32)
    for g in range(NY * H):
        x = sm[g] * (gref[g : g + 1, :] * gain_ref[0:1, g * GW : (g + 1) * GW])
        for j in range(G):
            total = total + x[:, j * HD : (j + 1) * HD]
    mean = jnp.sum(total, axis=1, keepdims=True) * (1.0 / (NY * H * GW))
    for g in range(NY * H):
        gained = gref[g : g + 1, :] * gain_ref[0:1, g * GW : (g + 1) * GW]
        out = jnp.where(valid_row, inv * (gained - sm[g] * mean), 0.0).astype(BF16)
        gro[g % H, g // H] = out
        lcopy(gro.at[g % H, g // H], out_gr.at[:, g * GW : (g + 1) * GW], gol.at[g]).start()
    for h in range(H):
        for k in (1, 3, 2):
            yy = yo(k)
            send(gro.at[h, yy], doi.at[h, y], grs.at[h, k - 1], grr.at[h, k - 1], ydev(yy))
        lcopy(gro.at[h, y], doi.at[h, y], grl.at[h]).start()

    def r1(h, way):
        dev, piece = (right, 0) if way == 0 else (left, 2)
        return rcopy(dkvo.at[h, 2, :, pl.ds(piece, 2)], rs1.at[h, way], r1s.at[h, way], r1r.at[h, way], dev)

    def r2(h, way):
        dev = right if way == 0 else left
        return rcopy(dkvo.at[h, 1 - way], rs2.at[h, way], r2s.at[h, way], r2r.at[h, way], dev)

    def gq_send(h, kk):
        yy = yo(kk)
        return rcopy(gqo.at[h, yy], out_gq.at[:, col(2 * y + h, GW)], gqs.at[h, kk - 1], gqr.at[h, kk - 1], ydev(yy))

    def gq_local(h):
        return lcopy(gqo.at[h, y], out_gq.at[:, col(2 * y + h, GW)], gql.at[h])

    def bwd_step(step, carry):
        rel = NZ - 1 - lax.div(step, H)
        h = lax.rem(step, H)

        @pl.when(rel == 3)
        def _():
            lcopy(gro.at[h, y], doi.at[h, y], grl.at[h]).wait()
            for k in range(1, NY):
                await_ref(doi.at[h, yo(NY - k)], grr.at[h, k - 1])

            def prep_g(yy, carry):
                for j in range(G):
                    dot_t[h, yy, :, j * T : (j + 1) * T] = doi[h, yy, :, j * HD : (j + 1) * HD].astype(F32).T
                dqa[h, yy] = jnp.zeros((HD, G * T), F32)
                return carry

            lax.fori_loop(0, NY, prep_g, 0)

        dka[...] = jnp.zeros((BK, HD), F32)
        dva[...] = jnp.zeros((BK, HD), F32)

        def chunk(t, carry):
            kk = lax.rem(t + 1, NY)
            yy = yo(kk)
            vals = kvb[h, rel, 1].reshape(BK, HD)
            half = G * T // 2
            for part in range(2):
                lanes = slice(part * half, (part + 1) * half)
                r = jnp.exp2((mb[h, rel, yy, :, lanes] - mrun[h, yy, :, lanes]) * LOG2E_FACTOR) * linv[h, yy, :, lanes]
                do = (dot_t[h, yy, :, lanes] * r).astype(BF16)
                delta = jnp.sum(do.astype(F32) * acc[h, yy, 0:HD, lanes], axis=0, keepdims=True)
                e = est[h, rel, yy, :, lanes]
                dp = dot(vals, do)
                ds = (e.astype(F32) * (dp - delta)).astype(BF16)
                dva[...] += dot(e, do, ((1,), (1,)))
                dka[...] += dot(ds, qs[h, yy, lanes, :])
                dqa[h, yy, :, lanes] += dot(kzt[h, rel], ds)

            @pl.when(rel == 0)
            def _():
                for j in range(G):
                    part = dqa[h, yy, :, j * T : (j + 1) * T] * FACTOR
                    gqo[h, yy, :, j * HD : (j + 1) * HD] = part.T.astype(BF16)

                @pl.when(kk > 0)
                def _():
                    gq_send(h, kk).start()

                @pl.when(kk == 0)
                def _():
                    gq_local(h).start()

            return carry

        lax.fori_loop(0, NY, chunk, 0)

        def store(slot, added):
            for c, ref in ((0, dka), (1, dva)):
                for p in range(NY):
                    x = ref[p * T : (p + 1) * T, :]
                    if c == 0:
                        x = x * FACTOR
                    if added is not None and p // 2 == added:
                        x = x + rs1[h, added, c, p % 2].astype(F32)
                    dkvo[h, slot, c, p] = x.astype(BF16)

        @pl.when(rel == 3)
        def _():
            store(2, None)
            r1(h, 0).start()
            r1(h, 1).start()

        @pl.when(rel == 2)
        def _():
            await_ref(rs1.at[h, 0], r1r.at[h, 0])
            store(1, 0)
            r2(h, 0).start()

        @pl.when(rel == 1)
        def _():
            await_ref(rs1.at[h, 1], r1r.at[h, 1])
            store(0, 1)
            r2(h, 1).start()

        @pl.when(rel == 0)
        def _():
            own[h, 0] = dka[...] * FACTOR
            own[h, 1] = dva[...]

        return carry

    lax.fori_loop(0, NZ * H, bwd_step, 0)

    def loss_row(i, total):
        row = emba[i]
        logit = 10.0 * (dots(row) * rho * own_rho(row)) - 2.0
        x = jnp.where(doc_ids == pos_ref[i], -logit, logit)
        term = jnp.maximum(x, 0.0) + jnp.log(1.0 + jnp.exp(-jnp.abs(x)))
        return total + jnp.where(doc_ids == i, 0.0, term)

    terms = lax.fori_loop(0, nb, loss_row, jnp.zeros((nb, HD), F32))
    loss_ref[0, 0] = jnp.sum(terms) * (1.0 / (HD * nb))

    for h in range(H):
        await_ref(rs2.at[h, 0], r2r.at[h, 0])
        await_ref(rs2.at[h, 1], r2r.at[h, 1])
        for p in range(NY):
            valid = lax.broadcasted_iota(jnp.int32, (T, HD), 0) + (p * NZ + zh) * T < length
            for c in range(2):
                x = own[h, c, p * T : (p + 1) * T, :] + rs2[h, 0, c, p].astype(F32) + rs2[h, 1, c, p].astype(F32)
                fin[h, c, p] = jnp.where(valid, x, 0.0).astype(BF16)
        for c, out in ((0, out_gk), (1, out_gv)):
            for k in (1, 3, 2):
                yy = yo(k)
                send(fin.at[h, c, yy], out.at[:, col(2 * y + h, HD)], gks.at[h, c, k - 1], gkr.at[h, c, k - 1], ydev(yy))
            lcopy(fin.at[h, c, y], out.at[:, col(2 * y + h, HD)], gkl.at[h, c]).start()

    for g in range(NY * H):
        lcopy(gro.at[g % H, g // H], out_gr.at[:, g * GW : (g + 1) * GW], gol.at[g]).wait()
    for h in range(H):
        gq_local(h).wait()
        for k in range(1, NY):
            await_ref(out_gq.at[:, col(2 * yo(NY - k) + h, GW)], gqr.at[h, k - 1])
        for c, out in ((0, out_gk), (1, out_gv)):
            lcopy(fin.at[h, c, y], out.at[:, col(2 * y + h, HD)], gkl.at[h, c]).wait()
            for k in range(1, NY):
                await_ref(out.at[:, col(2 * yo(NY - k) + h, HD)], gkr.at[h, c, k - 1])
    for copy in sends:
        copy.wait_send()
    for h in range(H):
        for way in range(2):
            hop2(h, way).wait_send()
            r1(h, way).wait_send()
            r2(h, way).wait_send()
        for k in range(1, NY):
            att_send(h, k).wait_send()
            gq_send(h, k).wait_send()


def on_device(nb, residual, query_proj, key_proj, value_proj, norm_gain, lengths, positives):
    T, D = residual.shape
    ns = NY * NZ
    BK, QC = NY * T, G * T
    V = pltpu.VMEM
    S = pltpu.SemaphoreType.DMA
    scratch = [
        V((H, NZ, 2, NY, T, HD), BF16),
        V((H, NZ, BK, HD), BF16),
        V((H, NZ, HD, BK), BF16),
        V((H, NZ, HD + 16, BK), BF16),
        V((H, NY, T, GW), BF16),
        V((H, NY, QC, HD), BF16),
        V((H, NY, HD, QC), BF16),
        V((H, NZ, NY, BK, QC), BF16),
        V((H, NZ, NY, 1, QC), F32),
        V((H, NY, 1, QC), F32),
        V((H, NY, 1, QC), F32),
        V((H, NY, HD + 16, QC), F32),
        V((H, NY, T, GW), BF16),
        V((H, NY, T, GW), BF16),
        V((T, D), BF16),
        V((NY * H, T, GW), F32),
        V((NY * H, GW), F32),
        V((ns, NY * H, GW), F32),
        V((nb, NY * H, GW), F32),
        V((NY * H, GW), F32),
        V((H, NY, T, GW), BF16),
        V((H, NY, T, GW), BF16),
        V((H, NY, HD, QC), F32),
        V((H, NY, HD, QC), F32),
        V((H, NY, T, GW), BF16),
        V((BK, HD), F32),
        V((BK, HD), F32),
        V((H, 3, 2, NY, T, HD), BF16),
        V((H, 2, BK, HD), F32),
        V((H, 2, 2, 2, T, HD), BF16),
        V((H, 2, 2, NY, T, HD), BF16),
        V((H, 2, NY, T, HD), BF16),
        S((H, 2, NY - 1)), S((H, 2, NY - 1)), S((H, 2)),
        S((H, NY - 1)), S((H, NY - 1)), S((H,)),
        S((H, 2, NY)), S((H, 2, NY)), S((H, 2)), S((H, 2)),
        S((H, NY - 1)), S((H, NY - 1)), S((H,)), S,
        S((ns - 1,)), S((ns - 1,)), S((nb - 1,)), S((nb - 1,)),
        S((H, NY - 1)), S((H, NY - 1)), S((H,)), S((NY * H,)),
        S((H, 2)), S((H, 2)), S((H, 2)), S((H, 2)),
        S((H, NY - 1)), S((H, NY - 1)), S((H,)),
        S((H, 2, NY - 1)), S((H, 2, NY - 1)), S((H, 2)),
    ]
    any_spec = pl.BlockSpec(memory_space=pl.ANY)
    smem = pl.BlockSpec(memory_space=pltpu.SMEM)
    loss, gr, gq, gk, gv = pl.pallas_call(
        functools.partial(kernel, nb, T),
        out_shape=(
            jax.ShapeDtypeStruct((1, 1), F32),
            jax.ShapeDtypeStruct((T, D), BF16),
            jax.ShapeDtypeStruct((T, D), BF16),
            jax.ShapeDtypeStruct(key_proj.shape, BF16),
            jax.ShapeDtypeStruct(key_proj.shape, BF16),
        ),
        in_specs=[smem, smem, any_spec, any_spec, any_spec, any_spec, pl.BlockSpec(memory_space=pltpu.VMEM)],
        out_specs=(smem, any_spec, any_spec, any_spec, any_spec),
        scratch_shapes=scratch,
        compiler_params=pltpu.CompilerParams(
            collective_id=0, has_side_effects=True, vmem_limit_bytes=56 * 1024 * 1024
        ),
        cost_estimate=pl.CostEstimate(flops=13 * 10**9, bytes_accessed=6 * 2**20, transcendentals=2**23),
        name="attention_backward",
    )(lengths, positives, residual, query_proj, key_proj, value_proj, norm_gain.reshape(1, D))
    return loss.reshape(()), gr, gq, gk, gv


def solution(mesh):
    rows = P(("batch", "seq"), None)
    return jax.shard_map(
        functools.partial(on_device, mesh.shape["batch"]),
        mesh=mesh,
        in_specs=(rows, rows, rows, rows, P(), P("batch"), P()),
        out_specs=(P(), rows, rows, rows, rows),
        check_vma=False,
    )
```

```python
import functools
import math

import jax
import jax.numpy as jnp
from jax import lax
from jax.experimental import pallas as pl
from jax.experimental.pallas import tpu as pltpu
from jax.sharding import PartitionSpec as P

MESH = pl.DeviceIdType.MESH
HD = 128
NY = 4
NZ = 4
H = 2
G = 4
GW = G * HD
EPS = 1e-6
F32 = jnp.float32
BF16 = jnp.bfloat16
FACTOR = 1.0 / math.sqrt(HD)
LOG2E_FACTOR = FACTOR * math.log2(math.e)


def dot(a, b, dims=((1,), (0,))):
    return lax.dot_general(a, b, (dims, ((), ())), preferred_element_type=F32)


def kernel(
    nb, t_rows,
    len_ref, pos_ref, res_hbm, q_hbm, k_hbm, v_hbm, gain_ref,
    loss_ref, out_gr, out_gq, out_gk, out_gv,
    kvb, kfx, kzt, vta, qin, qs, qt, est, mb, mrun, linv, acc, rin, smt,
    rsq, rsa, invr, pz, pza, emba, sga, lra, gbt, mrw, msa, mrc, dot_t, gro, dqa, gqo, dka, dva, dkvo, own, rs1, rs2, fin,
    kvs, kvr, kvl, qss, qsr, qsl, rns, rnr, rnl, z1s, z1r, z2s, z2r,
    sqs, sqr, pzs, pzr, ems, emr, sis, sir, los, lor, mns, mnr,
    grs, grr, grl, r1s, r1r, r2s, r2r, gqs, gqr, gql, gks, gkr, gkl,
):
    T = t_rows
    BK = NY * T
    NG = H * G
    b = lax.axis_index("batch")
    s = lax.axis_index("seq")
    y = lax.div(s, NZ)
    zh = lax.rem(s, NZ)
    right = (b, y * NZ + lax.rem(zh + 1, NZ))
    left = (b, y * NZ + lax.rem(zh + NZ - 1, NZ))

    def yo(k):
        return lax.rem(y + k, NY)

    def zo(k):
        return lax.rem(zh + k, NZ)

    def bo(k):
        return lax.rem(b + k, nb)

    def ydev(yy):
        return (b, yy * NZ + zh)

    def zdev(zz):
        return (b, y * NZ + zz)

    def col(index, width):
        return pl.ds(pl.multiple_of(index * width, width), width)

    def rcopy(src, dst, ssem, rsem, dev):
        return pltpu.make_async_remote_copy(
            src_ref=src, dst_ref=dst, send_sem=ssem, recv_sem=rsem, device_id=dev, device_id_type=MESH
        )

    def lcopy(src, dst, sem):
        return pltpu.make_async_copy(src, dst, sem)

    def await_ref(ref, sem):
        pltpu.make_async_copy(ref, ref, sem).wait()

    sends = []

    def send(src, dst, ssem, rsem, dev):
        copy = rcopy(src, dst, ssem, rsem, dev)
        copy.start()
        sends.append(copy)

    length = len_ref[0]
    lenf = length.astype(F32)

    for h in range(H):
        for c, src in ((0, k_hbm), (1, v_hbm)):
            lcopy(src.at[:, col(2 * y + h, HD)], kvb.at[h, 0, c, y], kvl.at[h, c]).start()
        lcopy(q_hbm.at[:, col(2 * y + h, GW)], qin.at[h, y], qsl.at[h]).start()
        lcopy(res_hbm.at[:, col(2 * y + h, GW)], rin.at[h, y], rnl.at[h]).start()

    barrier = pltpu.get_barrier_semaphore()
    for k in range(1, NY):
        pl.semaphore_signal(barrier, inc=1, device_id=ydev(yo(k)), device_id_type=MESH)
    for k in range(1, NZ):
        pl.semaphore_signal(barrier, inc=1, device_id=zdev(zo(k)), device_id_type=MESH)
    for k in range(1, nb):
        pl.semaphore_signal(barrier, inc=1, device_id=(bo(k), s), device_id_type=MESH)
    pl.semaphore_wait(barrier, NY - 1 + NZ - 1 + nb - 1)

    for h in range(H):
        for k in (1, 3, 2):
            yy = yo(k)
            for c, src in ((0, k_hbm), (1, v_hbm)):
                send(src.at[:, col(2 * yy + h, HD)], kvb.at[h, 0, c, y], kvs.at[h, c, k - 1], kvr.at[h, c, k - 1], ydev(yy))
        for k in (1, 3, 2):
            yy = yo(k)
            send(q_hbm.at[:, col(2 * yy + h, GW)], qin.at[h, y], qss.at[h, k - 1], qsr.at[h, k - 1], ydev(yy))
    for h in range(H):
        for k in (1, 3, 2):
            yy = yo(k)
            send(res_hbm.at[:, col(2 * yy + h, GW)], rin.at[h, y], rns.at[h, k - 1], rnr.at[h, k - 1], ydev(yy))

    for h in range(H):
        for k in (0, 1, 3, 2):
            p = yo(NY - k)
            for c, src in ((0, k_hbm), (1, v_hbm)):
                if k == 0:
                    lcopy(src.at[:, col(2 * y + h, HD)], kvb.at[h, 0, c, y], kvl.at[h, c]).wait()
                else:
                    await_ref(kvb.at[h, 0, c, p], kvr.at[h, c, k - 1])
            send(kvb.at[h, 0, :, p], kvb.at[h, 1, :, p], z1s.at[h, 0, k], z1r.at[h, 0, k], right)
            send(kvb.at[h, 0, :, p], kvb.at[h, 2, :, p], z1s.at[h, 1, k], z1r.at[h, 1, k], left)

    def hop2(h, way):
        src, dev, piece = (1, right, 0) if way == 0 else (2, left, 2)
        return rcopy(
            kvb.at[h, src, :, pl.ds(piece, 2)], kvb.at[h, 3, :, pl.ds(piece, 2)], z2s.at[h, way], z2r.at[h, way], dev
        )

    def forward_hops(h):
        for way in range(2):
            for k in range(NY):
                await_ref(kvb.at[h, 1 + way, :, yo(NY - k)], z1r.at[h, way, k])
            hop2(h, way).start()

    def await_columns(h, src, dst, lsem, rsem):
        lcopy(src.at[:, col(2 * y + h, GW)], dst.at[h, y], lsem.at[h]).wait()
        for k in range(1, NY):
            await_ref(dst.at[h, yo(NY - k)], rsem.at[h, k - 1])

    def prep_q(h):
        def body(yy, carry):
            for j in range(G):
                head = qin[h, yy, :, j * HD : (j + 1) * HD]
                qs[h, yy, j * T : (j + 1) * T, :] = head
                qt[h, yy, :, j * T : (j + 1) * T] = head.astype(F32).T.astype(BF16)
            mrun[h, yy] = jnp.full((1, G * T), -3e38, F32)
            acc[h, yy] = jnp.zeros((HD + 16, G * T), F32)
            return carry

        lax.fori_loop(0, NY, body, 0)

    def prep_res(h):
        def body(yy, carry):
            for j in range(G):
                smt[h, yy, :, j * T : (j + 1) * T] = rin[h, yy, :, j * HD : (j + 1) * HD].astype(F32).T
            return carry

        lax.fori_loop(0, NY, body, 0)

    def prep_kv(h, rel, zb):
        first_key = kvb[h, rel, 0, 0, 0:1, :].astype(F32)
        for yy in range(NY):
            base = (yy * NZ + zb) * T
            valid = lax.broadcasted_iota(jnp.int32, (T, HD), 0) + base < length
            rows = slice(yy * T, (yy + 1) * T)
            kp = kvb[h, rel, 0, yy].astype(F32)
            vp = kvb[h, rel, 1, yy].astype(F32)
            kfx[h, rel, rows, :] = jnp.where(valid, kp, first_key).astype(BF16)
            kzt[h, rel, :, rows] = jnp.where(valid, kp, 0.0).T.astype(BF16)
            vta[h, rel, 0:HD, rows] = jnp.where(valid, vp, 0.0).T.astype(BF16)
            lanes = lax.broadcasted_iota(jnp.int32, (16, T), 1) + base < length
            vta[h, rel, HD : HD + 16, rows] = jnp.where(lanes, 1.0, 0.0).astype(BF16)

    halves = [slice(part * (G * T // 2), (part + 1) * (G * T // 2)) for part in range(2)]

    def attend(h, rel, yy):
        for lanes in halves:
            sc = dot(kfx[h, rel], qt[h, yy, :, lanes])
            m = jnp.max(sc, axis=0, keepdims=True)
            e = jnp.exp2((sc - m) * LOG2E_FACTOR).astype(BF16)
            est[h, rel, yy, :, lanes] = e
            mb[h, rel, yy, :, lanes] = m
            o = dot(vta[h, rel], e)
            mo = mrun[h, yy, :, lanes]
            mn = jnp.maximum(mo, m)
            keep = jnp.exp2((mo - mn) * LOG2E_FACTOR)
            add = jnp.exp2((m - mn) * LOG2E_FACTOR)
            acc[h, yy, :, lanes] = acc[h, yy, :, lanes] * keep + o * add
            mrun[h, yy, :, lanes] = mn

    def over_chunks(body):
        def step(yy, carry):
            body(yy)
            return carry

        lax.fori_loop(0, NY, step, 0)

    def own_step(h, carry):
        @pl.when(h == 1)
        def _():
            forward_hops(0)

        await_columns(h, q_hbm, qin, qsl, qsr)
        prep_q(h)
        prep_kv(h, 0, zh)
        over_chunks(lambda yy: attend(h, 0, yy))
        return carry

    def near_step(m, carry):
        h = lax.div(m, 2)
        rel = 1 + lax.rem(m, 2)

        @pl.when(m == 2)
        def _():
            forward_hops(1)

        prep_kv(h, rel, zo(5 - 2 * rel))
        over_chunks(lambda yy: attend(h, rel, yy))
        return carry

    def far_step(h, carry):
        await_columns(h, res_hbm, rin, rnl, rnr)
        prep_res(h)
        for way in range(2):
            await_ref(kvb.at[h, 3, :, pl.ds(2 * way, 2)], z2r.at[h, way])
        prep_kv(h, 3, zo(2))

        def chunk(yy):
            attend(h, 3, yy)
            li = 1.0 / acc[h, yy, HD : HD + 1, :]
            linv[h, yy] = li
            o = acc[h, yy, 0:HD, :] * li
            acc[h, yy, 0:HD, :] = o
            x = smt[h, yy] + o.astype(BF16).astype(F32)
            smt[h, yy] = x
            sq = jnp.sum(x * x, axis=0, keepdims=True)
            rsq[yy] = rsq[yy] + sum(sq[:, j * T : (j + 1) * T] for j in range(G))

        over_chunks(chunk)
        return carry

    rsq[...] = jnp.zeros((NY, 1, T), F32)
    lax.fori_loop(0, H, own_step, 0)
    lax.fori_loop(0, 2 * H, near_step, 0)
    lax.fori_loop(0, H, far_step, 0)

    def sum_along_y(src, gathered, ssem, rsem):
        for k in (2, 1, 3):
            send(src, gathered.at[y], ssem.at[k - 1], rsem.at[k - 1], ydev(yo(k)))
        gathered[y] = src[...]
        for k in (1, 3, 2):
            await_ref(gathered.at[yo(NY - k)], rsem.at[k - 1])
        return (gathered[0] + gathered[1]) + (gathered[2] + gathered[3])

    mean_square = sum_along_y(rsq, rsa, sqs, sqr) * (1.0 / (NY * NG * HD))
    inv = lax.rsqrt(mean_square + EPS)
    lane = lax.broadcasted_iota(jnp.int32, (NY, 1, T), 2)
    chunk_id = lax.broadcasted_iota(jnp.int32, (NY, 1, T), 0)
    live = (chunk_id * NZ + zh) * T + lane < length
    inv = jnp.where(live, inv, 0.0)
    invr[...] = inv

    for h in range(H):
        for j in range(G):
            part = smt[h, 0, :, j * T : (j + 1) * T] * inv[0]
            for yy in range(1, NY):
                part = part + smt[h, yy, :, j * T : (j + 1) * T] * inv[yy]
            pz[h * G + j : h * G + j + 1, :] = jnp.sum(part.T, axis=0, keepdims=True)
    gain = gain_ref[y]
    pz[...] = pz[...] * gain / lenf
    for k in (2, 1, 3):
        send(pz, pza.at[zh], pzs.at[k - 1], pzr.at[k - 1], zdev(zo(k)))
    pza[zh] = pz[...]
    for k in (1, 3, 2):
        await_ref(pza.at[zo(NZ - k)], pzr.at[k - 1])
    mine = (pza[0] + pza[1]) + (pza[2] + pza[3])
    emba[b] = mine
    for k in range(1, nb):
        send(emba.at[b], emba.at[b], ems.at[k - 1], emr.at[k - 1], (bo(k), s))
    for k in range(1, nb):
        await_ref(emba.at[bo(nb - k)], emr.at[k - 1])

    doc_ids = lax.broadcasted_iota(jnp.int32, (nb, HD), 0)
    lane_ids = lax.broadcasted_iota(jnp.int32, (nb, HD), 1)
    dots = jnp.zeros((nb, HD), F32)
    squares = jnp.zeros((nb, HD), F32)
    for j in range(nb):
        row = emba[j]
        dots = jnp.where(doc_ids == j, jnp.sum(row * mine, axis=0, keepdims=True), dots)
        squares = jnp.where(doc_ids == j, jnp.sum(row * row, axis=0, keepdims=True), squares)
    dots = jnp.broadcast_to(jnp.sum(dots, axis=1, keepdims=True), (nb, HD))
    squares = jnp.broadcast_to(jnp.sum(squares, axis=1, keepdims=True), (nb, HD))
    sga[NY] = jnp.where(lane_ids < HD // 2, dots, squares)
    both = sum_along_y(sga.at[NY], sga, sis, sir)
    dots = jnp.broadcast_to(both[:, 0:1], (nb, HD))
    rho = lax.rsqrt(jnp.broadcast_to(both[:, HD // 2 : HD // 2 + 1], (nb, HD)) + EPS)
    row_rho = jnp.broadcast_to(jnp.sum(jnp.where(doc_ids == b, rho, 0.0), axis=0, keepdims=True), (nb, HD))
    sims = dots * rho * row_rho
    logits = 10.0 * sims - 2.0
    posv = jnp.zeros((nb, HD), jnp.int32)
    for j in range(nb):
        posv = jnp.where(doc_ids == j, pos_ref[j], posv)
    sign = jnp.where(doc_ids == pos_ref[b], 1.0, -1.0)

    def pull(label):
        return -10.0 / nb * label / (1.0 + jnp.exp(label * logits))

    pair = pull(sign) + pull(jnp.where(posv == b, 1.0, -1.0))
    pair = jnp.where(doc_ids == b, 0.0, pair) * (16.0 * NY * NZ * T)
    coef = pair * rho * row_rho
    self_coef = row_rho * row_rho * jnp.broadcast_to(jnp.sum(pair * sims, axis=0, keepdims=True), (nb, HD))
    grad = -self_coef[0:1, :] * mine
    for j in range(nb):
        grad = grad + coef[j : j + 1, :] * emba[j]
    gained = grad / lenf * gain

    for i in range(NG):
        gbt[i] = jnp.broadcast_to(gained[i : i + 1, :], (T, HD)).T
    for yy in range(NY):
        part = gbt[0] * smt[0, yy, :, 0:T]
        for i in range(1, NG):
            j = i % G
            part = part + gbt[i] * smt[i // G, yy, :, j * T : (j + 1) * T]
        mrw[yy] = jnp.sum(part, axis=0, keepdims=True)
    mean = sum_along_y(mrw, msa, mns, mnr) * invr[...] * (1.0 / (NY * NG * HD))
    mrw_scale = invr[...] * invr[...] * mean

    def r1(h, way):
        dev, piece = (right, 0) if way == 0 else (left, 2)
        return rcopy(dkvo.at[h, 2, :, pl.ds(piece, 2)], rs1.at[h, way], r1s.at[h, way], r1r.at[h, way], dev)

    def r2(h, way):
        dev = right if way == 0 else left
        return rcopy(dkvo.at[h, 1 - way], rs2.at[h, way], r2s.at[h, way], r2r.at[h, way], dev)

    def gq_send(h, kk):
        yy = yo(kk)
        return rcopy(gqo.at[h, yy], out_gq.at[:, col(2 * y + h, GW)], gqs.at[h, kk - 1], gqr.at[h, kk - 1], ydev(yy))

    def gq_local(h):
        return lcopy(gqo.at[h, y], out_gq.at[:, col(2 * y + h, GW)], gql.at[h])

    def gr_send(h, kk):
        yy = yo(kk)
        return rcopy(gro.at[h, yy], out_gr.at[:, col(2 * y + h, GW)], grs.at[h, kk - 1], grr.at[h, kk - 1], ydev(yy))

    def gr_local(h):
        return lcopy(gro.at[h, y], out_gr.at[:, col(2 * y + h, GW)], grl.at[h])

    def pull_back(h, rel, yy):
        vals = kvb[h, rel, 1].reshape(BK, HD)
        for lanes in halves:
            r = jnp.exp2((mb[h, rel, yy, :, lanes] - mrun[h, yy, :, lanes]) * LOG2E_FACTOR) * linv[h, yy, :, lanes]
            do = (dot_t[h, yy, :, lanes].astype(F32) * r).astype(BF16)
            delta = jnp.sum(do.astype(F32) * acc[h, yy, 0:HD, lanes], axis=0, keepdims=True)
            e = est[h, rel, yy, :, lanes]
            dp = dot(vals, do)
            ds = (e.astype(F32) * (dp - delta)).astype(BF16)
            dva[...] += dot(e, do, ((1,), (1,)))
            dka[...] += dot(ds, qs[h, yy, lanes, :])
            dqa[h, yy, :, lanes] += dot(kzt[h, rel], ds)

    def clear():
        dka[...] = jnp.zeros((BK, HD), F32)
        dva[...] = jnp.zeros((BK, HD), F32)

    def store(h, slot, added):
        for c, ref in ((0, dka), (1, dva)):
            for p in range(NY):
                x = ref[p * T : (p + 1) * T, :]
                if c == 0:
                    x = x * FACTOR
                if added is not None and p // 2 == added:
                    x = x + rs1[h, added, c, p % 2].astype(F32)
                dkvo[h, slot, c, p] = x.astype(BF16)

    def far_back(h, carry):
        for yy in range(NY):
            a = jnp.concatenate([invr[yy]] * G, axis=1)
            c = jnp.concatenate([mrc[yy]] * G, axis=1)
            g = jnp.concatenate([gbt[h * G + j] for j in range(G)], axis=1)
            dot_t[h, yy] = (g * a - smt[h, yy] * c).astype(BF16)
            dqa[h, yy] = jnp.zeros((HD, G * T), F32)
        clear()
        over_chunks(lambda yy: pull_back(h, 3, yy))
        store(h, 2, None)
        r1(h, 0).start()
        r1(h, 1).start()

        def give(t, carry):
            kk = lax.rem(t + 1, NY)
            yy = yo(kk)
            for j in range(G):
                gro[h, yy, :, j * HD : (j + 1) * HD] = dot_t[h, yy, :, j * T : (j + 1) * T].astype(F32).T.astype(BF16)

            @pl.when(kk > 0)
            def _():
                gr_send(h, kk).start()

            @pl.when(kk == 0)
            def _():
                gr_local(h).start()

            return carry

        lax.fori_loop(0, NY, give, 0)
        return carry

    def near_back(m, carry):
        h = lax.div(m, 2)
        way = lax.rem(m, 2)
        rel = 2 - way
        clear()
        over_chunks(lambda yy: pull_back(h, rel, yy))
        for w in range(2):

            @pl.when(way == w)
            def _(w=w):
                await_ref(rs1.at[h, w], r1r.at[h, w])
                store(h, 1 - w, w)
                r2(h, w).start()

        return carry

    def own_back(h, carry):
        clear()

        def chunk(t, carry):
            kk = lax.rem(t + 1, NY)
            yy = yo(kk)
            pull_back(h, 0, yy)
            for j in range(G):
                part = dqa[h, yy, :, j * T : (j + 1) * T] * FACTOR
                gqo[h, yy, :, j * HD : (j + 1) * HD] = part.T.astype(BF16)

            @pl.when(kk > 0)
            def _():
                gq_send(h, kk).start()

            @pl.when(kk == 0)
            def _():
                gq_local(h).start()

            return carry

        lax.fori_loop(0, NY, chunk, 0)
        own[h, 0] = dka[...] * FACTOR
        own[h, 1] = dva[...]
        return carry

    mrc[...] = mrw_scale
    lax.fori_loop(0, H, far_back, 0)

    x = -sign * logits
    term = jnp.maximum(x, 0.0) + jnp.log(1.0 + jnp.exp(-jnp.abs(x)))
    term = jnp.sum(jnp.where(doc_ids == b, 0.0, term), axis=0, keepdims=True)
    lra[b] = jnp.broadcast_to(term, (8, HD))
    for k in range(1, nb):
        send(lra.at[b], lra.at[b], los.at[k - 1], lor.at[k - 1], (bo(k), s))

    lax.fori_loop(0, 2 * H, near_back, 0)
    lax.fori_loop(0, H, own_back, 0)

    for k in range(1, nb):
        await_ref(lra.at[bo(nb - k)], lor.at[k - 1])
    loss = lra[0]
    for j in range(1, nb):
        loss = loss + lra[j]
    loss_ref[0, 0] = jnp.sum(loss) * (1.0 / (8 * HD * nb))

    for h in range(H):
        await_ref(rs2.at[h, 0], r2r.at[h, 0])
        await_ref(rs2.at[h, 1], r2r.at[h, 1])
        for p in range(NY):
            valid = lax.broadcasted_iota(jnp.int32, (T, HD), 0) + (p * NZ + zh) * T < length
            for c in range(2):
                x = own[h, c, p * T : (p + 1) * T, :] + rs2[h, 0, c, p].astype(F32) + rs2[h, 1, c, p].astype(F32)
                fin[h, c, p] = jnp.where(valid, x, 0.0).astype(BF16)
        for c, out in ((0, out_gk), (1, out_gv)):
            for k in (2, 1, 3):
                yy = yo(k)
                send(fin.at[h, c, yy], out.at[:, col(2 * y + h, HD)], gks.at[h, c, k - 1], gkr.at[h, c, k - 1], ydev(yy))
            lcopy(fin.at[h, c, y], out.at[:, col(2 * y + h, HD)], gkl.at[h, c]).start()

    for h in range(H):
        gq_local(h).wait()
        gr_local(h).wait()
        for k in range(1, NY):
            await_ref(out_gr.at[:, col(2 * yo(NY - k) + h, GW)], grr.at[h, k - 1])
            await_ref(out_gq.at[:, col(2 * yo(NY - k) + h, GW)], gqr.at[h, k - 1])
        for c, out in ((0, out_gk), (1, out_gv)):
            lcopy(fin.at[h, c, y], out.at[:, col(2 * y + h, HD)], gkl.at[h, c]).wait()
            for k in range(1, NY):
                await_ref(out.at[:, col(2 * yo(NY - k) + h, HD)], gkr.at[h, c, k - 1])
    for copy in sends:
        copy.wait_send()
    for h in range(H):
        for way in range(2):
            hop2(h, way).wait_send()
            r1(h, way).wait_send()
            r2(h, way).wait_send()
        for k in range(1, NY):
            gr_send(h, k).wait_send()
            gq_send(h, k).wait_send()


def copy_kernel(parts, *refs):
    n = len(refs) // 2
    sems = refs[-1]
    copies = []
    for i in range(n):
        src, dst = refs[i], refs[n + i]
        rows = src.shape[0] // parts
        for p in range(parts):
            span = pl.ds(p * rows, rows)
            copies.append(pltpu.make_async_copy(src.at[span], dst.at[span], sems.at[i, p]))
    for copy in copies:
        copy.start()
    for copy in copies:
        copy.wait()


def own_buffers(arrays):
    parts = 4
    any_spec = pl.BlockSpec(memory_space=pl.ANY)
    return pl.pallas_call(
        functools.partial(copy_kernel, parts),
        out_shape=tuple(jax.ShapeDtypeStruct(x.shape, x.dtype) for x in arrays),
        in_specs=[any_spec] * len(arrays),
        out_specs=(any_spec,) * len(arrays),
        scratch_shapes=[pltpu.SemaphoreType.DMA((len(arrays), parts))],
        compiler_params=pltpu.CompilerParams(vmem_limit_bytes=56 * 1024 * 1024),
        cost_estimate=pl.CostEstimate(flops=0, bytes_accessed=5 * 2**20, transcendentals=0),
        name="copy_out",
    )(*arrays)


def on_device(nb, residual, query_proj, key_proj, value_proj, norm_gain, lengths, positives):
    T, D = residual.shape
    BK, QC, NG = NY * T, G * T, H * G
    V = pltpu.VMEM
    S = pltpu.SemaphoreType.DMA
    columns = V((H, NY, T, GW), BF16)
    scratch = [
        V((H, NZ, 2, NY, T, HD), BF16),
        V((H, NZ, BK, HD), BF16),
        V((H, NZ, HD, BK), BF16),
        V((H, NZ, HD + 16, BK), BF16),
        columns,
        V((H, NY, QC, HD), BF16),
        V((H, NY, HD, QC), BF16),
        V((H, NZ, NY, BK, QC), BF16),
        V((H, NZ, NY, 1, QC), F32),
        V((H, NY, 1, QC), F32),
        V((H, NY, 1, QC), F32),
        V((H, NY, HD + 16, QC), F32),
        columns,
        V((H, NY, HD, QC), F32),
        V((NY, 1, T), F32), V((NY, NY, 1, T), F32), V((NY, 1, T), F32),
        V((NG, HD), F32), V((NZ, NG, HD), F32),
        V((nb, NG, HD), F32),
        V((NY + 1, nb, HD), F32),
        V((nb, 8, HD), F32),
        V((NG, HD, T), F32),
        V((NY, 1, T), F32), V((NY, NY, 1, T), F32), V((NY, 1, T), F32),
        V((H, NY, HD, QC), BF16),
        columns,
        V((H, NY, HD, QC), F32),
        columns,
        V((BK, HD), F32),
        V((BK, HD), F32),
        V((H, 3, 2, NY, T, HD), BF16),
        V((H, 2, BK, HD), F32),
        V((H, 2, 2, 2, T, HD), BF16),
        V((H, 2, 2, NY, T, HD), BF16),
        V((H, 2, NY, T, HD), BF16),
        S((H, 2, NY - 1)), S((H, 2, NY - 1)), S((H, 2)),
        S((H, NY - 1)), S((H, NY - 1)), S((H,)),
        S((H, NY - 1)), S((H, NY - 1)), S((H,)),
        S((H, 2, NY)), S((H, 2, NY)), S((H, 2)), S((H, 2)),
        S((NY - 1,)), S((NY - 1,)), S((NZ - 1,)), S((NZ - 1,)),
        S((nb - 1,)), S((nb - 1,)), S((NY - 1,)), S((NY - 1,)),
        S((nb - 1,)), S((nb - 1,)), S((NY - 1,)), S((NY - 1,)),
        S((H, NY - 1)), S((H, NY - 1)), S((H,)),
        S((H, 2)), S((H, 2)), S((H, 2)), S((H, 2)),
        S((H, NY - 1)), S((H, NY - 1)), S((H,)),
        S((H, 2, NY - 1)), S((H, 2, NY - 1)), S((H, 2)),
    ]
    any_spec = pl.BlockSpec(memory_space=pl.ANY)
    smem = pl.BlockSpec(memory_space=pltpu.SMEM)
    loss, *grads = pl.pallas_call(
        functools.partial(kernel, nb, T),
        out_shape=(
            jax.ShapeDtypeStruct((1, 1), F32),
            jax.ShapeDtypeStruct((T, D), BF16),
            jax.ShapeDtypeStruct((T, D), BF16),
            jax.ShapeDtypeStruct(key_proj.shape, BF16),
            jax.ShapeDtypeStruct(key_proj.shape, BF16),
        ),
        in_specs=[smem, smem, any_spec, any_spec, any_spec, any_spec, pl.BlockSpec(memory_space=pltpu.VMEM)],
        out_specs=(smem, any_spec, any_spec, any_spec, any_spec),
        scratch_shapes=scratch,
        compiler_params=pltpu.CompilerParams(
            collective_id=0, has_side_effects=True, vmem_limit_bytes=56 * 1024 * 1024
        ),
        cost_estimate=pl.CostEstimate(flops=13 * 10**9, bytes_accessed=6 * 2**20, transcendentals=2**23),
        name="attention_backward",
    )(lengths, positives, residual, query_proj, key_proj, value_proj, norm_gain.reshape(NY, NG, HD))
    return loss.reshape(()), *own_buffers(grads)


def solution(mesh):
    rows = P(("batch", "seq"), None)
    return jax.shard_map(
        functools.partial(on_device, mesh.shape["batch"]),
        mesh=mesh,
        in_specs=(rows, rows, rows, rows, P(), P("batch"), P()),
        out_specs=(P(), rows, rows, rows, rows),
        check_vma=False,
    )
```

```python
import functools
import math

import jax
import jax.numpy as jnp
from jax import lax
from jax.experimental import pallas as pl
from jax.experimental.pallas import tpu as pltpu
from jax.sharding import PartitionSpec as P

MESH = pl.DeviceIdType.MESH
HD = 128
NY = 4
NZ = 4
H = 2
G = 4
GW = G * HD
EPS = 1e-6
F32 = jnp.float32
BF16 = jnp.bfloat16
FACTOR = 1.0 / math.sqrt(HD)
LOG2E_FACTOR = FACTOR * math.log2(math.e)


def dot(a, b, dims=((1,), (0,))):
    return lax.dot_general(a, b, (dims, ((), ())), preferred_element_type=F32)


def kernel(
    nb, t_rows,
    len_ref, pos_ref, res_hbm, q_hbm, k_hbm, v_hbm, gain_ref,
    loss_ref, out_gr, out_gq, out_gk, out_gv,
    k_buf, v_buf, q_buf, res_buf, kvb, kfx, kzt, vta, qin, qs, qt, est, mb, mrun, linv, acc, rin, smt,
    rsq, rsa, invr, pz, pza, emba, sga, lra, gbt, mrw, msa, mrc, dot_t, gro, dqa, gqo, dka, dva, dkvo, own, rs1, rs2, fin,
    lds, kvs, kvr, kvl, qss, qsr, qsl, rns, rnr, rnl, z1s, z1r, z2s, z2r,
    sqs, sqr, pzs, pzr, ems, emr, sis, sir, los, lor, mns, mnr,
    grs, grr, grl, r1s, r1r, r2s, r2r, gqs, gqr, gql, gks, gkr, gkl,
):
    T = t_rows
    BK = NY * T
    NG = H * G
    b = lax.axis_index("batch")
    s = lax.axis_index("seq")
    y = lax.div(s, NZ)
    zh = lax.rem(s, NZ)
    right = (b, y * NZ + lax.rem(zh + 1, NZ))
    left = (b, y * NZ + lax.rem(zh + NZ - 1, NZ))

    def yo(k):
        return lax.rem(y + k, NY)

    def zo(k):
        return lax.rem(zh + k, NZ)

    def bo(k):
        return lax.rem(b + k, nb)

    def ydev(yy):
        return (b, yy * NZ + zh)

    def zdev(zz):
        return (b, y * NZ + zz)

    def col(index, width):
        return pl.ds(pl.multiple_of(index * width, width), width)

    def rcopy(src, dst, ssem, rsem, dev):
        return pltpu.make_async_remote_copy(
            src_ref=src, dst_ref=dst, send_sem=ssem, recv_sem=rsem, device_id=dev, device_id_type=MESH
        )

    def lcopy(src, dst, sem):
        return pltpu.make_async_copy(src, dst, sem)

    def await_ref(ref, sem):
        pltpu.make_async_copy(ref, ref, sem).wait()

    sends = []

    def send(src, dst, ssem, rsem, dev):
        copy = rcopy(src, dst, ssem, rsem, dev)
        copy.start()
        sends.append(copy)

    length = len_ref[0]
    lenf = length.astype(F32)

    loads = [
        lcopy(src, dst, lds.at[i])
        for i, (src, dst) in enumerate(((k_hbm, k_buf), (v_hbm, v_buf), (q_hbm, q_buf), (res_hbm, res_buf)))
    ]
    for load in loads:
        load.start()

    barrier = pltpu.get_barrier_semaphore()
    for k in range(1, NY):
        pl.semaphore_signal(barrier, inc=1, device_id=ydev(yo(k)), device_id_type=MESH)
    for k in range(1, NZ):
        pl.semaphore_signal(barrier, inc=1, device_id=zdev(zo(k)), device_id_type=MESH)
    for k in range(1, nb):
        pl.semaphore_signal(barrier, inc=1, device_id=(bo(k), s), device_id_type=MESH)
    pl.semaphore_wait(barrier, NY - 1 + NZ - 1 + nb - 1)

    for load in loads:
        load.wait()
    for h in range(H):
        for c, src in ((0, k_buf), (1, v_buf)):
            lcopy(src.at[:, col(2 * y + h, HD)], kvb.at[h, 0, c, y], kvl.at[h, c]).start()
            for k in (1, 3, 2):
                yy = yo(k)
                send(src.at[:, col(2 * yy + h, HD)], kvb.at[h, 0, c, y], kvs.at[h, c, k - 1], kvr.at[h, c, k - 1], ydev(yy))
        lcopy(q_buf.at[:, col(2 * y + h, GW)], qin.at[h, y], qsl.at[h]).start()
        for k in (1, 3, 2):
            yy = yo(k)
            send(q_buf.at[:, col(2 * yy + h, GW)], qin.at[h, y], qss.at[h, k - 1], qsr.at[h, k - 1], ydev(yy))
    for h in range(H):
        lcopy(res_buf.at[:, col(2 * y + h, GW)], rin.at[h, y], rnl.at[h]).start()
        for k in (1, 3, 2):
            yy = yo(k)
            send(res_buf.at[:, col(2 * yy + h, GW)], rin.at[h, y], rns.at[h, k - 1], rnr.at[h, k - 1], ydev(yy))

    for h in range(H):
        for k in (0, 1, 3, 2):
            p = yo(NY - k)
            for c, src in ((0, k_buf), (1, v_buf)):
                if k == 0:
                    lcopy(src.at[:, col(2 * y + h, HD)], kvb.at[h, 0, c, y], kvl.at[h, c]).wait()
                else:
                    await_ref(kvb.at[h, 0, c, p], kvr.at[h, c, k - 1])
            send(kvb.at[h, 0, :, p], kvb.at[h, 1, :, p], z1s.at[h, 0, k], z1r.at[h, 0, k], right)
            send(kvb.at[h, 0, :, p], kvb.at[h, 2, :, p], z1s.at[h, 1, k], z1r.at[h, 1, k], left)

    def hop2(h, way):
        src, dev, piece = (1, right, 0) if way == 0 else (2, left, 2)
        return rcopy(
            kvb.at[h, src, :, pl.ds(piece, 2)], kvb.at[h, 3, :, pl.ds(piece, 2)], z2s.at[h, way], z2r.at[h, way], dev
        )

    def forward_hops(h):
        for way in range(2):
            for k in range(NY):
                await_ref(kvb.at[h, 1 + way, :, yo(NY - k)], z1r.at[h, way, k])
            hop2(h, way).start()

    def await_columns(h, src, dst, lsem, rsem):
        lcopy(src.at[:, col(2 * y + h, GW)], dst.at[h, y], lsem.at[h]).wait()
        for k in range(1, NY):
            await_ref(dst.at[h, yo(NY - k)], rsem.at[h, k - 1])

    def prep_q(h):
        def body(yy, carry):
            for j in range(G):
                head = qin[h, yy, :, j * HD : (j + 1) * HD]
                qs[h, yy, j * T : (j + 1) * T, :] = head
                qt[h, yy, :, j * T : (j + 1) * T] = head.astype(F32).T.astype(BF16)
            mrun[h, yy] = jnp.full((1, G * T), -3e38, F32)
            acc[h, yy] = jnp.zeros((HD + 16, G * T), F32)
            return carry

        lax.fori_loop(0, NY, body, 0)

    def prep_res(h):
        def body(yy, carry):
            for j in range(G):
                smt[h, yy, :, j * T : (j + 1) * T] = rin[h, yy, :, j * HD : (j + 1) * HD].astype(F32).T
            return carry

        lax.fori_loop(0, NY, body, 0)

    def prep_kv(h, rel, zb):
        first_key = kvb[h, rel, 0, 0, 0:1, :].astype(F32)
        for yy in range(NY):
            base = (yy * NZ + zb) * T
            valid = lax.broadcasted_iota(jnp.int32, (T, HD), 0) + base < length
            rows = slice(yy * T, (yy + 1) * T)
            kp = kvb[h, rel, 0, yy].astype(F32)
            vp = kvb[h, rel, 1, yy].astype(F32)
            kfx[h, rel, rows, :] = jnp.where(valid, kp, first_key).astype(BF16)
            kzt[h, rel, :, rows] = jnp.where(valid, kp, 0.0).T.astype(BF16)
            vta[h, rel, 0:HD, rows] = jnp.where(valid, vp, 0.0).T.astype(BF16)
            lanes = lax.broadcasted_iota(jnp.int32, (16, T), 1) + base < length
            vta[h, rel, HD : HD + 16, rows] = jnp.where(lanes, 1.0, 0.0).astype(BF16)

    halves = [slice(part * (G * T // 2), (part + 1) * (G * T // 2)) for part in range(2)]

    def attend(h, rel, yy):
        for lanes in halves:
            sc = dot(kfx[h, rel], qt[h, yy, :, lanes])
            m = jnp.max(sc, axis=0, keepdims=True)
            e = jnp.exp2((sc - m) * LOG2E_FACTOR).astype(BF16)
            est[h, rel, yy, :, lanes] = e
            mb[h, rel, yy, :, lanes] = m
            o = dot(vta[h, rel], e)
            mo = mrun[h, yy, :, lanes]
            mn = jnp.maximum(mo, m)
            keep = jnp.exp2((mo - mn) * LOG2E_FACTOR)
            add = jnp.exp2((m - mn) * LOG2E_FACTOR)
            acc[h, yy, :, lanes] = acc[h, yy, :, lanes] * keep + o * add
            mrun[h, yy, :, lanes] = mn

    def over_chunks(body):
        def step(yy, carry):
            body(yy)
            return carry

        lax.fori_loop(0, NY, step, 0)

    def own_step(h, carry):
        @pl.when(h == 1)
        def _():
            forward_hops(0)

        await_columns(h, q_buf, qin, qsl, qsr)
        prep_q(h)
        prep_kv(h, 0, zh)
        over_chunks(lambda yy: attend(h, 0, yy))
        return carry

    def near_step(m, carry):
        h = lax.div(m, 2)
        rel = 1 + lax.rem(m, 2)

        @pl.when(m == 2)
        def _():
            forward_hops(1)

        prep_kv(h, rel, zo(5 - 2 * rel))
        over_chunks(lambda yy: attend(h, rel, yy))
        return carry

    def far_step(h, carry):
        await_columns(h, res_buf, rin, rnl, rnr)
        prep_res(h)
        for way in range(2):
            await_ref(kvb.at[h, 3, :, pl.ds(2 * way, 2)], z2r.at[h, way])
        prep_kv(h, 3, zo(2))

        def chunk(yy):
            attend(h, 3, yy)
            li = 1.0 / acc[h, yy, HD : HD + 1, :]
            linv[h, yy] = li
            o = acc[h, yy, 0:HD, :] * li
            acc[h, yy, 0:HD, :] = o
            x = smt[h, yy] + o.astype(BF16).astype(F32)
            smt[h, yy] = x
            sq = jnp.sum(x * x, axis=0, keepdims=True)
            rsq[yy] = rsq[yy] + sum(sq[:, j * T : (j + 1) * T] for j in range(G))

        over_chunks(chunk)
        return carry

    rsq[...] = jnp.zeros((NY, 1, T), F32)
    lax.fori_loop(0, H, own_step, 0)
    lax.fori_loop(0, 2 * H, near_step, 0)
    lax.fori_loop(0, H, far_step, 0)

    def sum_along_y(src, gathered, ssem, rsem):
        for k in (2, 1, 3):
            send(src, gathered.at[y], ssem.at[k - 1], rsem.at[k - 1], ydev(yo(k)))
        gathered[y] = src[...]
        for k in (1, 3, 2):
            await_ref(gathered.at[yo(NY - k)], rsem.at[k - 1])
        return (gathered[0] + gathered[1]) + (gathered[2] + gathered[3])

    mean_square = sum_along_y(rsq, rsa, sqs, sqr) * (1.0 / (NY * NG * HD))
    inv = lax.rsqrt(mean_square + EPS)
    lane = lax.broadcasted_iota(jnp.int32, (NY, 1, T), 2)
    chunk_id = lax.broadcasted_iota(jnp.int32, (NY, 1, T), 0)
    live = (chunk_id * NZ + zh) * T + lane < length
    inv = jnp.where(live, inv, 0.0)
    invr[...] = inv

    for h in range(H):
        for j in range(G):
            part = smt[h, 0, :, j * T : (j + 1) * T] * inv[0]
            for yy in range(1, NY):
                part = part + smt[h, yy, :, j * T : (j + 1) * T] * inv[yy]
            pz[h * G + j : h * G + j + 1, :] = jnp.sum(part.T, axis=0, keepdims=True)
    gain = gain_ref[y]
    pz[...] = pz[...] * gain / lenf
    for k in (2, 1, 3):
        send(pz, pza.at[zh], pzs.at[k - 1], pzr.at[k - 1], zdev(zo(k)))
    pza[zh] = pz[...]
    for k in (1, 3, 2):
        await_ref(pza.at[zo(NZ - k)], pzr.at[k - 1])
    mine = (pza[0] + pza[1]) + (pza[2] + pza[3])
    emba[b] = mine
    for k in range(1, nb):
        send(emba.at[b], emba.at[b], ems.at[k - 1], emr.at[k - 1], (bo(k), s))
    for k in range(1, nb):
        await_ref(emba.at[bo(nb - k)], emr.at[k - 1])

    doc_ids = lax.broadcasted_iota(jnp.int32, (nb, HD), 0)
    lane_ids = lax.broadcasted_iota(jnp.int32, (nb, HD), 1)
    dots = jnp.zeros((nb, HD), F32)
    squares = jnp.zeros((nb, HD), F32)
    for j in range(nb):
        row = emba[j]
        dots = jnp.where(doc_ids == j, jnp.sum(row * mine, axis=0, keepdims=True), dots)
        squares = jnp.where(doc_ids == j, jnp.sum(row * row, axis=0, keepdims=True), squares)
    dots = jnp.broadcast_to(jnp.sum(dots, axis=1, keepdims=True), (nb, HD))
    squares = jnp.broadcast_to(jnp.sum(squares, axis=1, keepdims=True), (nb, HD))
    sga[NY] = jnp.where(lane_ids < HD // 2, dots, squares)
    both = sum_along_y(sga.at[NY], sga, sis, sir)
    dots = jnp.broadcast_to(both[:, 0:1], (nb, HD))
    rho = lax.rsqrt(jnp.broadcast_to(both[:, HD // 2 : HD // 2 + 1], (nb, HD)) + EPS)
    row_rho = jnp.broadcast_to(jnp.sum(jnp.where(doc_ids == b, rho, 0.0), axis=0, keepdims=True), (nb, HD))
    sims = dots * rho * row_rho
    logits = 10.0 * sims - 2.0
    posv = jnp.zeros((nb, HD), jnp.int32)
    for j in range(nb):
        posv = jnp.where(doc_ids == j, pos_ref[j], posv)
    sign = jnp.where(doc_ids == pos_ref[b], 1.0, -1.0)

    def pull(label):
        return -10.0 / nb * label / (1.0 + jnp.exp(label * logits))

    pair = pull(sign) + pull(jnp.where(posv == b, 1.0, -1.0))
    pair = jnp.where(doc_ids == b, 0.0, pair) * (16.0 * NY * NZ * T)
    coef = pair * rho * row_rho
    self_coef = row_rho * row_rho * jnp.broadcast_to(jnp.sum(pair * sims, axis=0, keepdims=True), (nb, HD))
    grad = -self_coef[0:1, :] * mine
    for j in range(nb):
        grad = grad + coef[j : j + 1, :] * emba[j]
    gained = grad / lenf * gain

    for i in range(NG):
        gbt[i] = jnp.broadcast_to(gained[i : i + 1, :], (T, HD)).T
    for yy in range(NY):
        part = gbt[0] * smt[0, yy, :, 0:T]
        for i in range(1, NG):
            j = i % G
            part = part + gbt[i] * smt[i // G, yy, :, j * T : (j + 1) * T]
        mrw[yy] = jnp.sum(part, axis=0, keepdims=True)
    mean = sum_along_y(mrw, msa, mns, mnr) * invr[...] * (1.0 / (NY * NG * HD))
    mrw_scale = invr[...] * invr[...] * mean

    def r1(h, way):
        dev, piece = (right, 0) if way == 0 else (left, 2)
        return rcopy(dkvo.at[h, 2, :, pl.ds(piece, 2)], rs1.at[h, way], r1s.at[h, way], r1r.at[h, way], dev)

    def r2(h, way):
        dev = right if way == 0 else left
        return rcopy(dkvo.at[h, 1 - way], rs2.at[h, way], r2s.at[h, way], r2r.at[h, way], dev)

    def gq_send(h, kk):
        yy = yo(kk)
        return rcopy(gqo.at[h, yy], out_gq.at[:, col(2 * y + h, GW)], gqs.at[h, kk - 1], gqr.at[h, kk - 1], ydev(yy))

    def gq_local(h):
        return lcopy(gqo.at[h, y], out_gq.at[:, col(2 * y + h, GW)], gql.at[h])

    def gr_send(h, kk):
        yy = yo(kk)
        return rcopy(gro.at[h, yy], out_gr.at[:, col(2 * y + h, GW)], grs.at[h, kk - 1], grr.at[h, kk - 1], ydev(yy))

    def gr_local(h):
        return lcopy(gro.at[h, y], out_gr.at[:, col(2 * y + h, GW)], grl.at[h])

    def pull_back(h, rel, yy):
        vals = kvb[h, rel, 1].reshape(BK, HD)
        for lanes in halves:
            r = jnp.exp2((mb[h, rel, yy, :, lanes] - mrun[h, yy, :, lanes]) * LOG2E_FACTOR) * linv[h, yy, :, lanes]
            do = (dot_t[h, yy, :, lanes].astype(F32) * r).astype(BF16)
            delta = jnp.sum(do.astype(F32) * acc[h, yy, 0:HD, lanes], axis=0, keepdims=True)
            e = est[h, rel, yy, :, lanes]
            dp = dot(vals, do)
            ds = (e.astype(F32) * (dp - delta)).astype(BF16)
            dva[...] += dot(e, do, ((1,), (1,)))
            dka[...] += dot(ds, qs[h, yy, lanes, :])
            dqa[h, yy, :, lanes] += dot(kzt[h, rel], ds)

    def clear():
        dka[...] = jnp.zeros((BK, HD), F32)
        dva[...] = jnp.zeros((BK, HD), F32)

    def store(h, slot, added):
        for c, ref in ((0, dka), (1, dva)):
            for p in range(NY):
                x = ref[p * T : (p + 1) * T, :]
                if c == 0:
                    x = x * FACTOR
                if added is not None and p // 2 == added:
                    x = x + rs1[h, added, c, p % 2].astype(F32)
                dkvo[h, slot, c, p] = x.astype(BF16)

    def far_back(h, carry):
        for yy in range(NY):
            a = jnp.concatenate([invr[yy]] * G, axis=1)
            c = jnp.concatenate([mrc[yy]] * G, axis=1)
            g = jnp.concatenate([gbt[h * G + j] for j in range(G)], axis=1)
            dot_t[h, yy] = (g * a - smt[h, yy] * c).astype(BF16)
            dqa[h, yy] = jnp.zeros((HD, G * T), F32)
        clear()
        over_chunks(lambda yy: pull_back(h, 3, yy))
        store(h, 2, None)
        r1(h, 0).start()
        r1(h, 1).start()

        def give(t, carry):
            kk = lax.rem(t + 1, NY)
            yy = yo(kk)
            for j in range(G):
                gro[h, yy, :, j * HD : (j + 1) * HD] = dot_t[h, yy, :, j * T : (j + 1) * T].astype(F32).T.astype(BF16)

            @pl.when(kk > 0)
            def _():
                gr_send(h, kk).start()

            @pl.when(kk == 0)
            def _():
                gr_local(h).start()

            return carry

        lax.fori_loop(0, NY, give, 0)
        return carry

    def near_back(m, carry):
        h = lax.div(m, 2)
        way = lax.rem(m, 2)
        rel = 2 - way
        clear()
        over_chunks(lambda yy: pull_back(h, rel, yy))
        for w in range(2):

            @pl.when(way == w)
            def _(w=w):
                await_ref(rs1.at[h, w], r1r.at[h, w])
                store(h, 1 - w, w)
                r2(h, w).start()

        return carry

    def own_back(h, carry):
        clear()

        def chunk(t, carry):
            kk = lax.rem(t + 1, NY)
            yy = yo(kk)
            pull_back(h, 0, yy)
            for j in range(G):
                part = dqa[h, yy, :, j * T : (j + 1) * T] * FACTOR
                gqo[h, yy, :, j * HD : (j + 1) * HD] = part.T.astype(BF16)

            @pl.when(kk > 0)
            def _():
                gq_send(h, kk).start()

            @pl.when(kk == 0)
            def _():
                gq_local(h).start()

            return carry

        lax.fori_loop(0, NY, chunk, 0)
        own[h, 0] = dka[...] * FACTOR
        own[h, 1] = dva[...]
        return carry

    mrc[...] = mrw_scale
    lax.fori_loop(0, H, far_back, 0)

    x = -sign * logits
    term = jnp.maximum(x, 0.0) + jnp.log(1.0 + jnp.exp(-jnp.abs(x)))
    term = jnp.sum(jnp.where(doc_ids == b, 0.0, term), axis=0, keepdims=True)
    lra[b] = jnp.broadcast_to(term, (8, HD))
    for k in range(1, nb):
        send(lra.at[b], lra.at[b], los.at[k - 1], lor.at[k - 1], (bo(k), s))

    lax.fori_loop(0, 2 * H, near_back, 0)
    lax.fori_loop(0, H, own_back, 0)

    for k in range(1, nb):
        await_ref(lra.at[bo(nb - k)], lor.at[k - 1])
    loss = lra[0]
    for j in range(1, nb):
        loss = loss + lra[j]
    loss_ref[0, 0] = jnp.sum(loss) * (1.0 / (8 * HD * nb))

    for h in range(H):
        await_ref(rs2.at[h, 0], r2r.at[h, 0])
        await_ref(rs2.at[h, 1], r2r.at[h, 1])
        for p in range(NY):
            valid = lax.broadcasted_iota(jnp.int32, (T, HD), 0) + (p * NZ + zh) * T < length
            for c in range(2):
                x = own[h, c, p * T : (p + 1) * T, :] + rs2[h, 0, c, p].astype(F32) + rs2[h, 1, c, p].astype(F32)
                fin[h, c, p] = jnp.where(valid, x, 0.0).astype(BF16)
        for c, out in ((0, out_gk), (1, out_gv)):
            for k in (2, 1, 3):
                yy = yo(k)
                send(fin.at[h, c, yy], out.at[:, col(2 * y + h, HD)], gks.at[h, c, k - 1], gkr.at[h, c, k - 1], ydev(yy))
            lcopy(fin.at[h, c, y], out.at[:, col(2 * y + h, HD)], gkl.at[h, c]).start()

    for h in range(H):
        gq_local(h).wait()
        gr_local(h).wait()
        for k in range(1, NY):
            await_ref(out_gr.at[:, col(2 * yo(NY - k) + h, GW)], grr.at[h, k - 1])
            await_ref(out_gq.at[:, col(2 * yo(NY - k) + h, GW)], gqr.at[h, k - 1])
        for c, out in ((0, out_gk), (1, out_gv)):
            lcopy(fin.at[h, c, y], out.at[:, col(2 * y + h, HD)], gkl.at[h, c]).wait()
            for k in range(1, NY):
                await_ref(out.at[:, col(2 * yo(NY - k) + h, HD)], gkr.at[h, c, k - 1])
    for copy in sends:
        copy.wait_send()
    for h in range(H):
        for way in range(2):
            hop2(h, way).wait_send()
            r1(h, way).wait_send()
            r2(h, way).wait_send()
        for k in range(1, NY):
            gr_send(h, k).wait_send()
            gq_send(h, k).wait_send()


def copy_kernel(parts, n, *refs):
    srcs, dsts, bufs, sems = refs[:n], refs[n : 2 * n], refs[2 * n : 3 * n], refs[-1]
    pairs = []
    for i in range(n):
        rows = srcs[i].shape[0] // parts
        for p in range(parts):
            span = pl.ds(p * rows, rows)
            pairs.append(
                (
                    pltpu.make_async_copy(srcs[i].at[span], bufs[i].at[span], sems.at[0, i, p]),
                    pltpu.make_async_copy(bufs[i].at[span], dsts[i].at[span], sems.at[1, i, p]),
                )
            )
    for load, _ in pairs:
        load.start()
    for load, give in pairs:
        load.wait()
        give.start()
    for _, give in pairs:
        give.wait()


def own_buffers(arrays):
    parts = 2
    any_spec = pl.BlockSpec(memory_space=pl.ANY)
    return pl.pallas_call(
        functools.partial(copy_kernel, parts, len(arrays)),
        out_shape=tuple(jax.ShapeDtypeStruct(x.shape, x.dtype) for x in arrays),
        in_specs=[any_spec] * len(arrays),
        out_specs=(any_spec,) * len(arrays),
        scratch_shapes=[pltpu.VMEM(x.shape, x.dtype) for x in arrays]
        + [pltpu.SemaphoreType.DMA((2, len(arrays), parts))],
        compiler_params=pltpu.CompilerParams(vmem_limit_bytes=56 * 1024 * 1024),
        cost_estimate=pl.CostEstimate(flops=0, bytes_accessed=5 * 2**20, transcendentals=0),
        name="copy_out",
    )(*arrays)


def on_device(nb, residual, query_proj, key_proj, value_proj, norm_gain, lengths, positives):
    T, D = residual.shape
    BK, QC, NG = NY * T, G * T, H * G
    V = pltpu.VMEM
    S = pltpu.SemaphoreType.DMA
    columns = V((H, NY, T, GW), BF16)
    scratch = [
        V(key_proj.shape, BF16), V(key_proj.shape, BF16), V((T, D), BF16), V((T, D), BF16),
        V((H, NZ, 2, NY, T, HD), BF16),
        V((H, NZ, BK, HD), BF16),
        V((H, NZ, HD, BK), BF16),
        V((H, NZ, HD + 16, BK), BF16),
        columns,
        V((H, NY, QC, HD), BF16),
        V((H, NY, HD, QC), BF16),
        V((H, NZ, NY, BK, QC), BF16),
        V((H, NZ, NY, 1, QC), F32),
        V((H, NY, 1, QC), F32),
        V((H, NY, 1, QC), F32),
        V((H, NY, HD + 16, QC), F32),
        columns,
        V((H, NY, HD, QC), F32),
        V((NY, 1, T), F32), V((NY, NY, 1, T), F32), V((NY, 1, T), F32),
        V((NG, HD), F32), V((NZ, NG, HD), F32),
        V((nb, NG, HD), F32),
        V((NY + 1, nb, HD), F32),
        V((nb, 8, HD), F32),
        V((NG, HD, T), F32),
        V((NY, 1, T), F32), V((NY, NY, 1, T), F32), V((NY, 1, T), F32),
        V((H, NY, HD, QC), BF16),
        columns,
        V((H, NY, HD, QC), F32),
        columns,
        V((BK, HD), F32),
        V((BK, HD), F32),
        V((H, 3, 2, NY, T, HD), BF16),
        V((H, 2, BK, HD), F32),
        V((H, 2, 2, 2, T, HD), BF16),
        V((H, 2, 2, NY, T, HD), BF16),
        V((H, 2, NY, T, HD), BF16),
        S((4,)), S((H, 2, NY - 1)), S((H, 2, NY - 1)), S((H, 2)),
        S((H, NY - 1)), S((H, NY - 1)), S((H,)),
        S((H, NY - 1)), S((H, NY - 1)), S((H,)),
        S((H, 2, NY)), S((H, 2, NY)), S((H, 2)), S((H, 2)),
        S((NY - 1,)), S((NY - 1,)), S((NZ - 1,)), S((NZ - 1,)),
        S((nb - 1,)), S((nb - 1,)), S((NY - 1,)), S((NY - 1,)),
        S((nb - 1,)), S((nb - 1,)), S((NY - 1,)), S((NY - 1,)),
        S((H, NY - 1)), S((H, NY - 1)), S((H,)),
        S((H, 2)), S((H, 2)), S((H, 2)), S((H, 2)),
        S((H, NY - 1)), S((H, NY - 1)), S((H,)),
        S((H, 2, NY - 1)), S((H, 2, NY - 1)), S((H, 2)),
    ]
    any_spec = pl.BlockSpec(memory_space=pl.ANY)
    smem = pl.BlockSpec(memory_space=pltpu.SMEM)
    loss, *grads = pl.pallas_call(
        functools.partial(kernel, nb, T),
        out_shape=(
            jax.ShapeDtypeStruct((1, 1), F32),
            jax.ShapeDtypeStruct((T, D), BF16),
            jax.ShapeDtypeStruct((T, D), BF16),
            jax.ShapeDtypeStruct(key_proj.shape, BF16),
            jax.ShapeDtypeStruct(key_proj.shape, BF16),
        ),
        in_specs=[smem, smem, any_spec, any_spec, any_spec, any_spec, pl.BlockSpec(memory_space=pltpu.VMEM)],
        out_specs=(smem, any_spec, any_spec, any_spec, any_spec),
        scratch_shapes=scratch,
        compiler_params=pltpu.CompilerParams(
            collective_id=0, has_side_effects=True, vmem_limit_bytes=56 * 1024 * 1024
        ),
        cost_estimate=pl.CostEstimate(flops=13 * 10**9, bytes_accessed=6 * 2**20, transcendentals=2**23),
        name="attention_backward",
    )(lengths, positives, residual, query_proj, key_proj, value_proj, norm_gain.reshape(NY, NG, HD))
    return loss.reshape(()), *own_buffers(grads)


def solution(mesh):
    rows = P(("batch", "seq"), None)
    return jax.shard_map(
        functools.partial(on_device, mesh.shape["batch"]),
        mesh=mesh,
        in_specs=(rows, rows, rows, rows, P(), P("batch"), P()),
        out_specs=(P(), rows, rows, rows, rows),
        check_vma=False,
    )
```

```python
import functools
import math

import jax
import jax.numpy as jnp
from jax import lax
from jax.experimental import pallas as pl
from jax.experimental.pallas import tpu as pltpu
from jax.sharding import PartitionSpec as P

MESH = pl.DeviceIdType.MESH
HD = 128
NY = 4
NZ = 4
H = 2
G = 4
GW = G * HD
EPS = 1e-6
F32 = jnp.float32
BF16 = jnp.bfloat16
FACTOR = 1.0 / math.sqrt(HD)
LOG2E_FACTOR = FACTOR * math.log2(math.e)


def dot(a, b, dims=((1,), (0,))):
    return lax.dot_general(a, b, (dims, ((), ())), preferred_element_type=F32)


def kernel(
    nb, t_rows,
    len_ref, pos_ref, res_hbm, q_hbm, k_hbm, v_hbm, gain_ref,
    loss_ref, out_gr, out_gq, out_gk, out_gv,
    k_buf, v_buf, q_buf, res_buf, kvb, kfx, kzt, vta, qin, qs, qt, est, mb, mrun, linv, acc, rin, smt,
    rsq, rsa, invr, pz, pza, emba, sga, lra, gbt, mrw, msa, mrc, dot_t, gro, dqa, gqo, dka, dva, dkvo, own, rs1, rs2, fin,
    lds, kvs, kvr, kvl, qss, qsr, qsl, rns, rnr, rnl, z1s, z1r, z2s, z2r,
    sqs, sqr, pzs, pzr, ems, emr, sis, sir, los, lor, mns, mnr,
    grs, grr, grl, r1s, r1r, r2s, r2r, gqs, gqr, gql, gks, gkr, gkl,
):
    T = t_rows
    BK = NY * T
    NG = H * G
    b = lax.axis_index("batch")
    s = lax.axis_index("seq")
    y = lax.div(s, NZ)
    zh = lax.rem(s, NZ)
    right = (b, y * NZ + lax.rem(zh + 1, NZ))
    left = (b, y * NZ + lax.rem(zh + NZ - 1, NZ))

    def yo(k):
        return lax.rem(y + k, NY)

    def zo(k):
        return lax.rem(zh + k, NZ)

    def bo(k):
        return lax.rem(b + k, nb)

    def ydev(yy):
        return (b, yy * NZ + zh)

    def zdev(zz):
        return (b, y * NZ + zz)

    def col(index, width):
        return pl.ds(pl.multiple_of(index * width, width), width)

    def rcopy(src, dst, ssem, rsem, dev):
        return pltpu.make_async_remote_copy(
            src_ref=src, dst_ref=dst, send_sem=ssem, recv_sem=rsem, device_id=dev, device_id_type=MESH
        )

    def lcopy(src, dst, sem):
        return pltpu.make_async_copy(src, dst, sem)

    def await_ref(ref, sem):
        pltpu.make_async_copy(ref, ref, sem).wait()

    sends = []

    def send(src, dst, ssem, rsem, dev):
        copy = rcopy(src, dst, ssem, rsem, dev)
        copy.start()
        sends.append(copy)

    length = len_ref[0]
    lenf = length.astype(F32)

    loads = [
        lcopy(src, dst, lds.at[i])
        for i, (src, dst) in enumerate(((k_hbm, k_buf), (v_hbm, v_buf), (q_hbm, q_buf), (res_hbm, res_buf)))
    ]
    for load in loads:
        load.start()

    barrier = pltpu.get_barrier_semaphore()
    for k in range(1, NY):
        pl.semaphore_signal(barrier, inc=1, device_id=ydev(yo(k)), device_id_type=MESH)
    for k in range(1, NZ):
        pl.semaphore_signal(barrier, inc=1, device_id=zdev(zo(k)), device_id_type=MESH)
    for k in range(1, nb):
        pl.semaphore_signal(barrier, inc=1, device_id=(bo(k), s), device_id_type=MESH)
    pl.semaphore_wait(barrier, NY - 1 + NZ - 1 + nb - 1)

    for load in loads:
        load.wait()
    for h in range(H):
        for c, src in ((0, k_buf), (1, v_buf)):
            lcopy(src.at[:, col(2 * y + h, HD)], kvb.at[h, 0, c, y], kvl.at[h, c]).start()
            for k in (1, 3, 2):
                yy = yo(k)
                send(src.at[:, col(2 * yy + h, HD)], kvb.at[h, 0, c, y], kvs.at[h, c, k - 1], kvr.at[h, c, k - 1], ydev(yy))
        lcopy(q_buf.at[:, col(2 * y + h, GW)], qin.at[h, y], qsl.at[h]).start()
        for k in (1, 3, 2):
            yy = yo(k)
            send(q_buf.at[:, col(2 * yy + h, GW)], qin.at[h, y], qss.at[h, k - 1], qsr.at[h, k - 1], ydev(yy))
    for h in range(H):
        lcopy(res_buf.at[:, col(2 * y + h, GW)], rin.at[h, y], rnl.at[h]).start()
        for k in (1, 3, 2):
            yy = yo(k)
            send(res_buf.at[:, col(2 * yy + h, GW)], rin.at[h, y], rns.at[h, k - 1], rnr.at[h, k - 1], ydev(yy))

    for h in range(H):
        for k in (0, 1, 3, 2):
            p = yo(NY - k)
            for c, src in ((0, k_buf), (1, v_buf)):
                if k == 0:
                    lcopy(src.at[:, col(2 * y + h, HD)], kvb.at[h, 0, c, y], kvl.at[h, c]).wait()
                else:
                    await_ref(kvb.at[h, 0, c, p], kvr.at[h, c, k - 1])
            send(kvb.at[h, 0, :, p], kvb.at[h, 1, :, p], z1s.at[h, 0, k], z1r.at[h, 0, k], right)
            send(kvb.at[h, 0, :, p], kvb.at[h, 2, :, p], z1s.at[h, 1, k], z1r.at[h, 1, k], left)

    def hop2(h, way):
        src, dev, piece = (1, right, 0) if way == 0 else (2, left, 2)
        return rcopy(
            kvb.at[h, src, :, pl.ds(piece, 2)], kvb.at[h, 3, :, pl.ds(piece, 2)], z2s.at[h, way], z2r.at[h, way], dev
        )

    def forward_hops(h):
        for way in range(2):
            for k in range(NY):
                await_ref(kvb.at[h, 1 + way, :, yo(NY - k)], z1r.at[h, way, k])
            hop2(h, way).start()

    def await_columns(h, src, dst, lsem, rsem):
        lcopy(src.at[:, col(2 * y + h, GW)], dst.at[h, y], lsem.at[h]).wait()
        for k in range(1, NY):
            await_ref(dst.at[h, yo(NY - k)], rsem.at[h, k - 1])

    def prep_q(h):
        def body(yy, carry):
            for j in range(G):
                head = qin[h, yy, :, j * HD : (j + 1) * HD]
                qs[h, yy, j * T : (j + 1) * T, :] = head
                qt[h, yy, :, j * T : (j + 1) * T] = head.T
            mrun[h, yy] = jnp.full((1, G * T), -3e38, F32)
            acc[h, yy] = jnp.zeros((HD + 16, G * T), F32)
            return carry

        lax.fori_loop(0, NY, body, 0)

    def prep_res(h):
        def body(yy, carry):
            for j in range(G):
                smt[h, yy, :, j * T : (j + 1) * T] = rin[h, yy, :, j * HD : (j + 1) * HD].T.astype(F32)
            return carry

        lax.fori_loop(0, NY, body, 0)

    def prep_kv(h, rel, zb):
        first_key = kvb[h, rel, 0, 0, 0:1, :].astype(F32)
        for yy in range(NY):
            base = (yy * NZ + zb) * T
            rows = slice(yy * T, (yy + 1) * T)
            kp = kvb[h, rel, 0, yy]
            valid = lax.broadcasted_iota(jnp.int32, (T, HD), 0) + base < length
            kfx[h, rel, rows, :] = jnp.where(valid, kp.astype(F32), first_key).astype(BF16)
            lanes = lax.broadcasted_iota(jnp.int32, (16, T), 1) + base < length
            ones = jnp.where(lanes, 1.0, 0.0).astype(BF16)
            vta[h, rel, HD : HD + 16, rows] = ones
            kzt[h, rel, :, rows] = kp.T * ones[0:1, :]
            vta[h, rel, 0:HD, rows] = kvb[h, rel, 1, yy].T * ones[0:1, :]

    halves = [slice(part * (G * T // 2), (part + 1) * (G * T // 2)) for part in range(2)]

    def attend(h, rel, yy):
        for lanes in halves:
            sc = dot(kfx[h, rel], qt[h, yy, :, lanes])
            m = jnp.max(sc, axis=0, keepdims=True)
            e = jnp.exp2((sc - m) * LOG2E_FACTOR).astype(BF16)
            est[h, rel, yy, :, lanes] = e
            mb[h, rel, yy, :, lanes] = m
            o = dot(vta[h, rel], e)
            mo = mrun[h, yy, :, lanes]
            mn = jnp.maximum(mo, m)
            keep = jnp.exp2((mo - mn) * LOG2E_FACTOR)
            add = jnp.exp2((m - mn) * LOG2E_FACTOR)
            acc[h, yy, :, lanes] = acc[h, yy, :, lanes] * keep + o * add
            mrun[h, yy, :, lanes] = mn

    def over_chunks(body):
        def step(yy, carry):
            body(yy)
            return carry

        lax.fori_loop(0, NY, step, 0, unroll=2)

    def own_step(h, carry):
        @pl.when(h == 1)
        def _():
            forward_hops(0)

        await_columns(h, q_buf, qin, qsl, qsr)
        prep_q(h)
        prep_kv(h, 0, zh)
        over_chunks(lambda yy: attend(h, 0, yy))
        return carry

    def near_step(m, carry):
        h = lax.div(m, 2)
        rel = 1 + lax.rem(m, 2)

        @pl.when(m == 2)
        def _():
            forward_hops(1)

        prep_kv(h, rel, zo(5 - 2 * rel))
        over_chunks(lambda yy: attend(h, rel, yy))
        return carry

    def far_step(h, carry):
        await_columns(h, res_buf, rin, rnl, rnr)
        prep_res(h)
        for way in range(2):
            await_ref(kvb.at[h, 3, :, pl.ds(2 * way, 2)], z2r.at[h, way])
        prep_kv(h, 3, zo(2))

        def chunk(yy):
            attend(h, 3, yy)
            li = 1.0 / acc[h, yy, HD : HD + 1, :]
            linv[h, yy] = li
            o = acc[h, yy, 0:HD, :] * li
            acc[h, yy, 0:HD, :] = o
            x = smt[h, yy] + o.astype(BF16).astype(F32)
            smt[h, yy] = x
            sq = jnp.sum(x * x, axis=0, keepdims=True)
            rsq[yy] = rsq[yy] + sum(sq[:, j * T : (j + 1) * T] for j in range(G))

        over_chunks(chunk)
        return carry

    rsq[...] = jnp.zeros((NY, 1, T), F32)
    lax.fori_loop(0, H, own_step, 0)
    lax.fori_loop(0, 2 * H, near_step, 0)
    lax.fori_loop(0, H, far_step, 0)

    def sum_along_y(src, gathered, ssem, rsem):
        for k in (2, 1, 3):
            send(src, gathered.at[y], ssem.at[k - 1], rsem.at[k - 1], ydev(yo(k)))
        gathered[y] = src[...]
        for k in (1, 3, 2):
            await_ref(gathered.at[yo(NY - k)], rsem.at[k - 1])
        return (gathered[0] + gathered[1]) + (gathered[2] + gathered[3])

    mean_square = sum_along_y(rsq, rsa, sqs, sqr) * (1.0 / (NY * NG * HD))
    inv = lax.rsqrt(mean_square + EPS)
    lane = lax.broadcasted_iota(jnp.int32, (NY, 1, T), 2)
    chunk_id = lax.broadcasted_iota(jnp.int32, (NY, 1, T), 0)
    live = (chunk_id * NZ + zh) * T + lane < length
    inv = jnp.where(live, inv, 0.0)
    invr[...] = inv

    for h in range(H):
        for j in range(G):
            part = smt[h, 0, :, j * T : (j + 1) * T] * inv[0]
            for yy in range(1, NY):
                part = part + smt[h, yy, :, j * T : (j + 1) * T] * inv[yy]
            pz[h * G + j : h * G + j + 1, :] = jnp.sum(part.T, axis=0, keepdims=True)
    gain = gain_ref[y]
    pz[...] = pz[...] * gain / lenf
    for k in (2, 1, 3):
        send(pz, pza.at[zh], pzs.at[k - 1], pzr.at[k - 1], zdev(zo(k)))
    pza[zh] = pz[...]
    for k in (1, 3, 2):
        await_ref(pza.at[zo(NZ - k)], pzr.at[k - 1])
    mine = (pza[0] + pza[1]) + (pza[2] + pza[3])
    emba[b] = mine
    for k in range(1, nb):
        send(emba.at[b], emba.at[b], ems.at[k - 1], emr.at[k - 1], (bo(k), s))
    for k in range(1, nb):
        await_ref(emba.at[bo(nb - k)], emr.at[k - 1])

    doc_ids = lax.broadcasted_iota(jnp.int32, (nb, HD), 0)
    lane_ids = lax.broadcasted_iota(jnp.int32, (nb, HD), 1)
    dots = jnp.zeros((nb, HD), F32)
    squares = jnp.zeros((nb, HD), F32)
    for j in range(nb):
        row = emba[j]
        dots = jnp.where(doc_ids == j, jnp.sum(row * mine, axis=0, keepdims=True), dots)
        squares = jnp.where(doc_ids == j, jnp.sum(row * row, axis=0, keepdims=True), squares)
    dots = jnp.broadcast_to(jnp.sum(dots, axis=1, keepdims=True), (nb, HD))
    squares = jnp.broadcast_to(jnp.sum(squares, axis=1, keepdims=True), (nb, HD))
    sga[NY] = jnp.where(lane_ids < HD // 2, dots, squares)
    both = sum_along_y(sga.at[NY], sga, sis, sir)
    dots = jnp.broadcast_to(both[:, 0:1], (nb, HD))
    rho = lax.rsqrt(jnp.broadcast_to(both[:, HD // 2 : HD // 2 + 1], (nb, HD)) + EPS)
    row_rho = jnp.broadcast_to(jnp.sum(jnp.where(doc_ids == b, rho, 0.0), axis=0, keepdims=True), (nb, HD))
    sims = dots * rho * row_rho
    logits = 10.0 * sims - 2.0
    posv = jnp.zeros((nb, HD), jnp.int32)
    for j in range(nb):
        posv = jnp.where(doc_ids == j, pos_ref[j], posv)
    sign = jnp.where(doc_ids == pos_ref[b], 1.0, -1.0)

    def pull(label):
        return -10.0 / nb * label / (1.0 + jnp.exp(label * logits))

    pair = pull(sign) + pull(jnp.where(posv == b, 1.0, -1.0))
    pair = jnp.where(doc_ids == b, 0.0, pair) * (16.0 * NY * NZ * T)
    coef = pair * rho * row_rho
    self_coef = row_rho * row_rho * jnp.broadcast_to(jnp.sum(pair * sims, axis=0, keepdims=True), (nb, HD))
    grad = -self_coef[0:1, :] * mine
    for j in range(nb):
        grad = grad + coef[j : j + 1, :] * emba[j]
    gained = grad / lenf * gain

    for i in range(NG):
        gbt[i] = jnp.broadcast_to(gained[i : i + 1, :], (T, HD)).T
    for yy in range(NY):
        part = gbt[0] * smt[0, yy, :, 0:T]
        for i in range(1, NG):
            j = i % G
            part = part + gbt[i] * smt[i // G, yy, :, j * T : (j + 1) * T]
        mrw[yy] = jnp.sum(part, axis=0, keepdims=True)
    mean = sum_along_y(mrw, msa, mns, mnr) * invr[...] * (1.0 / (NY * NG * HD))
    mrw_scale = invr[...] * invr[...] * mean

    def r1(h, way):
        dev, piece = (right, 0) if way == 0 else (left, 2)
        return rcopy(dkvo.at[h, 2, :, pl.ds(piece, 2)], rs1.at[h, way], r1s.at[h, way], r1r.at[h, way], dev)

    def r2(h, way):
        dev = right if way == 0 else left
        return rcopy(dkvo.at[h, 1 - way], rs2.at[h, way], r2s.at[h, way], r2r.at[h, way], dev)

    def gq_send(h, kk):
        yy = yo(kk)
        return rcopy(gqo.at[h, yy], out_gq.at[:, col(2 * y + h, GW)], gqs.at[h, kk - 1], gqr.at[h, kk - 1], ydev(yy))

    def gq_local(h):
        return lcopy(gqo.at[h, y], out_gq.at[:, col(2 * y + h, GW)], gql.at[h])

    def gr_send(h, kk):
        yy = yo(kk)
        return rcopy(gro.at[h, yy], out_gr.at[:, col(2 * y + h, GW)], grs.at[h, kk - 1], grr.at[h, kk - 1], ydev(yy))

    def gr_local(h):
        return lcopy(gro.at[h, y], out_gr.at[:, col(2 * y + h, GW)], grl.at[h])

    def pull_back(h, rel, yy):
        vals = kvb[h, rel, 1].reshape(BK, HD)
        dos, scores = [], []
        for lanes in halves:
            r = jnp.exp2((mb[h, rel, yy, :, lanes] - mrun[h, yy, :, lanes]) * LOG2E_FACTOR) * linv[h, yy, :, lanes]
            do = (dot_t[h, yy, :, lanes].astype(F32) * r).astype(BF16)
            delta = jnp.sum(do.astype(F32) * acc[h, yy, 0:HD, lanes], axis=0, keepdims=True)
            dp = dot(vals, do)
            ds = est[h, rel, yy, :, lanes] * (dp - delta).astype(BF16)
            dqa[h, yy, :, lanes] += dot(kzt[h, rel], ds)
            dos.append(do)
            scores.append(ds)
        dva[...] += dot(est[h, rel, yy], jnp.concatenate(dos, axis=1), ((1,), (1,)))
        dka[...] += dot(jnp.concatenate(scores, axis=1), qs[h, yy])

    def clear():
        dka[...] = jnp.zeros((BK, HD), F32)
        dva[...] = jnp.zeros((BK, HD), F32)

    def store(h, slot, added):
        for c, ref in ((0, dka), (1, dva)):
            for p in range(NY):
                x = ref[p * T : (p + 1) * T, :]
                if c == 0:
                    x = x * FACTOR
                if added is not None and p // 2 == added:
                    x = x + rs1[h, added, c, p % 2].astype(F32)
                dkvo[h, slot, c, p] = x.astype(BF16)

    def far_back(h, carry):
        for yy in range(NY):
            a = jnp.concatenate([invr[yy]] * G, axis=1)
            c = jnp.concatenate([mrc[yy]] * G, axis=1)
            g = jnp.concatenate([gbt[h * G + j] for j in range(G)], axis=1)
            dot_t[h, yy] = (g * a - smt[h, yy] * c).astype(BF16)
            dqa[h, yy] = jnp.zeros((HD, G * T), F32)
        clear()
        over_chunks(lambda yy: pull_back(h, 3, yy))
        store(h, 2, None)
        r1(h, 0).start()
        r1(h, 1).start()

        def give(t, carry):
            kk = lax.rem(t + 1, NY)
            yy = yo(kk)
            for j in range(G):
                gro[h, yy, :, j * HD : (j + 1) * HD] = dot_t[h, yy, :, j * T : (j + 1) * T].T

            @pl.when(kk > 0)
            def _():
                gr_send(h, kk).start()

            @pl.when(kk == 0)
            def _():
                gr_local(h).start()

            return carry

        lax.fori_loop(0, NY, give, 0)
        return carry

    def near_back(m, carry):
        h = lax.div(m, 2)
        way = lax.rem(m, 2)
        rel = 2 - way
        clear()
        over_chunks(lambda yy: pull_back(h, rel, yy))
        for w in range(2):

            @pl.when(way == w)
            def _(w=w):
                await_ref(rs1.at[h, w], r1r.at[h, w])
                store(h, 1 - w, w)
                r2(h, w).start()

        return carry

    def own_back(h, carry):
        clear()

        def chunk(t, carry):
            for u in range(2):
                pull_back(h, 0, yo(lax.rem(2 * t + u + 1, NY)))
            for u in range(2):
                kk = lax.rem(2 * t + u + 1, NY)
                yy = yo(kk)
                for j in range(G):
                    part = dqa[h, yy, :, j * T : (j + 1) * T] * FACTOR
                    gqo[h, yy, :, j * HD : (j + 1) * HD] = part.astype(BF16).T

                @pl.when(kk > 0)
                def _(kk=kk):
                    gq_send(h, kk).start()

                @pl.when(kk == 0)
                def _():
                    gq_local(h).start()

            return carry

        lax.fori_loop(0, NY // 2, chunk, 0)
        own[h, 0] = dka[...] * FACTOR
        own[h, 1] = dva[...]
        return carry

    mrc[...] = mrw_scale
    lax.fori_loop(0, H, far_back, 0)

    x = -sign * logits
    term = jnp.maximum(x, 0.0) + jnp.log(1.0 + jnp.exp(-jnp.abs(x)))
    term = jnp.sum(jnp.where(doc_ids == b, 0.0, term), axis=0, keepdims=True)
    lra[b] = jnp.broadcast_to(term, (8, HD))
    for k in range(1, nb):
        send(lra.at[b], lra.at[b], los.at[k - 1], lor.at[k - 1], (bo(k), s))

    lax.fori_loop(0, 2 * H, near_back, 0)
    lax.fori_loop(0, H, own_back, 0)

    for k in range(1, nb):
        await_ref(lra.at[bo(nb - k)], lor.at[k - 1])
    loss = lra[0]
    for j in range(1, nb):
        loss = loss + lra[j]
    loss_ref[0, 0] = jnp.sum(loss) * (1.0 / (8 * HD * nb))

    for h in range(H):
        await_ref(rs2.at[h, 0], r2r.at[h, 0])
        await_ref(rs2.at[h, 1], r2r.at[h, 1])
        for p in range(NY):
            valid = lax.broadcasted_iota(jnp.int32, (T, HD), 0) + (p * NZ + zh) * T < length
            for c in range(2):
                x = own[h, c, p * T : (p + 1) * T, :] + rs2[h, 0, c, p].astype(F32) + rs2[h, 1, c, p].astype(F32)
                fin[h, c, p] = jnp.where(valid, x, 0.0).astype(BF16)
        for c, out in ((0, out_gk), (1, out_gv)):
            for k in (2, 1, 3):
                yy = yo(k)
                send(fin.at[h, c, yy], out.at[:, col(2 * y + h, HD)], gks.at[h, c, k - 1], gkr.at[h, c, k - 1], ydev(yy))
            lcopy(fin.at[h, c, y], out.at[:, col(2 * y + h, HD)], gkl.at[h, c]).start()

    for h in range(H):
        gq_local(h).wait()
        gr_local(h).wait()
        for k in range(1, NY):
            await_ref(out_gr.at[:, col(2 * yo(NY - k) + h, GW)], grr.at[h, k - 1])
            await_ref(out_gq.at[:, col(2 * yo(NY - k) + h, GW)], gqr.at[h, k - 1])
        for c, out in ((0, out_gk), (1, out_gv)):
            lcopy(fin.at[h, c, y], out.at[:, col(2 * y + h, HD)], gkl.at[h, c]).wait()
            for k in range(1, NY):
                await_ref(out.at[:, col(2 * yo(NY - k) + h, HD)], gkr.at[h, c, k - 1])
    for copy in sends:
        copy.wait_send()
    for h in range(H):
        for way in range(2):
            hop2(h, way).wait_send()
            r1(h, way).wait_send()
            r2(h, way).wait_send()
        for k in range(1, NY):
            gr_send(h, k).wait_send()
            gq_send(h, k).wait_send()


def copy_kernel(parts, n, *refs):
    srcs, dsts, bufs, sems = refs[:n], refs[n : 2 * n], refs[2 * n : 3 * n], refs[-1]
    pairs = []
    for i in range(n):
        rows = srcs[i].shape[0] // parts
        for p in range(parts):
            span = pl.ds(p * rows, rows)
            pairs.append(
                (
                    pltpu.make_async_copy(srcs[i].at[span], bufs[i].at[span], sems.at[0, i, p]),
                    pltpu.make_async_copy(bufs[i].at[span], dsts[i].at[span], sems.at[1, i, p]),
                )
            )
    for load, _ in pairs:
        load.start()
    for load, give in pairs:
        load.wait()
        give.start()
    for _, give in pairs:
        give.wait()


def own_buffers(arrays):
    parts = 2
    any_spec = pl.BlockSpec(memory_space=pl.ANY)
    return pl.pallas_call(
        functools.partial(copy_kernel, parts, len(arrays)),
        out_shape=tuple(jax.ShapeDtypeStruct(x.shape, x.dtype) for x in arrays),
        in_specs=[any_spec] * len(arrays),
        out_specs=(any_spec,) * len(arrays),
        scratch_shapes=[pltpu.VMEM(x.shape, x.dtype) for x in arrays]
        + [pltpu.SemaphoreType.DMA((2, len(arrays), parts))],
        compiler_params=pltpu.CompilerParams(vmem_limit_bytes=56 * 1024 * 1024),
        cost_estimate=pl.CostEstimate(flops=0, bytes_accessed=5 * 2**20, transcendentals=0),
        name="copy_out",
    )(*arrays)


def on_device(nb, residual, query_proj, key_proj, value_proj, norm_gain, lengths, positives):
    T, D = residual.shape
    BK, QC, NG = NY * T, G * T, H * G
    V = pltpu.VMEM
    S = pltpu.SemaphoreType.DMA
    columns = V((H, NY, T, GW), BF16)
    scratch = [
        V(key_proj.shape, BF16), V(key_proj.shape, BF16), V((T, D), BF16), V((T, D), BF16),
        V((H, NZ, 2, NY, T, HD), BF16),
        V((H, NZ, BK, HD), BF16),
        V((H, NZ, HD, BK), BF16),
        V((H, NZ, HD + 16, BK), BF16),
        columns,
        V((H, NY, QC, HD), BF16),
        V((H, NY, HD, QC), BF16),
        V((H, NZ, NY, BK, QC), BF16),
        V((H, NZ, NY, 1, QC), F32),
        V((H, NY, 1, QC), F32),
        V((H, NY, 1, QC), F32),
        V((H, NY, HD + 16, QC), F32),
        columns,
        V((H, NY, HD, QC), F32),
        V((NY, 1, T), F32), V((NY, NY, 1, T), F32), V((NY, 1, T), F32),
        V((NG, HD), F32), V((NZ, NG, HD), F32),
        V((nb, NG, HD), F32),
        V((NY + 1, nb, HD), F32),
        V((nb, 8, HD), F32),
        V((NG, HD, T), F32),
        V((NY, 1, T), F32), V((NY, NY, 1, T), F32), V((NY, 1, T), F32),
        V((H, NY, HD, QC), BF16),
        columns,
        V((H, NY, HD, QC), F32),
        columns,
        V((BK, HD), F32),
        V((BK, HD), F32),
        V((H, 3, 2, NY, T, HD), BF16),
        V((H, 2, BK, HD), F32),
        V((H, 2, 2, 2, T, HD), BF16),
        V((H, 2, 2, NY, T, HD), BF16),
        V((H, 2, NY, T, HD), BF16),
        S((4,)), S((H, 2, NY - 1)), S((H, 2, NY - 1)), S((H, 2)),
        S((H, NY - 1)), S((H, NY - 1)), S((H,)),
        S((H, NY - 1)), S((H, NY - 1)), S((H,)),
        S((H, 2, NY)), S((H, 2, NY)), S((H, 2)), S((H, 2)),
        S((NY - 1,)), S((NY - 1,)), S((NZ - 1,)), S((NZ - 1,)),
        S((nb - 1,)), S((nb - 1,)), S((NY - 1,)), S((NY - 1,)),
        S((nb - 1,)), S((nb - 1,)), S((NY - 1,)), S((NY - 1,)),
        S((H, NY - 1)), S((H, NY - 1)), S((H,)),
        S((H, 2)), S((H, 2)), S((H, 2)), S((H, 2)),
        S((H, NY - 1)), S((H, NY - 1)), S((H,)),
        S((H, 2, NY - 1)), S((H, 2, NY - 1)), S((H, 2)),
    ]
    any_spec = pl.BlockSpec(memory_space=pl.ANY)
    smem = pl.BlockSpec(memory_space=pltpu.SMEM)
    loss, *grads = pl.pallas_call(
        functools.partial(kernel, nb, T),
        out_shape=(
            jax.ShapeDtypeStruct((1, 1), F32),
            jax.ShapeDtypeStruct((T, D), BF16),
            jax.ShapeDtypeStruct((T, D), BF16),
            jax.ShapeDtypeStruct(key_proj.shape, BF16),
            jax.ShapeDtypeStruct(key_proj.shape, BF16),
        ),
        in_specs=[smem, smem, any_spec, any_spec, any_spec, any_spec, pl.BlockSpec(memory_space=pltpu.VMEM)],
        out_specs=(smem, any_spec, any_spec, any_spec, any_spec),
        scratch_shapes=scratch,
        compiler_params=pltpu.CompilerParams(
            collective_id=0, has_side_effects=True, vmem_limit_bytes=56 * 1024 * 1024
        ),
        cost_estimate=pl.CostEstimate(flops=13 * 10**9, bytes_accessed=6 * 2**20, transcendentals=2**23),
        name="attention_backward",
    )(lengths, positives, residual, query_proj, key_proj, value_proj, norm_gain.reshape(NY, NG, HD))
    return loss.reshape(()), *own_buffers(grads)


def solution(mesh):
    rows = P(("batch", "seq"), None)
    return jax.shard_map(
        functools.partial(on_device, mesh.shape["batch"]),
        mesh=mesh,
        in_specs=(rows, rows, rows, rows, P(), P("batch"), P()),
        out_specs=(P(), rows, rows, rows, rows),
        check_vma=False,
    )
```

```python
import functools
import math

import jax
import jax.numpy as jnp
from jax import lax
from jax.experimental import pallas as pl
from jax.experimental.pallas import tpu as pltpu
from jax.sharding import PartitionSpec as P

MESH = pl.DeviceIdType.MESH
HD = 128
NY = 4
NZ = 4
H = 2
G = 4
GW = G * HD
EPS = 1e-6
F32 = jnp.float32
BF16 = jnp.bfloat16
FACTOR = 1.0 / math.sqrt(HD)
LOG2E_FACTOR = FACTOR * math.log2(math.e)


def dot(a, b, dims=((1,), (0,))):
    return lax.dot_general(a, b, (dims, ((), ())), preferred_element_type=F32)


def kernel(
    nb, t_rows,
    len_ref, pos_ref, res_hbm, q_hbm, k_hbm, v_hbm, gain_ref,
    loss_ref, out_gr, out_gq, out_gk, out_gv,
    k_buf, v_buf, q_buf, res_buf, kvb, kfx, kzt, vta, qin, qs, qt, est, mb, mrun, linv, acc, rin, smt,
    rsq, rsa, invr, pz, pza, emba, sga, lra, gbt, mrw, msa, mrc, dot_t, gro, dqa, gqo, dka, dva, dkvo, own, rs1, rs2, fin,
    lds, kvs, kvr, kvl, qss, qsr, qsl, rns, rnr, rnl, z1s, z1r, z2s, z2r,
    sqs, sqr, pzs, pzr, ems, emr, sis, sir, los, lor, mns, mnr,
    grs, grr, grl, r1s, r1r, r2s, r2r, gqs, gqr, gql, gks, gkr, gkl,
):
    T = t_rows
    BK = NY * T
    NG = H * G
    b = lax.axis_index("batch")
    s = lax.axis_index("seq")
    y = lax.div(s, NZ)
    zh = lax.rem(s, NZ)
    right = (b, y * NZ + lax.rem(zh + 1, NZ))
    left = (b, y * NZ + lax.rem(zh + NZ - 1, NZ))

    def yo(k):
        return lax.rem(y + k, NY)

    def zo(k):
        return lax.rem(zh + k, NZ)

    def bo(k):
        return lax.rem(b + k, nb)

    def ydev(yy):
        return (b, yy * NZ + zh)

    def zdev(zz):
        return (b, y * NZ + zz)

    def col(index, width):
        return pl.ds(pl.multiple_of(index * width, width), width)

    def rcopy(src, dst, ssem, rsem, dev):
        return pltpu.make_async_remote_copy(
            src_ref=src, dst_ref=dst, send_sem=ssem, recv_sem=rsem, device_id=dev, device_id_type=MESH
        )

    def lcopy(src, dst, sem):
        return pltpu.make_async_copy(src, dst, sem)

    def await_ref(ref, sem):
        pltpu.make_async_copy(ref, ref, sem).wait()

    sends = []

    def send(src, dst, ssem, rsem, dev):
        copy = rcopy(src, dst, ssem, rsem, dev)
        copy.start()
        sends.append(copy)

    length = len_ref[0]
    lenf = length.astype(F32)

    loads = [
        lcopy(src, dst, lds.at[i])
        for i, (src, dst) in enumerate(((k_hbm, k_buf), (v_hbm, v_buf), (q_hbm, q_buf), (res_hbm, res_buf)))
    ]
    for load in loads:
        load.start()

    barrier = pltpu.get_barrier_semaphore()
    for k in range(1, NY):
        pl.semaphore_signal(barrier, inc=1, device_id=ydev(yo(k)), device_id_type=MESH)
    for k in range(1, NZ):
        pl.semaphore_signal(barrier, inc=1, device_id=zdev(zo(k)), device_id_type=MESH)
    for k in range(1, nb):
        pl.semaphore_signal(barrier, inc=1, device_id=(bo(k), s), device_id_type=MESH)
    pl.semaphore_wait(barrier, NY - 1 + NZ - 1 + nb - 1)

    for load in loads:
        load.wait()
    def kv_sends(h):
        for c, src in ((0, k_buf), (1, v_buf)):
            lcopy(src.at[:, col(2 * y + h, HD)], kvb.at[h, 0, c, y], kvl.at[h, c]).start()
            for k in (1, 3, 2):
                yy = yo(k)
                send(src.at[:, col(2 * yy + h, HD)], kvb.at[h, 0, c, y], kvs.at[h, c, k - 1], kvr.at[h, c, k - 1], ydev(yy))

    def q_send(h, k):
        yy = yo(k)
        send(q_buf.at[:, col(2 * yy + h, GW)], qin.at[h, y], qss.at[h, k - 1], qsr.at[h, k - 1], ydev(yy))

    def res_copy(h, k):
        yy = yo(k)
        return rcopy(res_buf.at[:, col(2 * yy + h, GW)], rin.at[h, y], rns.at[h, k - 1], rnr.at[h, k - 1], ydev(yy))

    def hop1(h, k):
        p = yo(NY - k)
        for c, src in ((0, k_buf), (1, v_buf)):
            if k == 0:
                lcopy(src.at[:, col(2 * y + h, HD)], kvb.at[h, 0, c, y], kvl.at[h, c]).wait()
            else:
                await_ref(kvb.at[h, 0, c, p], kvr.at[h, c, k - 1])
        send(kvb.at[h, 0, :, p], kvb.at[h, 1, :, p], z1s.at[h, 0, k], z1r.at[h, 0, k], right)
        send(kvb.at[h, 0, :, p], kvb.at[h, 2, :, p], z1s.at[h, 1, k], z1r.at[h, 1, k], left)

    kv_sends(0)
    kv_sends(1)
    for h in range(H):
        lcopy(q_buf.at[:, col(2 * y + h, GW)], qin.at[h, y], qsl.at[h]).start()
        lcopy(res_buf.at[:, col(2 * y + h, GW)], rin.at[h, y], rnl.at[h]).start()
        hop1(h, 0)
        for k in (1, 3, 2):
            q_send(h, k)
            hop1(h, k)

    def hop2(h, way):
        src, dev, piece = (1, right, 0) if way == 0 else (2, left, 2)
        return rcopy(
            kvb.at[h, src, :, pl.ds(piece, 2)], kvb.at[h, 3, :, pl.ds(piece, 2)], z2s.at[h, way], z2r.at[h, way], dev
        )

    def forward_hops(h):
        for way in range(2):
            for k in range(NY):
                await_ref(kvb.at[h, 1 + way, :, yo(NY - k)], z1r.at[h, way, k])
            hop2(h, way).start()

    def await_columns(h, src, dst, lsem, rsem):
        lcopy(src.at[:, col(2 * y + h, GW)], dst.at[h, y], lsem.at[h]).wait()
        for k in range(1, NY):
            await_ref(dst.at[h, yo(NY - k)], rsem.at[h, k - 1])

    def prep_q(h):
        def body(yy, carry):
            for j in range(G):
                head = qin[h, yy, :, j * HD : (j + 1) * HD]
                qs[h, yy, j * T : (j + 1) * T, :] = head
                qt[h, yy, :, j * T : (j + 1) * T] = head.T
            mrun[h, yy] = jnp.full((1, G * T), -3e38, F32)
            acc[h, yy] = jnp.zeros((HD + 16, G * T), F32)
            return carry

        lax.fori_loop(0, NY, body, 0)

    def prep_res(h):
        def body(yy, carry):
            for j in range(G):
                smt[h, yy, :, j * T : (j + 1) * T] = rin[h, yy, :, j * HD : (j + 1) * HD].T.astype(F32)
            return carry

        lax.fori_loop(0, NY, body, 0)

    def prep_kv(h, rel, zb):
        first_key = kvb[h, rel, 0, 0, 0:1, :].astype(F32)
        for yy in range(NY):
            base = (yy * NZ + zb) * T
            rows = slice(yy * T, (yy + 1) * T)
            kp = kvb[h, rel, 0, yy]
            valid = lax.broadcasted_iota(jnp.int32, (T, HD), 0) + base < length
            kfx[h, rel, rows, :] = jnp.where(valid, kp.astype(F32), first_key).astype(BF16)
            lanes = lax.broadcasted_iota(jnp.int32, (16, T), 1) + base < length
            ones = jnp.where(lanes, 1.0, 0.0).astype(BF16)
            vta[h, rel, HD : HD + 16, rows] = ones
            kzt[h, rel, :, rows] = kp.T * ones[0:1, :]
            vta[h, rel, 0:HD, rows] = kvb[h, rel, 1, yy].T * ones[0:1, :]

    halves = [slice(part * (G * T // 2), (part + 1) * (G * T // 2)) for part in range(2)]

    def attend(h, rel, yy):
        for lanes in halves:
            sc = dot(kfx[h, rel], qt[h, yy, :, lanes])
            m = jnp.max(sc, axis=0, keepdims=True)
            e = jnp.exp2((sc - m) * LOG2E_FACTOR).astype(BF16)
            est[h, rel, yy, :, lanes] = e
            mb[h, rel, yy, :, lanes] = m
            o = dot(vta[h, rel], e)
            mo = mrun[h, yy, :, lanes]
            mn = jnp.maximum(mo, m)
            keep = jnp.exp2((mo - mn) * LOG2E_FACTOR)
            add = jnp.exp2((m - mn) * LOG2E_FACTOR)
            acc[h, yy, :, lanes] = acc[h, yy, :, lanes] * keep + o * add
            mrun[h, yy, :, lanes] = mn

    def over_chunks(body):
        def step(yy, carry):
            body(yy)
            return carry

        lax.fori_loop(0, NY, step, 0, unroll=2)

    def own_step(h, carry):
        @pl.when(h == 1)
        def _():
            forward_hops(0)
            for k in (1, 3, 2):
                res_copy(0, k).start()

        await_columns(h, q_buf, qin, qsl, qsr)
        prep_q(h)
        prep_kv(h, 0, zh)
        over_chunks(lambda yy: attend(h, 0, yy))
        return carry

    def near_step(m, carry):
        h = lax.div(m, 2)
        rel = 1 + lax.rem(m, 2)

        @pl.when(m == 2)
        def _():
            forward_hops(1)
            for k in (1, 3, 2):
                res_copy(1, k).start()

        prep_kv(h, rel, zo(5 - 2 * rel))
        over_chunks(lambda yy: attend(h, rel, yy))
        return carry

    def far_step(h, carry):
        await_columns(h, res_buf, rin, rnl, rnr)
        prep_res(h)
        for way in range(2):
            await_ref(kvb.at[h, 3, :, pl.ds(2 * way, 2)], z2r.at[h, way])
        prep_kv(h, 3, zo(2))

        def chunk(yy):
            attend(h, 3, yy)
            li = 1.0 / acc[h, yy, HD : HD + 1, :]
            linv[h, yy] = li
            o = acc[h, yy, 0:HD, :] * li
            acc[h, yy, 0:HD, :] = o
            x = smt[h, yy] + o.astype(BF16).astype(F32)
            smt[h, yy] = x
            sq = jnp.sum(x * x, axis=0, keepdims=True)
            rsq[yy] = rsq[yy] + sum(sq[:, j * T : (j + 1) * T] for j in range(G))

        over_chunks(chunk)
        return carry

    rsq[...] = jnp.zeros((NY, 1, T), F32)
    lax.fori_loop(0, H, own_step, 0)
    lax.fori_loop(0, 2 * H, near_step, 0)
    lax.fori_loop(0, H, far_step, 0)

    def sum_along_y(src, gathered, ssem, rsem):
        for k in (2, 1, 3):
            send(src, gathered.at[y], ssem.at[k - 1], rsem.at[k - 1], ydev(yo(k)))
        gathered[y] = src[...]
        for k in (1, 3, 2):
            await_ref(gathered.at[yo(NY - k)], rsem.at[k - 1])
        return (gathered[0] + gathered[1]) + (gathered[2] + gathered[3])

    mean_square = sum_along_y(rsq, rsa, sqs, sqr) * (1.0 / (NY * NG * HD))
    inv = lax.rsqrt(mean_square + EPS)
    lane = lax.broadcasted_iota(jnp.int32, (NY, 1, T), 2)
    chunk_id = lax.broadcasted_iota(jnp.int32, (NY, 1, T), 0)
    live = (chunk_id * NZ + zh) * T + lane < length
    inv = jnp.where(live, inv, 0.0)
    invr[...] = inv

    for h in range(H):
        for j in range(G):
            part = smt[h, 0, :, j * T : (j + 1) * T] * inv[0]
            for yy in range(1, NY):
                part = part + smt[h, yy, :, j * T : (j + 1) * T] * inv[yy]
            pz[h * G + j : h * G + j + 1, :] = jnp.sum(part.T, axis=0, keepdims=True)
    gain = gain_ref[y]
    pz[...] = pz[...] * gain / lenf
    for k in (2, 1, 3):
        send(pz, pza.at[zh], pzs.at[k - 1], pzr.at[k - 1], zdev(zo(k)))
    pza[zh] = pz[...]
    for k in (1, 3, 2):
        await_ref(pza.at[zo(NZ - k)], pzr.at[k - 1])
    mine = (pza[0] + pza[1]) + (pza[2] + pza[3])
    emba[b] = mine
    for k in range(1, nb):
        send(emba.at[b], emba.at[b], ems.at[k - 1], emr.at[k - 1], (bo(k), s))
    for k in range(1, nb):
        await_ref(emba.at[bo(nb - k)], emr.at[k - 1])

    doc_ids = lax.broadcasted_iota(jnp.int32, (nb, HD), 0)
    lane_ids = lax.broadcasted_iota(jnp.int32, (nb, HD), 1)
    dots = jnp.zeros((nb, HD), F32)
    squares = jnp.zeros((nb, HD), F32)
    for j in range(nb):
        row = emba[j]
        dots = jnp.where(doc_ids == j, jnp.sum(row * mine, axis=0, keepdims=True), dots)
        squares = jnp.where(doc_ids == j, jnp.sum(row * row, axis=0, keepdims=True), squares)
    dots = jnp.broadcast_to(jnp.sum(dots, axis=1, keepdims=True), (nb, HD))
    squares = jnp.broadcast_to(jnp.sum(squares, axis=1, keepdims=True), (nb, HD))
    sga[NY] = jnp.where(lane_ids < HD // 2, dots, squares)
    both = sum_along_y(sga.at[NY], sga, sis, sir)
    dots = jnp.broadcast_to(both[:, 0:1], (nb, HD))
    rho = lax.rsqrt(jnp.broadcast_to(both[:, HD // 2 : HD // 2 + 1], (nb, HD)) + EPS)
    row_rho = jnp.broadcast_to(jnp.sum(jnp.where(doc_ids == b, rho, 0.0), axis=0, keepdims=True), (nb, HD))
    sims = dots * rho * row_rho
    logits = 10.0 * sims - 2.0
    posv = jnp.zeros((nb, HD), jnp.int32)
    for j in range(nb):
        posv = jnp.where(doc_ids == j, pos_ref[j], posv)
    sign = jnp.where(doc_ids == pos_ref[b], 1.0, -1.0)

    def pull(label):
        return -10.0 / nb * label / (1.0 + jnp.exp(label * logits))

    pair = pull(sign) + pull(jnp.where(posv == b, 1.0, -1.0))
    pair = jnp.where(doc_ids == b, 0.0, pair) * (16.0 * NY * NZ * T)
    coef = pair * rho * row_rho
    self_coef = row_rho * row_rho * jnp.broadcast_to(jnp.sum(pair * sims, axis=0, keepdims=True), (nb, HD))
    grad = -self_coef[0:1, :] * mine
    for j in range(nb):
        grad = grad + coef[j : j + 1, :] * emba[j]
    gained = grad / lenf * gain

    for i in range(NG):
        gbt[i] = jnp.broadcast_to(gained[i : i + 1, :], (T, HD)).T
    for yy in range(NY):
        part = gbt[0] * smt[0, yy, :, 0:T]
        for i in range(1, NG):
            j = i % G
            part = part + gbt[i] * smt[i // G, yy, :, j * T : (j + 1) * T]
        mrw[yy] = jnp.sum(part, axis=0, keepdims=True)
    mean = sum_along_y(mrw, msa, mns, mnr) * invr[...] * (1.0 / (NY * NG * HD))
    mrw_scale = invr[...] * invr[...] * mean

    def r1(h, way):
        dev, piece = (right, 0) if way == 0 else (left, 2)
        return rcopy(dkvo.at[h, 2, :, pl.ds(piece, 2)], rs1.at[h, way], r1s.at[h, way], r1r.at[h, way], dev)

    def r2(h, way):
        dev = right if way == 0 else left
        return rcopy(dkvo.at[h, 1 - way], rs2.at[h, way], r2s.at[h, way], r2r.at[h, way], dev)

    def gq_send(h, kk):
        yy = yo(kk)
        return rcopy(gqo.at[h, yy], out_gq.at[:, col(2 * y + h, GW)], gqs.at[h, kk - 1], gqr.at[h, kk - 1], ydev(yy))

    def gq_local(h):
        return lcopy(gqo.at[h, y], out_gq.at[:, col(2 * y + h, GW)], gql.at[h])

    def gr_send(h, kk):
        yy = yo(kk)
        return rcopy(gro.at[h, yy], out_gr.at[:, col(2 * y + h, GW)], grs.at[h, kk - 1], grr.at[h, kk - 1], ydev(yy))

    def gr_local(h):
        return lcopy(gro.at[h, y], out_gr.at[:, col(2 * y + h, GW)], grl.at[h])

    def pull_back(h, rel, yy):
        vals = kvb[h, rel, 1].reshape(BK, HD)
        dos, scores = [], []
        for lanes in halves:
            r = jnp.exp2((mb[h, rel, yy, :, lanes] - mrun[h, yy, :, lanes]) * LOG2E_FACTOR) * linv[h, yy, :, lanes]
            do = (dot_t[h, yy, :, lanes].astype(F32) * r).astype(BF16)
            delta = jnp.sum(do.astype(F32) * acc[h, yy, 0:HD, lanes], axis=0, keepdims=True)
            dp = dot(vals, do)
            ds = est[h, rel, yy, :, lanes] * (dp - delta).astype(BF16)
            dqa[h, yy, :, lanes] += dot(kzt[h, rel], ds)
            dos.append(do)
            scores.append(ds)
        dva[...] += dot(est[h, rel, yy], jnp.concatenate(dos, axis=1), ((1,), (1,)))
        dka[...] += dot(jnp.concatenate(scores, axis=1), qs[h, yy])

    def clear():
        dka[...] = jnp.zeros((BK, HD), F32)
        dva[...] = jnp.zeros((BK, HD), F32)

    def store(h, slot, added):
        for c, ref in ((0, dka), (1, dva)):
            for p in range(NY):
                x = ref[p * T : (p + 1) * T, :]
                if c == 0:
                    x = x * FACTOR
                if added is not None and p // 2 == added:
                    x = x + rs1[h, added, c, p % 2].astype(F32)
                dkvo[h, slot, c, p] = x.astype(BF16)

    def far_back(h, carry):
        for yy in range(NY):
            a = jnp.concatenate([invr[yy]] * G, axis=1)
            c = jnp.concatenate([mrc[yy]] * G, axis=1)
            g = jnp.concatenate([gbt[h * G + j] for j in range(G)], axis=1)
            dot_t[h, yy] = (g * a - smt[h, yy] * c).astype(BF16)
            dqa[h, yy] = jnp.zeros((HD, G * T), F32)
        clear()
        over_chunks(lambda yy: pull_back(h, 3, yy))
        store(h, 2, None)
        r1(h, 0).start()
        r1(h, 1).start()

        def give(t, carry):
            kk = lax.rem(t + 1, NY)
            yy = yo(kk)
            for j in range(G):
                gro[h, yy, :, j * HD : (j + 1) * HD] = dot_t[h, yy, :, j * T : (j + 1) * T].T

            @pl.when(kk > 0)
            def _():
                gr_send(h, kk).start()

            @pl.when(kk == 0)
            def _():
                gr_local(h).start()

            return carry

        lax.fori_loop(0, NY, give, 0)
        return carry

    def near_back(m, carry):
        h = lax.div(m, 2)
        way = lax.rem(m, 2)
        rel = 2 - way
        clear()
        over_chunks(lambda yy: pull_back(h, rel, yy))
        for w in range(2):

            @pl.when(way == w)
            def _(w=w):
                await_ref(rs1.at[h, w], r1r.at[h, w])
                store(h, 1 - w, w)
                r2(h, w).start()

        return carry

    def own_back(h, carry):
        clear()

        def chunk(t, carry):
            for u in range(2):
                pull_back(h, 0, yo(lax.rem(2 * t + u + 1, NY)))
            for u in range(2):
                kk = lax.rem(2 * t + u + 1, NY)
                yy = yo(kk)
                for j in range(G):
                    part = dqa[h, yy, :, j * T : (j + 1) * T] * FACTOR
                    gqo[h, yy, :, j * HD : (j + 1) * HD] = part.astype(BF16).T

                @pl.when(kk > 0)
                def _(kk=kk):
                    gq_send(h, kk).start()

                @pl.when(kk == 0)
                def _():
                    gq_local(h).start()

            return carry

        lax.fori_loop(0, NY // 2, chunk, 0)
        own[h, 0] = dka[...] * FACTOR
        own[h, 1] = dva[...]
        return carry

    mrc[...] = mrw_scale
    lax.fori_loop(0, H, far_back, 0)

    x = -sign * logits
    term = jnp.maximum(x, 0.0) + jnp.log(1.0 + jnp.exp(-jnp.abs(x)))
    term = jnp.sum(jnp.where(doc_ids == b, 0.0, term), axis=0, keepdims=True)
    lra[b] = jnp.broadcast_to(term, (8, HD))
    for k in range(1, nb):
        send(lra.at[b], lra.at[b], los.at[k - 1], lor.at[k - 1], (bo(k), s))

    lax.fori_loop(0, 2 * H, near_back, 0)
    lax.fori_loop(0, H, own_back, 0)

    for k in range(1, nb):
        await_ref(lra.at[bo(nb - k)], lor.at[k - 1])
    loss = lra[0]
    for j in range(1, nb):
        loss = loss + lra[j]
    loss_ref[0, 0] = jnp.sum(loss) * (1.0 / (8 * HD * nb))

    for h in range(H):
        await_ref(rs2.at[h, 0], r2r.at[h, 0])
        await_ref(rs2.at[h, 1], r2r.at[h, 1])
        for p in range(NY):
            valid = lax.broadcasted_iota(jnp.int32, (T, HD), 0) + (p * NZ + zh) * T < length
            for c in range(2):
                x = own[h, c, p * T : (p + 1) * T, :] + rs2[h, 0, c, p].astype(F32) + rs2[h, 1, c, p].astype(F32)
                fin[h, c, p] = jnp.where(valid, x, 0.0).astype(BF16)
        for c, out in ((0, out_gk), (1, out_gv)):
            for k in (2, 1, 3):
                yy = yo(k)
                send(fin.at[h, c, yy], out.at[:, col(2 * y + h, HD)], gks.at[h, c, k - 1], gkr.at[h, c, k - 1], ydev(yy))
            lcopy(fin.at[h, c, y], out.at[:, col(2 * y + h, HD)], gkl.at[h, c]).start()

    for h in range(H):
        gq_local(h).wait()
        gr_local(h).wait()
        for k in range(1, NY):
            await_ref(out_gr.at[:, col(2 * yo(NY - k) + h, GW)], grr.at[h, k - 1])
            await_ref(out_gq.at[:, col(2 * yo(NY - k) + h, GW)], gqr.at[h, k - 1])
        for c, out in ((0, out_gk), (1, out_gv)):
            lcopy(fin.at[h, c, y], out.at[:, col(2 * y + h, HD)], gkl.at[h, c]).wait()
            for k in range(1, NY):
                await_ref(out.at[:, col(2 * yo(NY - k) + h, HD)], gkr.at[h, c, k - 1])
    for copy in sends:
        copy.wait_send()
    for h in range(H):
        for way in range(2):
            hop2(h, way).wait_send()
            r1(h, way).wait_send()
            r2(h, way).wait_send()
        for k in range(1, NY):
            res_copy(h, k).wait_send()
            gr_send(h, k).wait_send()
            gq_send(h, k).wait_send()


def copy_kernel(parts, n, *refs):
    srcs, dsts, bufs, sems = refs[:n], refs[n : 2 * n], refs[2 * n : 3 * n], refs[-1]
    pairs = []
    for i in range(n):
        rows = srcs[i].shape[0] // parts
        for p in range(parts):
            span = pl.ds(p * rows, rows)
            pairs.append(
                (
                    pltpu.make_async_copy(srcs[i].at[span], bufs[i].at[span], sems.at[0, i, p]),
                    pltpu.make_async_copy(bufs[i].at[span], dsts[i].at[span], sems.at[1, i, p]),
                )
            )
    for load, _ in pairs:
        load.start()
    for load, give in pairs:
        load.wait()
        give.start()
    for _, give in pairs:
        give.wait()


def own_buffers(arrays):
    parts = 2
    any_spec = pl.BlockSpec(memory_space=pl.ANY)
    return pl.pallas_call(
        functools.partial(copy_kernel, parts, len(arrays)),
        out_shape=tuple(jax.ShapeDtypeStruct(x.shape, x.dtype) for x in arrays),
        in_specs=[any_spec] * len(arrays),
        out_specs=(any_spec,) * len(arrays),
        scratch_shapes=[pltpu.VMEM(x.shape, x.dtype) for x in arrays]
        + [pltpu.SemaphoreType.DMA((2, len(arrays), parts))],
        compiler_params=pltpu.CompilerParams(vmem_limit_bytes=56 * 1024 * 1024),
        cost_estimate=pl.CostEstimate(flops=0, bytes_accessed=5 * 2**20, transcendentals=0),
        name="copy_out",
    )(*arrays)


def on_device(nb, residual, query_proj, key_proj, value_proj, norm_gain, lengths, positives):
    T, D = residual.shape
    BK, QC, NG = NY * T, G * T, H * G
    V = pltpu.VMEM
    S = pltpu.SemaphoreType.DMA
    columns = V((H, NY, T, GW), BF16)
    scratch = [
        V(key_proj.shape, BF16), V(key_proj.shape, BF16), V((T, D), BF16), V((T, D), BF16),
        V((H, NZ, 2, NY, T, HD), BF16),
        V((H, NZ, BK, HD), BF16),
        V((H, NZ, HD, BK), BF16),
        V((H, NZ, HD + 16, BK), BF16),
        columns,
        V((H, NY, QC, HD), BF16),
        V((H, NY, HD, QC), BF16),
        V((H, NZ, NY, BK, QC), BF16),
        V((H, NZ, NY, 1, QC), F32),
        V((H, NY, 1, QC), F32),
        V((H, NY, 1, QC), F32),
        V((H, NY, HD + 16, QC), F32),
        columns,
        V((H, NY, HD, QC), F32),
        V((NY, 1, T), F32), V((NY, NY, 1, T), F32), V((NY, 1, T), F32),
        V((NG, HD), F32), V((NZ, NG, HD), F32),
        V((nb, NG, HD), F32),
        V((NY + 1, nb, HD), F32),
        V((nb, 8, HD), F32),
        V((NG, HD, T), F32),
        V((NY, 1, T), F32), V((NY, NY, 1, T), F32), V((NY, 1, T), F32),
        V((H, NY, HD, QC), BF16),
        columns,
        V((H, NY, HD, QC), F32),
        columns,
        V((BK, HD), F32),
        V((BK, HD), F32),
        V((H, 3, 2, NY, T, HD), BF16),
        V((H, 2, BK, HD), F32),
        V((H, 2, 2, 2, T, HD), BF16),
        V((H, 2, 2, NY, T, HD), BF16),
        V((H, 2, NY, T, HD), BF16),
        S((4,)), S((H, 2, NY - 1)), S((H, 2, NY - 1)), S((H, 2)),
        S((H, NY - 1)), S((H, NY - 1)), S((H,)),
        S((H, NY - 1)), S((H, NY - 1)), S((H,)),
        S((H, 2, NY)), S((H, 2, NY)), S((H, 2)), S((H, 2)),
        S((NY - 1,)), S((NY - 1,)), S((NZ - 1,)), S((NZ - 1,)),
        S((nb - 1,)), S((nb - 1,)), S((NY - 1,)), S((NY - 1,)),
        S((nb - 1,)), S((nb - 1,)), S((NY - 1,)), S((NY - 1,)),
        S((H, NY - 1)), S((H, NY - 1)), S((H,)),
        S((H, 2)), S((H, 2)), S((H, 2)), S((H, 2)),
        S((H, NY - 1)), S((H, NY - 1)), S((H,)),
        S((H, 2, NY - 1)), S((H, 2, NY - 1)), S((H, 2)),
    ]
    any_spec = pl.BlockSpec(memory_space=pl.ANY)
    smem = pl.BlockSpec(memory_space=pltpu.SMEM)
    loss, *grads = pl.pallas_call(
        functools.partial(kernel, nb, T),
        out_shape=(
            jax.ShapeDtypeStruct((1, 1), F32),
            jax.ShapeDtypeStruct((T, D), BF16),
            jax.ShapeDtypeStruct((T, D), BF16),
            jax.ShapeDtypeStruct(key_proj.shape, BF16),
            jax.ShapeDtypeStruct(key_proj.shape, BF16),
        ),
        in_specs=[smem, smem, any_spec, any_spec, any_spec, any_spec, pl.BlockSpec(memory_space=pltpu.VMEM)],
        out_specs=(smem, any_spec, any_spec, any_spec, any_spec),
        scratch_shapes=scratch,
        compiler_params=pltpu.CompilerParams(
            collective_id=0, has_side_effects=True, vmem_limit_bytes=56 * 1024 * 1024
        ),
        cost_estimate=pl.CostEstimate(flops=13 * 10**9, bytes_accessed=6 * 2**20, transcendentals=2**23),
        name="attention_backward",
    )(lengths, positives, residual, query_proj, key_proj, value_proj, norm_gain.reshape(NY, NG, HD))
    return loss.reshape(()), *own_buffers(grads)


def solution(mesh):
    rows = P(("batch", "seq"), None)
    return jax.shard_map(
        functools.partial(on_device, mesh.shape["batch"]),
        mesh=mesh,
        in_specs=(rows, rows, rows, rows, P(), P("batch"), P()),
        out_specs=(P(), rows, rows, rows, rows),
        check_vma=False,
    )
```

```python
import functools
import math

import jax
import jax.numpy as jnp
from jax import lax
from jax.experimental import pallas as pl
from jax.experimental.pallas import tpu as pltpu
from jax.sharding import PartitionSpec as P

MESH = pl.DeviceIdType.MESH
HD = 128
NY = 4
NZ = 4
H = 2
G = 4
GW = G * HD
EPS = 1e-6
F32 = jnp.float32
BF16 = jnp.bfloat16
FACTOR = 1.0 / math.sqrt(HD)
LOG2E_FACTOR = FACTOR * math.log2(math.e)


def dot(a, b, dims=((1,), (0,))):
    return lax.dot_general(a, b, (dims, ((), ())), preferred_element_type=F32)


def kernel(
    nb, t_rows,
    len_ref, pos_ref, res_hbm, q_hbm, k_hbm, v_hbm, gain_ref,
    loss_ref, out_gr, out_gq, out_gk, out_gv,
    k_buf, v_buf, q_buf, res_buf, kvb, kfx, kzt, vta, qin, qs, qt, est, mb, mrun, linv, acc, rin, smt,
    rsq, rsa, invr, pz, pza, emba, sga, lra, gbt, mrw, msa, mrc, dot_t, gro, dqa, gqo, dka, dva, dkvo, own, rs1, rs2, fin,
    lds, kvs, kvr, kvl, qss, qsr, qsl, rns, rnr, rnl, z1s, z1r, z2s, z2r,
    sqs, sqr, pzs, pzr, ems, emr, sis, sir, los, lor, mns, mnr,
    grs, grr, grl, r1s, r1r, r2s, r2r, gqs, gqr, gql, gks, gkr, gkl,
):
    T = t_rows
    BK = NY * T
    NG = H * G
    b = lax.axis_index("batch")
    s = lax.axis_index("seq")
    y = lax.div(s, NZ)
    zh = lax.rem(s, NZ)
    right = (b, y * NZ + lax.rem(zh + 1, NZ))
    left = (b, y * NZ + lax.rem(zh + NZ - 1, NZ))

    def yo(k):
        return lax.rem(y + k, NY)

    def zo(k):
        return lax.rem(zh + k, NZ)

    def bo(k):
        return lax.rem(b + k, nb)

    def ydev(yy):
        return (b, yy * NZ + zh)

    def zdev(zz):
        return (b, y * NZ + zz)

    def col(index, width):
        return pl.ds(pl.multiple_of(index * width, width), width)

    def rcopy(src, dst, ssem, rsem, dev):
        return pltpu.make_async_remote_copy(
            src_ref=src, dst_ref=dst, send_sem=ssem, recv_sem=rsem, device_id=dev, device_id_type=MESH
        )

    def lcopy(src, dst, sem):
        return pltpu.make_async_copy(src, dst, sem)

    def await_ref(ref, sem):
        pltpu.make_async_copy(ref, ref, sem).wait()

    sends = []

    def send(src, dst, ssem, rsem, dev):
        copy = rcopy(src, dst, ssem, rsem, dev)
        copy.start()
        sends.append(copy)

    length = len_ref[0]
    lenf = length.astype(F32)

    loads = [
        lcopy(src, dst, lds.at[i])
        for i, (src, dst) in enumerate(((k_hbm, k_buf), (v_hbm, v_buf), (q_hbm, q_buf), (res_hbm, res_buf)))
    ]
    for load in loads:
        load.start()

    barrier = pltpu.get_barrier_semaphore()
    for k in range(1, NY):
        pl.semaphore_signal(barrier, inc=1, device_id=ydev(yo(k)), device_id_type=MESH)
    for k in range(1, NZ):
        pl.semaphore_signal(barrier, inc=1, device_id=zdev(zo(k)), device_id_type=MESH)
    for k in range(1, nb):
        pl.semaphore_signal(barrier, inc=1, device_id=(bo(k), s), device_id_type=MESH)
    pl.semaphore_wait(barrier, NY - 1 + NZ - 1 + nb - 1)

    for load in loads:
        load.wait()
    def kv_sends(h):
        for c, src in ((0, k_buf), (1, v_buf)):
            lcopy(src.at[:, col(2 * y + h, HD)], kvb.at[h, 0, c, y], kvl.at[h, c]).start()
            for k in (1, 3, 2):
                yy = yo(k)
                send(src.at[:, col(2 * yy + h, HD)], kvb.at[h, 0, c, y], kvs.at[h, c, k - 1], kvr.at[h, c, k - 1], ydev(yy))

    def q_send(h, k):
        yy = yo(k)
        send(q_buf.at[:, col(2 * yy + h, GW)], qin.at[h, y], qss.at[h, k - 1], qsr.at[h, k - 1], ydev(yy))

    def res_copy(h, k):
        yy = yo(k)
        return rcopy(res_buf.at[:, col(2 * yy + h, GW)], rin.at[h, y], rns.at[h, k - 1], rnr.at[h, k - 1], ydev(yy))

    def hop1(h, k):
        p = yo(NY - k)
        for c, src in ((0, k_buf), (1, v_buf)):
            if k == 0:
                lcopy(src.at[:, col(2 * y + h, HD)], kvb.at[h, 0, c, y], kvl.at[h, c]).wait()
            else:
                await_ref(kvb.at[h, 0, c, p], kvr.at[h, c, k - 1])
        send(kvb.at[h, 0, :, p], kvb.at[h, 1, :, p], z1s.at[h, 0, k], z1r.at[h, 0, k], right)
        send(kvb.at[h, 0, :, p], kvb.at[h, 2, :, p], z1s.at[h, 1, k], z1r.at[h, 1, k], left)

    kv_sends(0)
    kv_sends(1)
    for h in range(H):
        lcopy(q_buf.at[:, col(2 * y + h, GW)], qin.at[h, y], qsl.at[h]).start()
        lcopy(res_buf.at[:, col(2 * y + h, GW)], rin.at[h, y], rnl.at[h]).start()
        hop1(h, 0)
        for k in (1, 3, 2):
            q_send(h, k)
            hop1(h, k)

    def hop2(h, way):
        src, dev, piece = (1, right, 0) if way == 0 else (2, left, 2)
        return rcopy(
            kvb.at[h, src, :, pl.ds(piece, 2)], kvb.at[h, 3, :, pl.ds(piece, 2)], z2s.at[h, way], z2r.at[h, way], dev
        )

    def forward_hops(h):
        for way in range(2):
            for k in range(NY):
                await_ref(kvb.at[h, 1 + way, :, yo(NY - k)], z1r.at[h, way, k])
            hop2(h, way).start()

    def await_columns(h, src, dst, lsem, rsem):
        lcopy(src.at[:, col(2 * y + h, GW)], dst.at[h, y], lsem.at[h]).wait()
        for k in range(1, NY):
            await_ref(dst.at[h, yo(NY - k)], rsem.at[h, k - 1])

    def prep_q(h):
        def body(yy, carry):
            for j in range(G):
                head = qin[h, yy, :, j * HD : (j + 1) * HD]
                qs[h, yy, j * T : (j + 1) * T, :] = head
                qt[h, yy, :, j * T : (j + 1) * T] = head.T
            mrun[h, yy] = jnp.full((1, G * T), -3e38, F32)
            acc[h, yy] = jnp.zeros((HD + 16, G * T), F32)
            return carry

        lax.fori_loop(0, NY, body, 0)

    def prep_res(h):
        def body(yy, carry):
            for j in range(G):
                smt[h, yy, :, j * T : (j + 1) * T] = rin[h, yy, :, j * HD : (j + 1) * HD].T.astype(F32)
            return carry

        lax.fori_loop(0, NY, body, 0)

    def prep_kv(h, rel, zb):
        first_key = kvb[h, rel, 0, 0, 0:1, :].astype(F32)
        for yy in range(NY):
            base = (yy * NZ + zb) * T
            rows = slice(yy * T, (yy + 1) * T)
            kp = kvb[h, rel, 0, yy]
            valid = lax.broadcasted_iota(jnp.int32, (T, HD), 0) + base < length
            kfx[h, rel, rows, :] = jnp.where(valid, kp.astype(F32), first_key).astype(BF16)
            lanes = lax.broadcasted_iota(jnp.int32, (16, T), 1) + base < length
            ones = jnp.where(lanes, 1.0, 0.0).astype(BF16)
            vta[h, rel, HD : HD + 16, rows] = ones
            kzt[h, rel, :, rows] = kp.T * ones[0:1, :]
            vta[h, rel, 0:HD, rows] = kvb[h, rel, 1, yy].T * ones[0:1, :]

    halves = [slice(part * (G * T // 2), (part + 1) * (G * T // 2)) for part in range(2)]

    def attend(h, rel, yy):
        for lanes in halves:
            sc = dot(kfx[h, rel], qt[h, yy, :, lanes])
            m = jnp.max(sc, axis=0, keepdims=True)
            e = jnp.exp2((sc - m) * LOG2E_FACTOR).astype(BF16)
            est[h, rel, yy, :, lanes] = e
            mb[h, rel, yy, :, lanes] = m
            o = dot(vta[h, rel], e)
            mo = mrun[h, yy, :, lanes]
            mn = jnp.maximum(mo, m)
            keep = jnp.exp2((mo - mn) * LOG2E_FACTOR)
            add = jnp.exp2((m - mn) * LOG2E_FACTOR)
            acc[h, yy, :, lanes] = acc[h, yy, :, lanes] * keep + o * add
            mrun[h, yy, :, lanes] = mn

    def over_chunks(body):
        def step(yy, carry):
            body(yy)
            return carry

        lax.fori_loop(0, NY, step, 0, unroll=2)

    def own_step(h, carry):
        @pl.when(h == 1)
        def _():
            forward_hops(0)
            for k in (1, 3, 2):
                res_copy(0, k).start()

        await_columns(h, q_buf, qin, qsl, qsr)
        prep_q(h)
        prep_kv(h, 0, zh)
        over_chunks(lambda yy: attend(h, 0, yy))
        return carry

    def near_step(m, carry):
        h = lax.div(m, 2)
        rel = 1 + lax.rem(m, 2)

        @pl.when(m == 2)
        def _():
            forward_hops(1)
            for k in (1, 3, 2):
                res_copy(1, k).start()

        prep_kv(h, rel, zo(5 - 2 * rel))
        over_chunks(lambda yy: attend(h, rel, yy))
        return carry

    def far_step(h, carry):
        await_columns(h, res_buf, rin, rnl, rnr)
        prep_res(h)
        for way in range(2):
            await_ref(kvb.at[h, 3, :, pl.ds(2 * way, 2)], z2r.at[h, way])
        prep_kv(h, 3, zo(2))

        def chunk(yy):
            attend(h, 3, yy)
            li = 1.0 / acc[h, yy, HD : HD + 1, :]
            linv[h, yy] = li
            o = acc[h, yy, 0:HD, :] * li
            acc[h, yy, 0:HD, :] = o
            x = smt[h, yy] + o.astype(BF16).astype(F32)
            smt[h, yy] = x
            sq = jnp.sum(x * x, axis=0, keepdims=True)
            rsq[yy] = rsq[yy] + sum(sq[:, j * T : (j + 1) * T] for j in range(G))

        over_chunks(chunk)
        return carry

    rsq[...] = jnp.zeros((NY, 1, T), F32)
    lax.fori_loop(0, H, own_step, 0)
    lax.fori_loop(0, 2 * H, near_step, 0)
    lax.fori_loop(0, H, far_step, 0)

    def sum_along_y(src, gathered, ssem, rsem):
        for k in (2, 1, 3):
            send(src, gathered.at[y], ssem.at[k - 1], rsem.at[k - 1], ydev(yo(k)))
        gathered[y] = src[...]
        for k in (1, 3, 2):
            await_ref(gathered.at[yo(NY - k)], rsem.at[k - 1])
        return (gathered[0] + gathered[1]) + (gathered[2] + gathered[3])

    mean_square = sum_along_y(rsq, rsa, sqs, sqr) * (1.0 / (NY * NG * HD))
    inv = lax.rsqrt(mean_square + EPS)
    lane = lax.broadcasted_iota(jnp.int32, (NY, 1, T), 2)
    chunk_id = lax.broadcasted_iota(jnp.int32, (NY, 1, T), 0)
    live = (chunk_id * NZ + zh) * T + lane < length
    inv = jnp.where(live, inv, 0.0)
    invr[...] = inv

    for h in range(H):
        for j in range(G):
            part = smt[h, 0, :, j * T : (j + 1) * T] * inv[0]
            for yy in range(1, NY):
                part = part + smt[h, yy, :, j * T : (j + 1) * T] * inv[yy]
            pz[h * G + j : h * G + j + 1, :] = jnp.sum(part.T, axis=0, keepdims=True)
    gain = gain_ref[y]
    pz[...] = pz[...] * gain / lenf
    for k in (2, 1, 3):
        send(pz, pza.at[zh], pzs.at[k - 1], pzr.at[k - 1], zdev(zo(k)))
    pza[zh] = pz[...]
    for k in (1, 3, 2):
        await_ref(pza.at[zo(NZ - k)], pzr.at[k - 1])
    mine = (pza[0] + pza[1]) + (pza[2] + pza[3])
    emba[b] = mine
    for k in range(1, nb):
        send(emba.at[b], emba.at[b], ems.at[k - 1], emr.at[k - 1], (bo(k), s))
    for k in range(1, nb):
        await_ref(emba.at[bo(nb - k)], emr.at[k - 1])

    doc_ids = lax.broadcasted_iota(jnp.int32, (nb, HD), 0)
    lane_ids = lax.broadcasted_iota(jnp.int32, (nb, HD), 1)
    dots = jnp.zeros((nb, HD), F32)
    squares = jnp.zeros((nb, HD), F32)
    for j in range(nb):
        row = emba[j]
        dots = jnp.where(doc_ids == j, jnp.sum(row * mine, axis=0, keepdims=True), dots)
        squares = jnp.where(doc_ids == j, jnp.sum(row * row, axis=0, keepdims=True), squares)
    dots = jnp.broadcast_to(jnp.sum(dots, axis=1, keepdims=True), (nb, HD))
    squares = jnp.broadcast_to(jnp.sum(squares, axis=1, keepdims=True), (nb, HD))
    sga[NY] = jnp.where(lane_ids < HD // 2, dots, squares)
    both = sum_along_y(sga.at[NY], sga, sis, sir)
    dots = jnp.broadcast_to(both[:, 0:1], (nb, HD))
    rho = lax.rsqrt(jnp.broadcast_to(both[:, HD // 2 : HD // 2 + 1], (nb, HD)) + EPS)
    row_rho = jnp.broadcast_to(jnp.sum(jnp.where(doc_ids == b, rho, 0.0), axis=0, keepdims=True), (nb, HD))
    sims = dots * rho * row_rho
    logits = 10.0 * sims - 2.0
    posv = jnp.zeros((nb, HD), jnp.int32)
    for j in range(nb):
        posv = jnp.where(doc_ids == j, pos_ref[j], posv)
    sign = jnp.where(doc_ids == pos_ref[b], 1.0, -1.0)

    def pull(label):
        return -10.0 / nb * label / (1.0 + jnp.exp(label * logits))

    pair = pull(sign) + pull(jnp.where(posv == b, 1.0, -1.0))
    pair = jnp.where(doc_ids == b, 0.0, pair) * (16.0 * NY * NZ * T)
    coef = pair * rho * row_rho
    self_coef = row_rho * row_rho * jnp.broadcast_to(jnp.sum(pair * sims, axis=0, keepdims=True), (nb, HD))
    grad = -self_coef[0:1, :] * mine
    for j in range(nb):
        grad = grad + coef[j : j + 1, :] * emba[j]
    gained = grad / lenf * gain

    for i in range(NG):
        gbt[i] = jnp.broadcast_to(gained[i : i + 1, :], (T, HD)).T
    for yy in range(NY):
        part = gbt[0] * smt[0, yy, :, 0:T]
        for i in range(1, NG):
            j = i % G
            part = part + gbt[i] * smt[i // G, yy, :, j * T : (j + 1) * T]
        mrw[yy] = jnp.sum(part, axis=0, keepdims=True)
    mean = sum_along_y(mrw, msa, mns, mnr) * invr[...] * (1.0 / (NY * NG * HD))
    mrw_scale = invr[...] * invr[...] * mean

    def r1(h, way, c):
        dev, piece = (right, 0) if way == 0 else (left, 2)
        return rcopy(
            dkvo.at[h, 2, c, pl.ds(piece, 2)], rs1.at[h, way, c], r1s.at[h, way, c], r1r.at[h, way, c], dev
        )

    def r2(h, way, c):
        dev = right if way == 0 else left
        return rcopy(dkvo.at[h, 1 - way, c], rs2.at[h, way, c], r2s.at[h, way, c], r2r.at[h, way, c], dev)

    def gq_send(h, kk):
        yy = yo(kk)
        return rcopy(gqo.at[h, yy], out_gq.at[:, col(2 * y + h, GW)], gqs.at[h, kk - 1], gqr.at[h, kk - 1], ydev(yy))

    def gq_local(h):
        return lcopy(gqo.at[h, y], out_gq.at[:, col(2 * y + h, GW)], gql.at[h])

    def gr_send(h, kk):
        yy = yo(kk)
        return rcopy(gro.at[h, yy], out_gr.at[:, col(2 * y + h, GW)], grs.at[h, kk - 1], grr.at[h, kk - 1], ydev(yy))

    def gr_local(h):
        return lcopy(gro.at[h, y], out_gr.at[:, col(2 * y + h, GW)], grl.at[h])

    def scaled_grads(h, rel, yy, lanes):
        r = jnp.exp2((mb[h, rel, yy, :, lanes] - mrun[h, yy, :, lanes]) * LOG2E_FACTOR) * linv[h, yy, :, lanes]
        return (dot_t[h, yy, :, lanes].astype(F32) * r).astype(BF16)

    def values_back(h, rel, yy, dos=None):
        if dos is None:
            dos = [scaled_grads(h, rel, yy, lanes) for lanes in halves]
        dva[...] += dot(est[h, rel, yy], jnp.concatenate(dos, axis=1), ((1,), (1,)))

    def keys_back(h, rel, yy):
        vals = kvb[h, rel, 1].reshape(BK, HD)
        dos, scores = [], []
        for lanes in halves:
            do = scaled_grads(h, rel, yy, lanes)
            delta = jnp.sum(do.astype(F32) * acc[h, yy, 0:HD, lanes], axis=0, keepdims=True)
            dp = dot(vals, do)
            ds = est[h, rel, yy, :, lanes] * (dp - delta).astype(BF16)
            dqa[h, yy, :, lanes] += dot(kzt[h, rel], ds)
            dos.append(do)
            scores.append(ds)
        dka[...] += dot(jnp.concatenate(scores, axis=1), qs[h, yy])
        return dos

    def pull_back(h, rel, yy):
        values_back(h, rel, yy, keys_back(h, rel, yy))

    def clear():
        dka[...] = jnp.zeros((BK, HD), F32)
        dva[...] = jnp.zeros((BK, HD), F32)

    def store(h, slot, c, added):
        for p in range(NY):
            x = dva[p * T : (p + 1) * T, :] if c == 1 else dka[p * T : (p + 1) * T, :] * FACTOR
            if added is not None and p // 2 == added:
                x = x + rs1[h, added, c, p % 2].astype(F32)
            dkvo[h, slot, c, p] = x.astype(BF16)

    def far_back(h, carry):
        for yy in range(NY):
            a = jnp.concatenate([invr[yy]] * G, axis=1)
            c = jnp.concatenate([mrc[yy]] * G, axis=1)
            g = jnp.concatenate([gbt[h * G + j] for j in range(G)], axis=1)
            dot_t[h, yy] = (g * a - smt[h, yy] * c).astype(BF16)
            dqa[h, yy] = jnp.zeros((HD, G * T), F32)
        clear()
        over_chunks(lambda yy: values_back(h, 3, yy))
        store(h, 2, 1, None)
        r1(h, 0, 1).start()
        r1(h, 1, 1).start()
        over_chunks(lambda yy: keys_back(h, 3, yy))
        store(h, 2, 0, None)
        r1(h, 0, 0).start()
        r1(h, 1, 0).start()

        def give(t, carry):
            kk = lax.rem(t + 1, NY)
            yy = yo(kk)
            for j in range(G):
                gro[h, yy, :, j * HD : (j + 1) * HD] = dot_t[h, yy, :, j * T : (j + 1) * T].T

            @pl.when(kk > 0)
            def _():
                gr_send(h, kk).start()

            @pl.when(kk == 0)
            def _():
                gr_local(h).start()

            return carry

        lax.fori_loop(0, NY, give, 0)
        return carry

    def near_back(m, carry):
        h = lax.div(m, 2)
        way = lax.rem(m, 2)
        rel = 2 - way
        clear()
        over_chunks(lambda yy: pull_back(h, rel, yy))
        for w in range(2):

            @pl.when(way == w)
            def _(w=w):
                for c in (1, 0):
                    await_ref(rs1.at[h, w, c], r1r.at[h, w, c])
                    store(h, 1 - w, c, w)
                    r2(h, w, c).start()

        return carry

    def own_back(h, carry):
        clear()

        def chunk(t, carry):
            for u in range(2):
                pull_back(h, 0, yo(lax.rem(2 * t + u + 1, NY)))
            for u in range(2):
                kk = lax.rem(2 * t + u + 1, NY)
                yy = yo(kk)
                for j in range(G):
                    part = dqa[h, yy, :, j * T : (j + 1) * T] * FACTOR
                    gqo[h, yy, :, j * HD : (j + 1) * HD] = part.astype(BF16).T

                @pl.when(kk > 0)
                def _(kk=kk):
                    gq_send(h, kk).start()

                @pl.when(kk == 0)
                def _():
                    gq_local(h).start()

            return carry

        lax.fori_loop(0, NY // 2, chunk, 0)
        own[h, 0] = dka[...] * FACTOR
        own[h, 1] = dva[...]
        return carry

    mrc[...] = mrw_scale
    lax.fori_loop(0, H, far_back, 0)

    x = -sign * logits
    term = jnp.maximum(x, 0.0) + jnp.log(1.0 + jnp.exp(-jnp.abs(x)))
    term = jnp.sum(jnp.where(doc_ids == b, 0.0, term), axis=0, keepdims=True)
    lra[b] = jnp.broadcast_to(term, (8, HD))
    for k in range(1, nb):
        send(lra.at[b], lra.at[b], los.at[k - 1], lor.at[k - 1], (bo(k), s))

    def finish_head(h, carry):
        lax.fori_loop(2 * h, 2 * h + 2, near_back, 0)
        return own_back(h, carry)

    lax.fori_loop(0, H, finish_head, 0)

    for k in range(1, nb):
        await_ref(lra.at[bo(nb - k)], lor.at[k - 1])
    loss = lra[0]
    for j in range(1, nb):
        loss = loss + lra[j]
    loss_ref[0, 0] = jnp.sum(loss) * (1.0 / (8 * HD * nb))

    for h in range(H):
        for c, out in ((1, out_gv), (0, out_gk)):
            await_ref(rs2.at[h, 0, c], r2r.at[h, 0, c])
            await_ref(rs2.at[h, 1, c], r2r.at[h, 1, c])
            for p in range(NY):
                valid = lax.broadcasted_iota(jnp.int32, (T, HD), 0) + (p * NZ + zh) * T < length
                x = own[h, c, p * T : (p + 1) * T, :] + rs2[h, 0, c, p].astype(F32) + rs2[h, 1, c, p].astype(F32)
                fin[h, c, p] = jnp.where(valid, x, 0.0).astype(BF16)
            for k in (2, 1, 3):
                yy = yo(k)
                send(fin.at[h, c, yy], out.at[:, col(2 * y + h, HD)], gks.at[h, c, k - 1], gkr.at[h, c, k - 1], ydev(yy))
            lcopy(fin.at[h, c, y], out.at[:, col(2 * y + h, HD)], gkl.at[h, c]).start()

    for h in range(H):
        gq_local(h).wait()
        gr_local(h).wait()
        for k in range(1, NY):
            await_ref(out_gr.at[:, col(2 * yo(NY - k) + h, GW)], grr.at[h, k - 1])
            await_ref(out_gq.at[:, col(2 * yo(NY - k) + h, GW)], gqr.at[h, k - 1])
        for c, out in ((0, out_gk), (1, out_gv)):
            lcopy(fin.at[h, c, y], out.at[:, col(2 * y + h, HD)], gkl.at[h, c]).wait()
            for k in range(1, NY):
                await_ref(out.at[:, col(2 * yo(NY - k) + h, HD)], gkr.at[h, c, k - 1])
    for copy in sends:
        copy.wait_send()
    for h in range(H):
        for way in range(2):
            hop2(h, way).wait_send()
            for c in range(2):
                r1(h, way, c).wait_send()
                r2(h, way, c).wait_send()
        for k in range(1, NY):
            res_copy(h, k).wait_send()
            gr_send(h, k).wait_send()
            gq_send(h, k).wait_send()


def copy_kernel(parts, n, *refs):
    srcs, dsts, bufs, sems = refs[:n], refs[n : 2 * n], refs[2 * n : 3 * n], refs[-1]
    pairs = []
    for i in range(n):
        rows = srcs[i].shape[0] // parts
        for p in range(parts):
            span = pl.ds(p * rows, rows)
            pairs.append(
                (
                    pltpu.make_async_copy(srcs[i].at[span], bufs[i].at[span], sems.at[0, i, p]),
                    pltpu.make_async_copy(bufs[i].at[span], dsts[i].at[span], sems.at[1, i, p]),
                )
            )
    for load, _ in pairs:
        load.start()
    for load, give in pairs:
        load.wait()
        give.start()
    for _, give in pairs:
        give.wait()


def own_buffers(arrays):
    parts = 2
    any_spec = pl.BlockSpec(memory_space=pl.ANY)
    return pl.pallas_call(
        functools.partial(copy_kernel, parts, len(arrays)),
        out_shape=tuple(jax.ShapeDtypeStruct(x.shape, x.dtype) for x in arrays),
        in_specs=[any_spec] * len(arrays),
        out_specs=(any_spec,) * len(arrays),
        scratch_shapes=[pltpu.VMEM(x.shape, x.dtype) for x in arrays]
        + [pltpu.SemaphoreType.DMA((2, len(arrays), parts))],
        compiler_params=pltpu.CompilerParams(vmem_limit_bytes=56 * 1024 * 1024),
        cost_estimate=pl.CostEstimate(flops=0, bytes_accessed=5 * 2**20, transcendentals=0),
        name="copy_out",
    )(*arrays)


def on_device(nb, residual, query_proj, key_proj, value_proj, norm_gain, lengths, positives):
    T, D = residual.shape
    BK, QC, NG = NY * T, G * T, H * G
    V = pltpu.VMEM
    S = pltpu.SemaphoreType.DMA
    columns = V((H, NY, T, GW), BF16)
    scratch = [
        V(key_proj.shape, BF16), V(key_proj.shape, BF16), V((T, D), BF16), V((T, D), BF16),
        V((H, NZ, 2, NY, T, HD), BF16),
        V((H, NZ, BK, HD), BF16),
        V((H, NZ, HD, BK), BF16),
        V((H, NZ, HD + 16, BK), BF16),
        columns,
        V((H, NY, QC, HD), BF16),
        V((H, NY, HD, QC), BF16),
        V((H, NZ, NY, BK, QC), BF16),
        V((H, NZ, NY, 1, QC), F32),
        V((H, NY, 1, QC), F32),
        V((H, NY, 1, QC), F32),
        V((H, NY, HD + 16, QC), F32),
        columns,
        V((H, NY, HD, QC), F32),
        V((NY, 1, T), F32), V((NY, NY, 1, T), F32), V((NY, 1, T), F32),
        V((NG, HD), F32), V((NZ, NG, HD), F32),
        V((nb, NG, HD), F32),
        V((NY + 1, nb, HD), F32),
        V((nb, 8, HD), F32),
        V((NG, HD, T), F32),
        V((NY, 1, T), F32), V((NY, NY, 1, T), F32), V((NY, 1, T), F32),
        V((H, NY, HD, QC), BF16),
        columns,
        V((H, NY, HD, QC), F32),
        columns,
        V((BK, HD), F32),
        V((BK, HD), F32),
        V((H, 3, 2, NY, T, HD), BF16),
        V((H, 2, BK, HD), F32),
        V((H, 2, 2, 2, T, HD), BF16),
        V((H, 2, 2, NY, T, HD), BF16),
        V((H, 2, NY, T, HD), BF16),
        S((4,)), S((H, 2, NY - 1)), S((H, 2, NY - 1)), S((H, 2)),
        S((H, NY - 1)), S((H, NY - 1)), S((H,)),
        S((H, NY - 1)), S((H, NY - 1)), S((H,)),
        S((H, 2, NY)), S((H, 2, NY)), S((H, 2)), S((H, 2)),
        S((NY - 1,)), S((NY - 1,)), S((NZ - 1,)), S((NZ - 1,)),
        S((nb - 1,)), S((nb - 1,)), S((NY - 1,)), S((NY - 1,)),
        S((nb - 1,)), S((nb - 1,)), S((NY - 1,)), S((NY - 1,)),
        S((H, NY - 1)), S((H, NY - 1)), S((H,)),
        S((H, 2, 2)), S((H, 2, 2)), S((H, 2, 2)), S((H, 2, 2)),
        S((H, NY - 1)), S((H, NY - 1)), S((H,)),
        S((H, 2, NY - 1)), S((H, 2, NY - 1)), S((H, 2)),
    ]
    any_spec = pl.BlockSpec(memory_space=pl.ANY)
    smem = pl.BlockSpec(memory_space=pltpu.SMEM)
    loss, *grads = pl.pallas_call(
        functools.partial(kernel, nb, T),
        out_shape=(
            jax.ShapeDtypeStruct((1, 1), F32),
            jax.ShapeDtypeStruct((T, D), BF16),
            jax.ShapeDtypeStruct((T, D), BF16),
            jax.ShapeDtypeStruct(key_proj.shape, BF16),
            jax.ShapeDtypeStruct(key_proj.shape, BF16),
        ),
        in_specs=[smem, smem, any_spec, any_spec, any_spec, any_spec, pl.BlockSpec(memory_space=pltpu.VMEM)],
        out_specs=(smem, any_spec, any_spec, any_spec, any_spec),
        scratch_shapes=scratch,
        compiler_params=pltpu.CompilerParams(
            collective_id=0, has_side_effects=True, vmem_limit_bytes=56 * 1024 * 1024
        ),
        cost_estimate=pl.CostEstimate(flops=13 * 10**9, bytes_accessed=6 * 2**20, transcendentals=2**23),
        name="attention_backward",
    )(lengths, positives, residual, query_proj, key_proj, value_proj, norm_gain.reshape(NY, NG, HD))
    return loss.reshape(()), *own_buffers(grads)


def solution(mesh):
    rows = P(("batch", "seq"), None)
    return jax.shard_map(
        functools.partial(on_device, mesh.shape["batch"]),
        mesh=mesh,
        in_specs=(rows, rows, rows, rows, P(), P("batch"), P()),
        out_specs=(P(), rows, rows, rows, rows),
        check_vma=False,
    )
```

```python
import functools
import math

import jax
import jax.numpy as jnp
from jax import lax
from jax.experimental import pallas as pl
from jax.experimental.pallas import tpu as pltpu
from jax.sharding import PartitionSpec as P

MESH = pl.DeviceIdType.MESH
HD = 128
NY = 4
NZ = 4
H = 2
G = 4
GW = G * HD
EPS = 1e-6
F32 = jnp.float32
BF16 = jnp.bfloat16
FACTOR = 1.0 / math.sqrt(HD)
LOG2E_FACTOR = FACTOR * math.log2(math.e)


def dot(a, b, dims=((1,), (0,))):
    return lax.dot_general(a, b, (dims, ((), ())), preferred_element_type=F32)


def kernel(
    nb, t_rows,
    len_ref, pos_ref, res_hbm, q_hbm, k_hbm, v_hbm, gain_ref,
    loss_ref, out_gr, out_gq, out_gk, out_gv,
    k_buf, v_buf, q_buf, res_buf, kvb, kfx, kzt, vta, qin, qs, qt, est, mb, mrun, linv, acc, rin, smt,
    rsq, rsa, invr, pz, pza, emba, sga, lra, gbt, mrw, msa, mrc, dot_t, gro, dqa, gqo, dka, dva, dkvo, own, rs1, rs2, fin,
    lds, kvs, kvr, kvl, qss, qsr, qsl, rns, rnr, rnl, z1s, z1r, z2s, z2r,
    sqs, sqr, pzs, pzr, ems, emr, sis, sir, los, lor, mns, mnr,
    grs, grr, grl, r1s, r1r, r2s, r2r, gqs, gqr, gql, gks, gkr, gkl,
):
    T = t_rows
    BK = NY * T
    NG = H * G
    b = lax.axis_index("batch")
    s = lax.axis_index("seq")
    y = lax.div(s, NZ)
    zh = lax.rem(s, NZ)
    right = (b, y * NZ + lax.rem(zh + 1, NZ))
    left = (b, y * NZ + lax.rem(zh + NZ - 1, NZ))

    def yo(k):
        return lax.rem(y + k, NY)

    def zo(k):
        return lax.rem(zh + k, NZ)

    def bo(k):
        return lax.rem(b + k, nb)

    def ydev(yy):
        return (b, yy * NZ + zh)

    def zdev(zz):
        return (b, y * NZ + zz)

    def col(index, width):
        return pl.ds(pl.multiple_of(index * width, width), width)

    def rcopy(src, dst, ssem, rsem, dev):
        return pltpu.make_async_remote_copy(
            src_ref=src, dst_ref=dst, send_sem=ssem, recv_sem=rsem, device_id=dev, device_id_type=MESH
        )

    def lcopy(src, dst, sem):
        return pltpu.make_async_copy(src, dst, sem)

    def await_ref(ref, sem):
        pltpu.make_async_copy(ref, ref, sem).wait()

    sends = []

    def send(src, dst, ssem, rsem, dev):
        copy = rcopy(src, dst, ssem, rsem, dev)
        copy.start()
        sends.append(copy)

    length = len_ref[0]
    lenf = length.astype(F32)

    loads = [
        lcopy(src, dst, lds.at[i])
        for i, (src, dst) in enumerate(((k_hbm, k_buf), (v_hbm, v_buf), (q_hbm, q_buf), (res_hbm, res_buf)))
    ]
    for load in loads:
        load.start()

    barrier = pltpu.get_barrier_semaphore()
    for k in range(1, NY):
        pl.semaphore_signal(barrier, inc=1, device_id=ydev(yo(k)), device_id_type=MESH)
    for k in range(1, NZ):
        pl.semaphore_signal(barrier, inc=1, device_id=zdev(zo(k)), device_id_type=MESH)
    for k in range(1, nb):
        pl.semaphore_signal(barrier, inc=1, device_id=(bo(k), s), device_id_type=MESH)
    pl.semaphore_wait(barrier, NY - 1 + NZ - 1 + nb - 1)

    for load in loads:
        load.wait()
    def kv_sends(h):
        for c, src in ((0, k_buf), (1, v_buf)):
            lcopy(src.at[:, col(2 * y + h, HD)], kvb.at[h, 0, c, y], kvl.at[h, c]).start()
            for k in (1, 3, 2):
                yy = yo(k)
                send(src.at[:, col(2 * yy + h, HD)], kvb.at[h, 0, c, y], kvs.at[h, c, k - 1], kvr.at[h, c, k - 1], ydev(yy))

    def q_send(h, k):
        yy = yo(k)
        send(q_buf.at[:, col(2 * yy + h, GW)], qin.at[h, y], qss.at[h, k - 1], qsr.at[h, k - 1], ydev(yy))

    def res_copy(h, k):
        yy = yo(k)
        return rcopy(res_buf.at[:, col(2 * yy + h, GW)], rin.at[h, y], rns.at[h, k - 1], rnr.at[h, k - 1], ydev(yy))

    def hop1(h, k):
        p = yo(NY - k)
        for c, src in ((0, k_buf), (1, v_buf)):
            if k == 0:
                lcopy(src.at[:, col(2 * y + h, HD)], kvb.at[h, 0, c, y], kvl.at[h, c]).wait()
            else:
                await_ref(kvb.at[h, 0, c, p], kvr.at[h, c, k - 1])
        send(kvb.at[h, 0, :, p], kvb.at[h, 1, :, p], z1s.at[h, 0, k], z1r.at[h, 0, k], right)
        send(kvb.at[h, 0, :, p], kvb.at[h, 2, :, p], z1s.at[h, 1, k], z1r.at[h, 1, k], left)

    kv_sends(0)
    kv_sends(1)
    for h in range(H):
        lcopy(q_buf.at[:, col(2 * y + h, GW)], qin.at[h, y], qsl.at[h]).start()
        lcopy(res_buf.at[:, col(2 * y + h, GW)], rin.at[h, y], rnl.at[h]).start()
        hop1(h, 0)
        for k in (1, 3, 2):
            q_send(h, k)
            hop1(h, k)

    def hop2(h, way):
        src, dev, piece = (1, right, 0) if way == 0 else (2, left, 2)
        return rcopy(
            kvb.at[h, src, :, pl.ds(piece, 2)], kvb.at[h, 3, :, pl.ds(piece, 2)], z2s.at[h, way], z2r.at[h, way], dev
        )

    def forward_hops(h):
        for way in range(2):
            for k in range(NY):
                await_ref(kvb.at[h, 1 + way, :, yo(NY - k)], z1r.at[h, way, k])
            hop2(h, way).start()

    def await_columns(h, src, dst, lsem, rsem):
        lcopy(src.at[:, col(2 * y + h, GW)], dst.at[h, y], lsem.at[h]).wait()
        for k in range(1, NY):
            await_ref(dst.at[h, yo(NY - k)], rsem.at[h, k - 1])

    def prep_q(h):
        def body(yy, carry):
            for j in range(G):
                head = qin[h, yy, :, j * HD : (j + 1) * HD]
                qs[h, yy, j * T : (j + 1) * T, :] = head
                qt[h, yy, :, j * T : (j + 1) * T] = head.T
            mrun[h, yy] = jnp.full((1, G * T), -3e38, F32)
            acc[h, yy] = jnp.zeros((HD + 16, G * T), F32)
            return carry

        lax.fori_loop(0, NY, body, 0)

    def prep_res(h):
        def body(yy, carry):
            for j in range(G):
                smt[h, yy, :, j * T : (j + 1) * T] = rin[h, yy, :, j * HD : (j + 1) * HD].T.astype(F32)
            return carry

        lax.fori_loop(0, NY, body, 0)

    def prep_kv(h, rel, zb):
        first_key = kvb[h, rel, 0, 0, 0:1, :].astype(F32)
        for yy in range(NY):
            base = (yy * NZ + zb) * T
            rows = slice(yy * T, (yy + 1) * T)
            kp = kvb[h, rel, 0, yy]
            valid = lax.broadcasted_iota(jnp.int32, (T, HD), 0) + base < length
            kfx[h, rel, rows, :] = jnp.where(valid, kp.astype(F32), first_key).astype(BF16)
            lanes = lax.broadcasted_iota(jnp.int32, (16, T), 1) + base < length
            ones = jnp.where(lanes, 1.0, 0.0).astype(BF16)
            vta[h, rel, HD : HD + 16, rows] = ones
            kzt[h, rel, :, rows] = kp.T * ones[0:1, :]
            vta[h, rel, 0:HD, rows] = kvb[h, rel, 1, yy].T * ones[0:1, :]

    halves = [slice(part * (G * T // 2), (part + 1) * (G * T // 2)) for part in range(2)]

    def attend(h, rel, yy):
        for lanes in halves:
            sc = dot(kfx[h, rel], qt[h, yy, :, lanes])
            m = jnp.max(sc, axis=0, keepdims=True)
            e = jnp.exp2((sc - m) * LOG2E_FACTOR).astype(BF16)
            est[h, rel, yy, :, lanes] = e
            mb[h, rel, yy, :, lanes] = m
            o = dot(vta[h, rel], e)
            mo = mrun[h, yy, :, lanes]
            mn = jnp.maximum(mo, m)
            keep = jnp.exp2((mo - mn) * LOG2E_FACTOR)
            add = jnp.exp2((m - mn) * LOG2E_FACTOR)
            acc[h, yy, :, lanes] = acc[h, yy, :, lanes] * keep + o * add
            mrun[h, yy, :, lanes] = mn

    def over_chunks(body):
        def step(yy, carry):
            body(yy)
            return carry

        lax.fori_loop(0, NY, step, 0, unroll=NY)

    def own_step(h, carry):
        @pl.when(h == 1)
        def _():
            forward_hops(0)
            for k in (1, 3, 2):
                res_copy(0, k).start()

        await_columns(h, q_buf, qin, qsl, qsr)
        prep_q(h)
        prep_kv(h, 0, zh)
        over_chunks(lambda yy: attend(h, 0, yy))
        return carry

    def near_step(m, carry):
        h = lax.div(m, 2)
        rel = 1 + lax.rem(m, 2)

        @pl.when(m == 2)
        def _():
            forward_hops(1)
            for k in (1, 3, 2):
                res_copy(1, k).start()

        prep_kv(h, rel, zo(5 - 2 * rel))
        over_chunks(lambda yy: attend(h, rel, yy))
        return carry

    def far_step(h, carry):
        await_columns(h, res_buf, rin, rnl, rnr)
        prep_res(h)
        for way in range(2):
            await_ref(kvb.at[h, 3, :, pl.ds(2 * way, 2)], z2r.at[h, way])
        prep_kv(h, 3, zo(2))

        def chunk(yy):
            attend(h, 3, yy)
            li = 1.0 / acc[h, yy, HD : HD + 1, :]
            linv[h, yy] = li
            o = acc[h, yy, 0:HD, :] * li
            acc[h, yy, 0:HD, :] = o
            x = smt[h, yy] + o.astype(BF16).astype(F32)
            smt[h, yy] = x
            sq = jnp.sum(x * x, axis=0, keepdims=True)
            rsq[yy] = rsq[yy] + sum(sq[:, j * T : (j + 1) * T] for j in range(G))

        over_chunks(chunk)
        return carry

    rsq[...] = jnp.zeros((NY, 1, T), F32)
    lax.fori_loop(0, H, own_step, 0)
    lax.fori_loop(0, 2 * H, near_step, 0)
    lax.fori_loop(0, H, far_step, 0)

    def sum_along_y(src, gathered, ssem, rsem):
        for k in (2, 1, 3):
            send(src, gathered.at[y], ssem.at[k - 1], rsem.at[k - 1], ydev(yo(k)))
        gathered[y] = src[...]
        for k in (1, 3, 2):
            await_ref(gathered.at[yo(NY - k)], rsem.at[k - 1])
        return (gathered[0] + gathered[1]) + (gathered[2] + gathered[3])

    mean_square = sum_along_y(rsq, rsa, sqs, sqr) * (1.0 / (NY * NG * HD))
    inv = lax.rsqrt(mean_square + EPS)
    lane = lax.broadcasted_iota(jnp.int32, (NY, 1, T), 2)
    chunk_id = lax.broadcasted_iota(jnp.int32, (NY, 1, T), 0)
    live = (chunk_id * NZ + zh) * T + lane < length
    inv = jnp.where(live, inv, 0.0)
    invr[...] = inv

    for h in range(H):
        for j in range(G):
            part = smt[h, 0, :, j * T : (j + 1) * T] * inv[0]
            for yy in range(1, NY):
                part = part + smt[h, yy, :, j * T : (j + 1) * T] * inv[yy]
            pz[h * G + j : h * G + j + 1, :] = jnp.sum(part.T, axis=0, keepdims=True)
    gain = gain_ref[y]
    pz[...] = pz[...] * gain / lenf
    for k in (2, 1, 3):
        send(pz, pza.at[zh], pzs.at[k - 1], pzr.at[k - 1], zdev(zo(k)))
    pza[zh] = pz[...]
    for k in (1, 3, 2):
        await_ref(pza.at[zo(NZ - k)], pzr.at[k - 1])
    mine = (pza[0] + pza[1]) + (pza[2] + pza[3])
    emba[b] = mine
    for k in range(1, nb):
        send(emba.at[b], emba.at[b], ems.at[k - 1], emr.at[k - 1], (bo(k), s))
    for k in range(1, nb):
        await_ref(emba.at[bo(nb - k)], emr.at[k - 1])

    doc_ids = lax.broadcasted_iota(jnp.int32, (nb, HD), 0)
    lane_ids = lax.broadcasted_iota(jnp.int32, (nb, HD), 1)
    dots = jnp.zeros((nb, HD), F32)
    squares = jnp.zeros((nb, HD), F32)
    for j in range(nb):
        row = emba[j]
        dots = jnp.where(doc_ids == j, jnp.sum(row * mine, axis=0, keepdims=True), dots)
        squares = jnp.where(doc_ids == j, jnp.sum(row * row, axis=0, keepdims=True), squares)
    dots = jnp.broadcast_to(jnp.sum(dots, axis=1, keepdims=True), (nb, HD))
    squares = jnp.broadcast_to(jnp.sum(squares, axis=1, keepdims=True), (nb, HD))
    sga[NY] = jnp.where(lane_ids < HD // 2, dots, squares)
    both = sum_along_y(sga.at[NY], sga, sis, sir)
    dots = jnp.broadcast_to(both[:, 0:1], (nb, HD))
    rho = lax.rsqrt(jnp.broadcast_to(both[:, HD // 2 : HD // 2 + 1], (nb, HD)) + EPS)
    row_rho = jnp.broadcast_to(jnp.sum(jnp.where(doc_ids == b, rho, 0.0), axis=0, keepdims=True), (nb, HD))
    sims = dots * rho * row_rho
    logits = 10.0 * sims - 2.0
    posv = jnp.zeros((nb, HD), jnp.int32)
    for j in range(nb):
        posv = jnp.where(doc_ids == j, pos_ref[j], posv)
    sign = jnp.where(doc_ids == pos_ref[b], 1.0, -1.0)

    def pull(label):
        return -10.0 / nb * label / (1.0 + jnp.exp(label * logits))

    pair = pull(sign) + pull(jnp.where(posv == b, 1.0, -1.0))
    pair = jnp.where(doc_ids == b, 0.0, pair) * (16.0 * NY * NZ * T)
    coef = pair * rho * row_rho
    self_coef = row_rho * row_rho * jnp.broadcast_to(jnp.sum(pair * sims, axis=0, keepdims=True), (nb, HD))
    grad = -self_coef[0:1, :] * mine
    for j in range(nb):
        grad = grad + coef[j : j + 1, :] * emba[j]
    gained = grad / lenf * gain

    for i in range(NG):
        gbt[i] = jnp.broadcast_to(gained[i : i + 1, :], (T, HD)).T
    for yy in range(NY):
        part = gbt[0] * smt[0, yy, :, 0:T]
        for i in range(1, NG):
            j = i % G
            part = part + gbt[i] * smt[i // G, yy, :, j * T : (j + 1) * T]
        mrw[yy] = jnp.sum(part, axis=0, keepdims=True)
    mean = sum_along_y(mrw, msa, mns, mnr) * invr[...] * (1.0 / (NY * NG * HD))
    mrw_scale = invr[...] * invr[...] * mean

    def r1(h, way, c):
        dev, piece = (right, 0) if way == 0 else (left, 2)
        return rcopy(
            dkvo.at[h, 2, c, pl.ds(piece, 2)], rs1.at[h, way, c], r1s.at[h, way, c], r1r.at[h, way, c], dev
        )

    def r2(h, way, c):
        dev = right if way == 0 else left
        return rcopy(dkvo.at[h, 1 - way, c], rs2.at[h, way, c], r2s.at[h, way, c], r2r.at[h, way, c], dev)

    def gq_send(h, kk):
        yy = yo(kk)
        return rcopy(gqo.at[h, yy], out_gq.at[:, col(2 * y + h, GW)], gqs.at[h, kk - 1], gqr.at[h, kk - 1], ydev(yy))

    def gq_local(h):
        return lcopy(gqo.at[h, y], out_gq.at[:, col(2 * y + h, GW)], gql.at[h])

    def gr_send(h, kk):
        yy = yo(kk)
        return rcopy(gro.at[h, yy], out_gr.at[:, col(2 * y + h, GW)], grs.at[h, kk - 1], grr.at[h, kk - 1], ydev(yy))

    def gr_local(h):
        return lcopy(gro.at[h, y], out_gr.at[:, col(2 * y + h, GW)], grl.at[h])

    def scaled_grads(h, rel, yy, lanes):
        r = jnp.exp2((mb[h, rel, yy, :, lanes] - mrun[h, yy, :, lanes]) * LOG2E_FACTOR) * linv[h, yy, :, lanes]
        return (dot_t[h, yy, :, lanes].astype(F32) * r).astype(BF16)

    def values_back(h, rel, yy, dos=None):
        if dos is None:
            dos = [scaled_grads(h, rel, yy, lanes) for lanes in halves]
        dva[...] += dot(est[h, rel, yy], jnp.concatenate(dos, axis=1), ((1,), (1,)))

    def keys_back(h, rel, yy):
        vals = kvb[h, rel, 1].reshape(BK, HD)
        dos, scores = [], []
        for lanes in halves:
            do = scaled_grads(h, rel, yy, lanes)
            delta = jnp.sum(do.astype(F32) * acc[h, yy, 0:HD, lanes], axis=0, keepdims=True)
            dp = dot(vals, do)
            ds = est[h, rel, yy, :, lanes] * (dp - delta).astype(BF16)
            dqa[h, yy, :, lanes] += dot(kzt[h, rel], ds)
            dos.append(do)
            scores.append(ds)
        dka[...] += dot(jnp.concatenate(scores, axis=1), qs[h, yy])
        return dos

    def pull_back(h, rel, yy):
        values_back(h, rel, yy, keys_back(h, rel, yy))

    def clear():
        dka[...] = jnp.zeros((BK, HD), F32)
        dva[...] = jnp.zeros((BK, HD), F32)

    def store(h, slot, c, added):
        for p in range(NY):
            x = dva[p * T : (p + 1) * T, :] if c == 1 else dka[p * T : (p + 1) * T, :] * FACTOR
            if added is not None and p // 2 == added:
                x = x + rs1[h, added, c, p % 2].astype(F32)
            dkvo[h, slot, c, p] = x.astype(BF16)

    def far_back(h, carry):
        for yy in range(NY):
            a = jnp.concatenate([invr[yy]] * G, axis=1)
            c = jnp.concatenate([mrc[yy]] * G, axis=1)
            g = jnp.concatenate([gbt[h * G + j] for j in range(G)], axis=1)
            dot_t[h, yy] = (g * a - smt[h, yy] * c).astype(BF16)
            dqa[h, yy] = jnp.zeros((HD, G * T), F32)
        clear()
        over_chunks(lambda yy: values_back(h, 3, yy))
        store(h, 2, 1, None)
        r1(h, 0, 1).start()
        r1(h, 1, 1).start()
        over_chunks(lambda yy: keys_back(h, 3, yy))
        store(h, 2, 0, None)
        r1(h, 0, 0).start()
        r1(h, 1, 0).start()

        def give(t, carry):
            kk = lax.rem(t + 1, NY)
            yy = yo(kk)
            for j in range(G):
                gro[h, yy, :, j * HD : (j + 1) * HD] = dot_t[h, yy, :, j * T : (j + 1) * T].T

            @pl.when(kk > 0)
            def _():
                gr_send(h, kk).start()

            @pl.when(kk == 0)
            def _():
                gr_local(h).start()

            return carry

        lax.fori_loop(0, NY, give, 0)
        return carry

    def near_back(m, carry):
        h = lax.div(m, 2)
        way = lax.rem(m, 2)
        rel = 2 - way
        clear()
        over_chunks(lambda yy: pull_back(h, rel, yy))
        for w in range(2):

            @pl.when(way == w)
            def _(w=w):
                for c in (1, 0):
                    await_ref(rs1.at[h, w, c], r1r.at[h, w, c])
                    store(h, 1 - w, c, w)
                    r2(h, w, c).start()

        return carry

    def own_back(h, carry):
        clear()

        order = (2, 1, 3, 0)
        for kk in order:
            pull_back(h, 0, yo(kk))
        for kk in order:
            yy = yo(kk)
            for j in range(G):
                part = dqa[h, yy, :, j * T : (j + 1) * T] * FACTOR
                gqo[h, yy, :, j * HD : (j + 1) * HD] = part.astype(BF16).T
            if kk > 0:
                gq_send(h, kk).start()
            else:
                gq_local(h).start()

        own[h, 0] = dka[...] * FACTOR
        own[h, 1] = dva[...]
        return carry

    mrc[...] = mrw_scale
    lax.fori_loop(0, H, far_back, 0)

    x = -sign * logits
    term = jnp.maximum(x, 0.0) + jnp.log(1.0 + jnp.exp(-jnp.abs(x)))
    term = jnp.sum(jnp.where(doc_ids == b, 0.0, term), axis=0, keepdims=True)
    lra[b] = jnp.broadcast_to(term, (8, HD))
    for k in range(1, nb):
        send(lra.at[b], lra.at[b], los.at[k - 1], lor.at[k - 1], (bo(k), s))

    def finish_head(h, carry):
        lax.fori_loop(2 * h, 2 * h + 2, near_back, 0)
        return own_back(h, carry)

    lax.fori_loop(0, H, finish_head, 0)

    for k in range(1, nb):
        await_ref(lra.at[bo(nb - k)], lor.at[k - 1])
    loss = lra[0]
    for j in range(1, nb):
        loss = loss + lra[j]
    loss_ref[0, 0] = jnp.sum(loss) * (1.0 / (8 * HD * nb))

    for h in range(H):
        for c, out in ((1, out_gv), (0, out_gk)):
            await_ref(rs2.at[h, 0, c], r2r.at[h, 0, c])
            await_ref(rs2.at[h, 1, c], r2r.at[h, 1, c])
            for p in range(NY):
                valid = lax.broadcasted_iota(jnp.int32, (T, HD), 0) + (p * NZ + zh) * T < length
                x = own[h, c, p * T : (p + 1) * T, :] + rs2[h, 0, c, p].astype(F32) + rs2[h, 1, c, p].astype(F32)
                fin[h, c, p] = jnp.where(valid, x, 0.0).astype(BF16)
            for k in (2, 1, 3):
                yy = yo(k)
                send(fin.at[h, c, yy], out.at[:, col(2 * y + h, HD)], gks.at[h, c, k - 1], gkr.at[h, c, k - 1], ydev(yy))
            lcopy(fin.at[h, c, y], out.at[:, col(2 * y + h, HD)], gkl.at[h, c]).start()

    for h in range(H):
        gq_local(h).wait()
        gr_local(h).wait()
        for k in range(1, NY):
            await_ref(out_gr.at[:, col(2 * yo(NY - k) + h, GW)], grr.at[h, k - 1])
            await_ref(out_gq.at[:, col(2 * yo(NY - k) + h, GW)], gqr.at[h, k - 1])
        for c, out in ((0, out_gk), (1, out_gv)):
            lcopy(fin.at[h, c, y], out.at[:, col(2 * y + h, HD)], gkl.at[h, c]).wait()
            for k in range(1, NY):
                await_ref(out.at[:, col(2 * yo(NY - k) + h, HD)], gkr.at[h, c, k - 1])
    for copy in sends:
        copy.wait_send()
    for h in range(H):
        for way in range(2):
            hop2(h, way).wait_send()
            for c in range(2):
                r1(h, way, c).wait_send()
                r2(h, way, c).wait_send()
        for k in range(1, NY):
            res_copy(h, k).wait_send()
            gr_send(h, k).wait_send()
            gq_send(h, k).wait_send()


def copy_kernel(parts, n, *refs):
    srcs, dsts, bufs, sems = refs[:n], refs[n : 2 * n], refs[2 * n : 3 * n], refs[-1]
    pairs = []
    for i in range(n):
        rows = srcs[i].shape[0] // parts
        for p in range(parts):
            span = pl.ds(p * rows, rows)
            pairs.append(
                (
                    pltpu.make_async_copy(srcs[i].at[span], bufs[i].at[span], sems.at[0, i, p]),
                    pltpu.make_async_copy(bufs[i].at[span], dsts[i].at[span], sems.at[1, i, p]),
                )
            )
    for load, _ in pairs:
        load.start()
    for load, give in pairs:
        load.wait()
        give.start()
    for _, give in pairs:
        give.wait()


def own_buffers(arrays):
    parts = 2
    any_spec = pl.BlockSpec(memory_space=pl.ANY)
    return pl.pallas_call(
        functools.partial(copy_kernel, parts, len(arrays)),
        out_shape=tuple(jax.ShapeDtypeStruct(x.shape, x.dtype) for x in arrays),
        in_specs=[any_spec] * len(arrays),
        out_specs=(any_spec,) * len(arrays),
        scratch_shapes=[pltpu.VMEM(x.shape, x.dtype) for x in arrays]
        + [pltpu.SemaphoreType.DMA((2, len(arrays), parts))],
        compiler_params=pltpu.CompilerParams(vmem_limit_bytes=56 * 1024 * 1024),
        cost_estimate=pl.CostEstimate(flops=0, bytes_accessed=5 * 2**20, transcendentals=0),
        name="copy_out",
    )(*arrays)


def on_device(nb, residual, query_proj, key_proj, value_proj, norm_gain, lengths, positives):
    T, D = residual.shape
    BK, QC, NG = NY * T, G * T, H * G
    V = pltpu.VMEM
    S = pltpu.SemaphoreType.DMA
    columns = V((H, NY, T, GW), BF16)
    scratch = [
        V(key_proj.shape, BF16), V(key_proj.shape, BF16), V((T, D), BF16), V((T, D), BF16),
        V((H, NZ, 2, NY, T, HD), BF16),
        V((H, NZ, BK, HD), BF16),
        V((H, NZ, HD, BK), BF16),
        V((H, NZ, HD + 16, BK), BF16),
        columns,
        V((H, NY, QC, HD), BF16),
        V((H, NY, HD, QC), BF16),
        V((H, NZ, NY, BK, QC), BF16),
        V((H, NZ, NY, 1, QC), F32),
        V((H, NY, 1, QC), F32),
        V((H, NY, 1, QC), F32),
        V((H, NY, HD + 16, QC), F32),
        columns,
        V((H, NY, HD, QC), F32),
        V((NY, 1, T), F32), V((NY, NY, 1, T), F32), V((NY, 1, T), F32),
        V((NG, HD), F32), V((NZ, NG, HD), F32),
        V((nb, NG, HD), F32),
        V((NY + 1, nb, HD), F32),
        V((nb, 8, HD), F32),
        V((NG, HD, T), F32),
        V((NY, 1, T), F32), V((NY, NY, 1, T), F32), V((NY, 1, T), F32),
        V((H, NY, HD, QC), BF16),
        columns,
        V((H, NY, HD, QC), F32),
        columns,
        V((BK, HD), F32),
        V((BK, HD), F32),
        V((H, 3, 2, NY, T, HD), BF16),
        V((H, 2, BK, HD), F32),
        V((H, 2, 2, 2, T, HD), BF16),
        V((H, 2, 2, NY, T, HD), BF16),
        V((H, 2, NY, T, HD), BF16),
        S((4,)), S((H, 2, NY - 1)), S((H, 2, NY - 1)), S((H, 2)),
        S((H, NY - 1)), S((H, NY - 1)), S((H,)),
        S((H, NY - 1)), S((H, NY - 1)), S((H,)),
        S((H, 2, NY)), S((H, 2, NY)), S((H, 2)), S((H, 2)),
        S((NY - 1,)), S((NY - 1,)), S((NZ - 1,)), S((NZ - 1,)),
        S((nb - 1,)), S((nb - 1,)), S((NY - 1,)), S((NY - 1,)),
        S((nb - 1,)), S((nb - 1,)), S((NY - 1,)), S((NY - 1,)),
        S((H, NY - 1)), S((H, NY - 1)), S((H,)),
        S((H, 2, 2)), S((H, 2, 2)), S((H, 2, 2)), S((H, 2, 2)),
        S((H, NY - 1)), S((H, NY - 1)), S((H,)),
        S((H, 2, NY - 1)), S((H, 2, NY - 1)), S((H, 2)),
    ]
    any_spec = pl.BlockSpec(memory_space=pl.ANY)
    smem = pl.BlockSpec(memory_space=pltpu.SMEM)
    loss, *grads = pl.pallas_call(
        functools.partial(kernel, nb, T),
        out_shape=(
            jax.ShapeDtypeStruct((1, 1), F32),
            jax.ShapeDtypeStruct((T, D), BF16),
            jax.ShapeDtypeStruct((T, D), BF16),
            jax.ShapeDtypeStruct(key_proj.shape, BF16),
            jax.ShapeDtypeStruct(key_proj.shape, BF16),
        ),
        in_specs=[smem, smem, any_spec, any_spec, any_spec, any_spec, pl.BlockSpec(memory_space=pltpu.VMEM)],
        out_specs=(smem, any_spec, any_spec, any_spec, any_spec),
        scratch_shapes=scratch,
        compiler_params=pltpu.CompilerParams(
            collective_id=0, has_side_effects=True, vmem_limit_bytes=56 * 1024 * 1024
        ),
        cost_estimate=pl.CostEstimate(flops=13 * 10**9, bytes_accessed=6 * 2**20, transcendentals=2**23),
        name="attention_backward",
    )(lengths, positives, residual, query_proj, key_proj, value_proj, norm_gain.reshape(NY, NG, HD))
    return loss.reshape(()), *own_buffers(grads)


def solution(mesh):
    rows = P(("batch", "seq"), None)
    return jax.shard_map(
        functools.partial(on_device, mesh.shape["batch"]),
        mesh=mesh,
        in_specs=(rows, rows, rows, rows, P(), P("batch"), P()),
        out_specs=(P(), rows, rows, rows, rows),
        check_vma=False,
    )
```

```python
import functools
import math

import jax
import jax.numpy as jnp
from jax import lax
from jax.experimental import pallas as pl
from jax.experimental.pallas import tpu as pltpu
from jax.sharding import PartitionSpec as P

MESH = pl.DeviceIdType.MESH
HD = 128
NY = 4
NZ = 4
H = 2
G = 4
GW = G * HD
EPS = 1e-6
F32 = jnp.float32
BF16 = jnp.bfloat16
FACTOR = 1.0 / math.sqrt(HD)
LOG2E_FACTOR = FACTOR * math.log2(math.e)


def dot(a, b, dims=((1,), (0,))):
    return lax.dot_general(a, b, (dims, ((), ())), preferred_element_type=F32)


def kernel(
    nb, t_rows,
    len_ref, pos_ref, res_hbm, q_hbm, k_hbm, v_hbm, gain_ref,
    loss_ref, out_gr, out_gq, out_gk, out_gv,
    k_buf, v_buf, q_buf, res_buf, kvb, kfx, kzt, vta, qin, qs, qt, est, mb, mrun, linv, acc, rin, smt,
    rsq, rsa, invr, pz, pza, emba, sga, lra, gbt, mrw, msa, mrc, dot_t, gro, dqa, gqo, dka, dva, dkvo, own, rs1, rs2, fin,
    lds, kvs, kvr, kvl, qss, qsr, qsl, rns, rnr, rnl, z1s, z1r, z2s, z2r,
    sqs, sqr, pzs, pzr, ems, emr, sis, sir, los, lor, mns, mnr,
    grs, grr, grl, r1s, r1r, r2s, r2r, gqs, gqr, gql, gks, gkr, gkl, rly, rys, ryr, rfs, rfr,
):
    T = t_rows
    BK = NY * T
    NG = H * G
    b = lax.axis_index("batch")
    s = lax.axis_index("seq")
    y = lax.div(s, NZ)
    zh = lax.rem(s, NZ)
    right = (b, y * NZ + lax.rem(zh + 1, NZ))
    left = (b, y * NZ + lax.rem(zh + NZ - 1, NZ))

    def yo(k):
        return lax.rem(y + k, NY)

    def zo(k):
        return lax.rem(zh + k, NZ)

    def bo(k):
        return lax.rem(b + k, nb)

    def ydev(yy):
        return (b, yy * NZ + zh)

    def zdev(zz):
        return (b, y * NZ + zz)

    def col(index, width):
        return pl.ds(pl.multiple_of(index * width, width), width)

    def rcopy(src, dst, ssem, rsem, dev):
        return pltpu.make_async_remote_copy(
            src_ref=src, dst_ref=dst, send_sem=ssem, recv_sem=rsem, device_id=dev, device_id_type=MESH
        )

    def lcopy(src, dst, sem):
        return pltpu.make_async_copy(src, dst, sem)

    def await_ref(ref, sem):
        pltpu.make_async_copy(ref, ref, sem).wait()

    def half_rows(way):
        return pl.ds(way * (T // 2), T // 2)

    def relay_out(t, h, way, src):
        dev = ydev(yo(1 if way == 0 else NY - 1))
        return rcopy(src, rly.at[t, h, way], rys.at[t, h, way], ryr.at[t, h, way], dev)

    def relay_on(t, h, way, dst):
        dev = ydev(yo(1 if way == 0 else NY - 1))
        return rcopy(rly.at[t, h, way], dst, rfs.at[t, h, way], rfr.at[t, h, way], dev)

    def relay(t, h, place):
        for way in range(2):
            await_ref(rly.at[t, h, way], ryr.at[t, h, way])
            relay_on(t, h, way, place(h, yo(NY - 1 if way == 0 else 1), half_rows(way))).start()

    def await_relayed(t, h, place):
        for way in range(2):
            await_ref(place(h, yo(2), half_rows(way)), rfr.at[t, h, way])

    def q_place(h, yy, rows):
        return qin.at[h, yy, rows]

    def res_place(h, yy, rows):
        return rin.at[h, yy, rows]

    def gr_place(h, yy, rows):
        return out_gr.at[rows, col(2 * yy + h, GW)]

    def gq_place(h, yy, rows):
        return out_gq.at[rows, col(2 * yy + h, GW)]

    sends = []

    def send(src, dst, ssem, rsem, dev):
        copy = rcopy(src, dst, ssem, rsem, dev)
        copy.start()
        sends.append(copy)

    length = len_ref[0]
    lenf = length.astype(F32)

    loads = [
        lcopy(src, dst, lds.at[i])
        for i, (src, dst) in enumerate(((k_hbm, k_buf), (v_hbm, v_buf), (q_hbm, q_buf), (res_hbm, res_buf)))
    ]
    for load in loads:
        load.start()

    barrier = pltpu.get_barrier_semaphore()
    for k in range(1, NY):
        pl.semaphore_signal(barrier, inc=1, device_id=ydev(yo(k)), device_id_type=MESH)
    for k in range(1, NZ):
        pl.semaphore_signal(barrier, inc=1, device_id=zdev(zo(k)), device_id_type=MESH)
    for k in range(1, nb):
        pl.semaphore_signal(barrier, inc=1, device_id=(bo(k), s), device_id_type=MESH)
    pl.semaphore_wait(barrier, NY - 1 + NZ - 1 + nb - 1)

    for load in loads:
        load.wait()
    def kv_sends(h):
        for c, src in ((0, k_buf), (1, v_buf)):
            lcopy(src.at[:, col(2 * y + h, HD)], kvb.at[h, 0, c, y], kvl.at[h, c]).start()
            for k in (1, 3, 2):
                yy = yo(k)
                send(src.at[:, col(2 * yy + h, HD)], kvb.at[h, 0, c, y], kvs.at[h, c, k - 1], kvr.at[h, c, k - 1], ydev(yy))

    def q_send(h, k):
        yy = yo(k)
        if k == 2:
            for way in range(2):
                relay_out(0, h, way, q_buf.at[half_rows(way), col(2 * yy + h, GW)]).start()
            return
        send(q_buf.at[:, col(2 * yy + h, GW)], qin.at[h, y], qss.at[h, k - 1], qsr.at[h, k - 1], ydev(yy))

    def res_copy(h, k):
        yy = yo(k)
        return rcopy(res_buf.at[:, col(2 * yy + h, GW)], rin.at[h, y], rns.at[h, k - 1], rnr.at[h, k - 1], ydev(yy))

    def res_sends(h):
        for k in (1, 3):
            res_copy(h, k).start()
        for way in range(2):
            relay_out(1, h, way, res_buf.at[half_rows(way), col(2 * yo(2) + h, GW)]).start()

    def hop1(h, k):
        p = yo(NY - k)
        for c, src in ((0, k_buf), (1, v_buf)):
            if k == 0:
                lcopy(src.at[:, col(2 * y + h, HD)], kvb.at[h, 0, c, y], kvl.at[h, c]).wait()
            else:
                await_ref(kvb.at[h, 0, c, p], kvr.at[h, c, k - 1])
        send(kvb.at[h, 0, :, p], kvb.at[h, 1, :, p], z1s.at[h, 0, k], z1r.at[h, 0, k], right)
        send(kvb.at[h, 0, :, p], kvb.at[h, 2, :, p], z1s.at[h, 1, k], z1r.at[h, 1, k], left)

    kv_sends(0)
    kv_sends(1)
    for h in range(H):
        lcopy(q_buf.at[:, col(2 * y + h, GW)], qin.at[h, y], qsl.at[h]).start()
        lcopy(res_buf.at[:, col(2 * y + h, GW)], rin.at[h, y], rnl.at[h]).start()
        hop1(h, 0)
        for k in (1, 3, 2):
            q_send(h, k)
            hop1(h, k)

    relay(0, 0, q_place)

    def hop2(h, way):
        src, dev, piece = (1, right, 0) if way == 0 else (2, left, 2)
        return rcopy(
            kvb.at[h, src, :, pl.ds(piece, 2)], kvb.at[h, 3, :, pl.ds(piece, 2)], z2s.at[h, way], z2r.at[h, way], dev
        )

    def forward_hops(h):
        for way in range(2):
            for k in range(NY):
                await_ref(kvb.at[h, 1 + way, :, yo(NY - k)], z1r.at[h, way, k])
            hop2(h, way).start()

    def await_columns(t, h, src, dst, lsem, rsem, place):
        lcopy(src.at[:, col(2 * y + h, GW)], dst.at[h, y], lsem.at[h]).wait()
        for k in (1, 3):
            await_ref(dst.at[h, yo(NY - k)], rsem.at[h, k - 1])
        await_relayed(t, h, place)

    def prep_q(h):
        def body(yy, carry):
            for j in range(G):
                head = qin[h, yy, :, j * HD : (j + 1) * HD]
                qs[h, yy, j * T : (j + 1) * T, :] = head
                qt[h, yy, :, j * T : (j + 1) * T] = head.T
            mrun[h, yy] = jnp.full((1, G * T), -3e38, F32)
            acc[h, yy] = jnp.zeros((HD + 16, G * T), F32)
            return carry

        lax.fori_loop(0, NY, body, 0)

    def prep_res(h):
        def body(yy, carry):
            for j in range(G):
                smt[h, yy, :, j * T : (j + 1) * T] = rin[h, yy, :, j * HD : (j + 1) * HD].T.astype(F32)
            return carry

        lax.fori_loop(0, NY, body, 0)

    def prep_kv(h, rel, zb):
        first_key = kvb[h, rel, 0, 0, 0:1, :].astype(F32)
        for yy in range(NY):
            base = (yy * NZ + zb) * T
            rows = slice(yy * T, (yy + 1) * T)
            kp = kvb[h, rel, 0, yy]
            valid = lax.broadcasted_iota(jnp.int32, (T, HD), 0) + base < length
            kfx[h, rel, rows, :] = jnp.where(valid, kp.astype(F32), first_key).astype(BF16)
            lanes = lax.broadcasted_iota(jnp.int32, (16, T), 1) + base < length
            ones = jnp.where(lanes, 1.0, 0.0).astype(BF16)
            vta[h, rel, HD : HD + 16, rows] = ones
            kzt[h, rel, :, rows] = kp.T * ones[0:1, :]
            vta[h, rel, 0:HD, rows] = kvb[h, rel, 1, yy].T * ones[0:1, :]

    halves = [slice(part * (G * T // 2), (part + 1) * (G * T // 2)) for part in range(2)]

    def attend(h, rel, yy):
        for lanes in halves:
            sc = dot(kfx[h, rel], qt[h, yy, :, lanes])
            m = jnp.max(sc, axis=0, keepdims=True)
            e = jnp.exp2((sc - m) * LOG2E_FACTOR).astype(BF16)
            est[h, rel, yy, :, lanes] = e
            mb[h, rel, yy, :, lanes] = m
            o = dot(vta[h, rel], e)
            mo = mrun[h, yy, :, lanes]
            mn = jnp.maximum(mo, m)
            keep = jnp.exp2((mo - mn) * LOG2E_FACTOR)
            add = jnp.exp2((m - mn) * LOG2E_FACTOR)
            acc[h, yy, :, lanes] = acc[h, yy, :, lanes] * keep + o * add
            mrun[h, yy, :, lanes] = mn

    def over_chunks(body):
        def step(yy, carry):
            body(yy)
            return carry

        lax.fori_loop(0, NY, step, 0, unroll=NY)

    def own_step(h, carry):
        @pl.when(h == 1)
        def _():
            forward_hops(0)
            res_sends(0)

        await_columns(0, h, q_buf, qin, qsl, qsr, q_place)
        prep_q(h)
        prep_kv(h, 0, zh)

        @pl.when(h == 0)
        def _():
            relay(0, 1, q_place)

        over_chunks(lambda yy: attend(h, 0, yy))
        return carry

    def near_step(m, carry):
        h = lax.div(m, 2)
        rel = 1 + lax.rem(m, 2)

        @pl.when(m == 2)
        def _():
            forward_hops(1)
            res_sends(1)
            relay(1, 0, res_place)

        prep_kv(h, rel, zo(5 - 2 * rel))
        over_chunks(lambda yy: attend(h, rel, yy))
        return carry

    def far_step(h, carry):
        @pl.when(h == 0)
        def _():
            relay(1, 1, res_place)

        await_columns(1, h, res_buf, rin, rnl, rnr, res_place)
        prep_res(h)
        for way in range(2):
            await_ref(kvb.at[h, 3, :, pl.ds(2 * way, 2)], z2r.at[h, way])
        prep_kv(h, 3, zo(2))

        def chunk(yy):
            attend(h, 3, yy)
            li = 1.0 / acc[h, yy, HD : HD + 1, :]
            linv[h, yy] = li
            o = acc[h, yy, 0:HD, :] * li
            acc[h, yy, 0:HD, :] = o
            x = smt[h, yy] + o.astype(BF16).astype(F32)
            smt[h, yy] = x
            sq = jnp.sum(x * x, axis=0, keepdims=True)
            rsq[yy] = rsq[yy] + sum(sq[:, j * T : (j + 1) * T] for j in range(G))

        over_chunks(chunk)
        return carry

    rsq[...] = jnp.zeros((NY, 1, T), F32)
    lax.fori_loop(0, H, own_step, 0)
    lax.fori_loop(0, 2 * H, near_step, 0)
    lax.fori_loop(0, H, far_step, 0)

    def sum_along_y(src, gathered, ssem, rsem):
        for k in (2, 1, 3):
            send(src, gathered.at[y], ssem.at[k - 1], rsem.at[k - 1], ydev(yo(k)))
        gathered[y] = src[...]
        for k in (1, 3, 2):
            await_ref(gathered.at[yo(NY - k)], rsem.at[k - 1])
        return (gathered[0] + gathered[1]) + (gathered[2] + gathered[3])

    mean_square = sum_along_y(rsq, rsa, sqs, sqr) * (1.0 / (NY * NG * HD))
    inv = lax.rsqrt(mean_square + EPS)
    lane = lax.broadcasted_iota(jnp.int32, (NY, 1, T), 2)
    chunk_id = lax.broadcasted_iota(jnp.int32, (NY, 1, T), 0)
    live = (chunk_id * NZ + zh) * T + lane < length
    inv = jnp.where(live, inv, 0.0)
    invr[...] = inv

    for h in range(H):
        for j in range(G):
            part = smt[h, 0, :, j * T : (j + 1) * T] * inv[0]
            for yy in range(1, NY):
                part = part + smt[h, yy, :, j * T : (j + 1) * T] * inv[yy]
            pz[h * G + j : h * G + j + 1, :] = jnp.sum(part.T, axis=0, keepdims=True)
    gain = gain_ref[y]
    pz[...] = pz[...] * gain / lenf
    for k in (2, 1, 3):
        send(pz, pza.at[zh], pzs.at[k - 1], pzr.at[k - 1], zdev(zo(k)))
    pza[zh] = pz[...]
    for k in (1, 3, 2):
        await_ref(pza.at[zo(NZ - k)], pzr.at[k - 1])
    mine = (pza[0] + pza[1]) + (pza[2] + pza[3])
    emba[b] = mine
    for k in range(1, nb):
        send(emba.at[b], emba.at[b], ems.at[k - 1], emr.at[k - 1], (bo(k), s))
    for k in range(1, nb):
        await_ref(emba.at[bo(nb - k)], emr.at[k - 1])

    doc_ids = lax.broadcasted_iota(jnp.int32, (nb, HD), 0)
    lane_ids = lax.broadcasted_iota(jnp.int32, (nb, HD), 1)
    dots = jnp.zeros((nb, HD), F32)
    squares = jnp.zeros((nb, HD), F32)
    for j in range(nb):
        row = emba[j]
        dots = jnp.where(doc_ids == j, jnp.sum(row * mine, axis=0, keepdims=True), dots)
        squares = jnp.where(doc_ids == j, jnp.sum(row * row, axis=0, keepdims=True), squares)
    dots = jnp.broadcast_to(jnp.sum(dots, axis=1, keepdims=True), (nb, HD))
    squares = jnp.broadcast_to(jnp.sum(squares, axis=1, keepdims=True), (nb, HD))
    sga[NY] = jnp.where(lane_ids < HD // 2, dots, squares)
    both = sum_along_y(sga.at[NY], sga, sis, sir)
    dots = jnp.broadcast_to(both[:, 0:1], (nb, HD))
    rho = lax.rsqrt(jnp.broadcast_to(both[:, HD // 2 : HD // 2 + 1], (nb, HD)) + EPS)
    row_rho = jnp.broadcast_to(jnp.sum(jnp.where(doc_ids == b, rho, 0.0), axis=0, keepdims=True), (nb, HD))
    sims = dots * rho * row_rho
    logits = 10.0 * sims - 2.0
    posv = jnp.zeros((nb, HD), jnp.int32)
    for j in range(nb):
        posv = jnp.where(doc_ids == j, pos_ref[j], posv)
    sign = jnp.where(doc_ids == pos_ref[b], 1.0, -1.0)

    def pull(label):
        return -10.0 / nb * label / (1.0 + jnp.exp(label * logits))

    pair = pull(sign) + pull(jnp.where(posv == b, 1.0, -1.0))
    pair = jnp.where(doc_ids == b, 0.0, pair) * (16.0 * NY * NZ * T)
    coef = pair * rho * row_rho
    self_coef = row_rho * row_rho * jnp.broadcast_to(jnp.sum(pair * sims, axis=0, keepdims=True), (nb, HD))
    grad = -self_coef[0:1, :] * mine
    for j in range(nb):
        grad = grad + coef[j : j + 1, :] * emba[j]
    gained = grad / lenf * gain

    for i in range(NG):
        gbt[i] = jnp.broadcast_to(gained[i : i + 1, :], (T, HD)).T
    for yy in range(NY):
        part = gbt[0] * smt[0, yy, :, 0:T]
        for i in range(1, NG):
            j = i % G
            part = part + gbt[i] * smt[i // G, yy, :, j * T : (j + 1) * T]
        mrw[yy] = jnp.sum(part, axis=0, keepdims=True)
    mean = sum_along_y(mrw, msa, mns, mnr) * invr[...] * (1.0 / (NY * NG * HD))
    mrw_scale = invr[...] * invr[...] * mean

    def r1(h, way, c):
        dev, piece = (right, 0) if way == 0 else (left, 2)
        return rcopy(
            dkvo.at[h, 2, c, pl.ds(piece, 2)], rs1.at[h, way, c], r1s.at[h, way, c], r1r.at[h, way, c], dev
        )

    def r2(h, way, c):
        dev = right if way == 0 else left
        return rcopy(dkvo.at[h, 1 - way, c], rs2.at[h, way, c], r2s.at[h, way, c], r2r.at[h, way, c], dev)

    def gq_send(h, kk):
        yy = yo(kk)
        return rcopy(gqo.at[h, yy], out_gq.at[:, col(2 * y + h, GW)], gqs.at[h, kk - 1], gqr.at[h, kk - 1], ydev(yy))

    def gq_local(h):
        return lcopy(gqo.at[h, y], out_gq.at[:, col(2 * y + h, GW)], gql.at[h])

    def gr_send(h, kk):
        yy = yo(kk)
        return rcopy(gro.at[h, yy], out_gr.at[:, col(2 * y + h, GW)], grs.at[h, kk - 1], grr.at[h, kk - 1], ydev(yy))

    def gr_local(h):
        return lcopy(gro.at[h, y], out_gr.at[:, col(2 * y + h, GW)], grl.at[h])

    def scaled_grads(h, rel, yy, lanes):
        r = jnp.exp2((mb[h, rel, yy, :, lanes] - mrun[h, yy, :, lanes]) * LOG2E_FACTOR) * linv[h, yy, :, lanes]
        return (dot_t[h, yy, :, lanes].astype(F32) * r).astype(BF16)

    def values_back(h, rel, yy, dos=None):
        if dos is None:
            dos = [scaled_grads(h, rel, yy, lanes) for lanes in halves]
        dva[...] += dot(est[h, rel, yy], jnp.concatenate(dos, axis=1), ((1,), (1,)))

    def keys_back(h, rel, yy):
        vals = kvb[h, rel, 1].reshape(BK, HD)
        dos, scores = [], []
        for lanes in halves:
            do = scaled_grads(h, rel, yy, lanes)
            delta = jnp.sum(do.astype(F32) * acc[h, yy, 0:HD, lanes], axis=0, keepdims=True)
            dp = dot(vals, do)
            ds = est[h, rel, yy, :, lanes] * (dp - delta).astype(BF16)
            dqa[h, yy, :, lanes] += dot(kzt[h, rel], ds)
            dos.append(do)
            scores.append(ds)
        dka[...] += dot(jnp.concatenate(scores, axis=1), qs[h, yy])
        return dos

    def pull_back(h, rel, yy):
        values_back(h, rel, yy, keys_back(h, rel, yy))

    def clear():
        dka[...] = jnp.zeros((BK, HD), F32)
        dva[...] = jnp.zeros((BK, HD), F32)

    def store(h, slot, c, added):
        for p in range(NY):
            x = dva[p * T : (p + 1) * T, :] if c == 1 else dka[p * T : (p + 1) * T, :] * FACTOR
            if added is not None and p // 2 == added:
                x = x + rs1[h, added, c, p % 2].astype(F32)
            dkvo[h, slot, c, p] = x.astype(BF16)

    def far_back(h, carry):
        for yy in range(NY):
            a = jnp.concatenate([invr[yy]] * G, axis=1)
            c = jnp.concatenate([mrc[yy]] * G, axis=1)
            g = jnp.concatenate([gbt[h * G + j] for j in range(G)], axis=1)
            dot_t[h, yy] = (g * a - smt[h, yy] * c).astype(BF16)
            dqa[h, yy] = jnp.zeros((HD, G * T), F32)
        clear()
        over_chunks(lambda yy: values_back(h, 3, yy))
        store(h, 2, 1, None)
        r1(h, 0, 1).start()
        r1(h, 1, 1).start()
        over_chunks(lambda yy: keys_back(h, 3, yy))
        store(h, 2, 0, None)
        r1(h, 0, 0).start()
        r1(h, 1, 0).start()

        for kk in (2, 1, 3, 0):
            yy = yo(kk)
            for j in range(G):
                gro[h, yy, :, j * HD : (j + 1) * HD] = dot_t[h, yy, :, j * T : (j + 1) * T].T
            if kk == 2:
                for way in range(2):
                    relay_out(2, h, way, gro.at[h, yy, half_rows(way)]).start()
            elif kk > 0:
                gr_send(h, kk).start()
            else:
                gr_local(h).start()
        return carry

    def near_back(m, carry):
        h = lax.div(m, 2)
        way = lax.rem(m, 2)
        rel = 2 - way

        @pl.when(m == 2)
        def _():
            relay(2, 0, gr_place)

        @pl.when(m == 3)
        def _():
            relay(2, 1, gr_place)
            relay(3, 0, gq_place)

        clear()
        over_chunks(lambda yy: pull_back(h, rel, yy))
        for w in range(2):

            @pl.when(way == w)
            def _(w=w):
                for c in (1, 0):
                    await_ref(rs1.at[h, w, c], r1r.at[h, w, c])
                    store(h, 1 - w, c, w)
                    r2(h, w, c).start()

        return carry

    def own_back(h, carry):
        clear()

        order = (2, 1, 3, 0)
        for kk in order:
            pull_back(h, 0, yo(kk))
        for kk in order:
            yy = yo(kk)
            for j in range(G):
                part = dqa[h, yy, :, j * T : (j + 1) * T] * FACTOR
                gqo[h, yy, :, j * HD : (j + 1) * HD] = part.astype(BF16).T
            if kk == 2:
                for way in range(2):
                    relay_out(3, h, way, gqo.at[h, yy, half_rows(way)]).start()
            elif kk > 0:
                gq_send(h, kk).start()
            else:
                gq_local(h).start()

        own[h, 0] = dka[...] * FACTOR
        own[h, 1] = dva[...]
        return carry

    mrc[...] = mrw_scale
    lax.fori_loop(0, H, far_back, 0)

    x = -sign * logits
    term = jnp.maximum(x, 0.0) + jnp.log(1.0 + jnp.exp(-jnp.abs(x)))
    term = jnp.sum(jnp.where(doc_ids == b, 0.0, term), axis=0, keepdims=True)
    lra[b] = jnp.broadcast_to(term, (8, HD))
    for k in range(1, nb):
        send(lra.at[b], lra.at[b], los.at[k - 1], lor.at[k - 1], (bo(k), s))

    def finish_head(h, carry):
        lax.fori_loop(2 * h, 2 * h + 2, near_back, 0)
        return own_back(h, carry)

    lax.fori_loop(0, H, finish_head, 0)

    for k in range(1, nb):
        await_ref(lra.at[bo(nb - k)], lor.at[k - 1])
    loss = lra[0]
    for j in range(1, nb):
        loss = loss + lra[j]
    loss_ref[0, 0] = jnp.sum(loss) * (1.0 / (8 * HD * nb))

    for h in range(H):
        if h == H - 1:
            relay(3, h, gq_place)
        for c, out in ((1, out_gv), (0, out_gk)):
            await_ref(rs2.at[h, 0, c], r2r.at[h, 0, c])
            await_ref(rs2.at[h, 1, c], r2r.at[h, 1, c])
            for p in range(NY):
                valid = lax.broadcasted_iota(jnp.int32, (T, HD), 0) + (p * NZ + zh) * T < length
                x = own[h, c, p * T : (p + 1) * T, :] + rs2[h, 0, c, p].astype(F32) + rs2[h, 1, c, p].astype(F32)
                fin[h, c, p] = jnp.where(valid, x, 0.0).astype(BF16)
            for k in (2, 1, 3):
                yy = yo(k)
                send(fin.at[h, c, yy], out.at[:, col(2 * y + h, HD)], gks.at[h, c, k - 1], gkr.at[h, c, k - 1], ydev(yy))
            lcopy(fin.at[h, c, y], out.at[:, col(2 * y + h, HD)], gkl.at[h, c]).start()

    for h in range(H):
        gq_local(h).wait()
        gr_local(h).wait()
        for k in (1, 3):
            await_ref(out_gr.at[:, col(2 * yo(NY - k) + h, GW)], grr.at[h, k - 1])
            await_ref(out_gq.at[:, col(2 * yo(NY - k) + h, GW)], gqr.at[h, k - 1])
        await_relayed(2, h, gr_place)
        await_relayed(3, h, gq_place)
        for c, out in ((0, out_gk), (1, out_gv)):
            lcopy(fin.at[h, c, y], out.at[:, col(2 * y + h, HD)], gkl.at[h, c]).wait()
            for k in range(1, NY):
                await_ref(out.at[:, col(2 * yo(NY - k) + h, HD)], gkr.at[h, c, k - 1])
    for copy in sends:
        copy.wait_send()
    for h in range(H):
        for way in range(2):
            hop2(h, way).wait_send()
            for c in range(2):
                r1(h, way, c).wait_send()
                r2(h, way, c).wait_send()
            for t in range(4):
                relay_out(t, h, way, rly.at[t, h, way]).wait_send()
                relay_on(t, h, way, rly.at[t, h, way]).wait_send()
        for k in (1, 3):
            res_copy(h, k).wait_send()
            gr_send(h, k).wait_send()
            gq_send(h, k).wait_send()


def copy_kernel(parts, n, *refs):
    srcs, dsts, bufs, sems = refs[:n], refs[n : 2 * n], refs[2 * n : 3 * n], refs[-1]
    pairs = []
    for i in range(n):
        rows = srcs[i].shape[0] // parts
        for p in range(parts):
            span = pl.ds(p * rows, rows)
            pairs.append(
                (
                    pltpu.make_async_copy(srcs[i].at[span], bufs[i].at[span], sems.at[0, i, p]),
                    pltpu.make_async_copy(bufs[i].at[span], dsts[i].at[span], sems.at[1, i, p]),
                )
            )
    for load, _ in pairs:
        load.start()
    for load, give in pairs:
        load.wait()
        give.start()
    for _, give in pairs:
        give.wait()


def own_buffers(arrays):
    parts = 2
    any_spec = pl.BlockSpec(memory_space=pl.ANY)
    return pl.pallas_call(
        functools.partial(copy_kernel, parts, len(arrays)),
        out_shape=tuple(jax.ShapeDtypeStruct(x.shape, x.dtype) for x in arrays),
        in_specs=[any_spec] * len(arrays),
        out_specs=(any_spec,) * len(arrays),
        scratch_shapes=[pltpu.VMEM(x.shape, x.dtype) for x in arrays]
        + [pltpu.SemaphoreType.DMA((2, len(arrays), parts))],
        compiler_params=pltpu.CompilerParams(vmem_limit_bytes=56 * 1024 * 1024),
        cost_estimate=pl.CostEstimate(flops=0, bytes_accessed=5 * 2**20, transcendentals=0),
        name="copy_out",
    )(*arrays)


def on_device(nb, residual, query_proj, key_proj, value_proj, norm_gain, lengths, positives):
    T, D = residual.shape
    BK, QC, NG = NY * T, G * T, H * G
    V = pltpu.VMEM
    S = pltpu.SemaphoreType.DMA
    columns = V((H, NY, T, GW), BF16)
    scratch = [
        V(key_proj.shape, BF16), V(key_proj.shape, BF16), V((T, D), BF16), V((T, D), BF16),
        V((H, NZ, 2, NY, T, HD), BF16),
        V((H, NZ, BK, HD), BF16),
        V((H, NZ, HD, BK), BF16),
        V((H, NZ, HD + 16, BK), BF16),
        columns,
        V((H, NY, QC, HD), BF16),
        V((H, NY, HD, QC), BF16),
        V((H, NZ, NY, BK, QC), BF16),
        V((H, NZ, NY, 1, QC), F32),
        V((H, NY, 1, QC), F32),
        V((H, NY, 1, QC), F32),
        V((H, NY, HD + 16, QC), F32),
        columns,
        V((H, NY, HD, QC), F32),
        V((NY, 1, T), F32), V((NY, NY, 1, T), F32), V((NY, 1, T), F32),
        V((NG, HD), F32), V((NZ, NG, HD), F32),
        V((nb, NG, HD), F32),
        V((NY + 1, nb, HD), F32),
        V((nb, 8, HD), F32),
        V((NG, HD, T), F32),
        V((NY, 1, T), F32), V((NY, NY, 1, T), F32), V((NY, 1, T), F32),
        V((H, NY, HD, QC), BF16),
        columns,
        V((H, NY, HD, QC), F32),
        columns,
        V((BK, HD), F32),
        V((BK, HD), F32),
        V((H, 3, 2, NY, T, HD), BF16),
        V((H, 2, BK, HD), F32),
        V((H, 2, 2, 2, T, HD), BF16),
        V((H, 2, 2, NY, T, HD), BF16),
        V((H, 2, NY, T, HD), BF16),
        S((4,)), S((H, 2, NY - 1)), S((H, 2, NY - 1)), S((H, 2)),
        S((H, NY - 1)), S((H, NY - 1)), S((H,)),
        S((H, NY - 1)), S((H, NY - 1)), S((H,)),
        S((H, 2, NY)), S((H, 2, NY)), S((H, 2)), S((H, 2)),
        S((NY - 1,)), S((NY - 1,)), S((NZ - 1,)), S((NZ - 1,)),
        S((nb - 1,)), S((nb - 1,)), S((NY - 1,)), S((NY - 1,)),
        S((nb - 1,)), S((nb - 1,)), S((NY - 1,)), S((NY - 1,)),
        S((H, NY - 1)), S((H, NY - 1)), S((H,)),
        S((H, 2, 2)), S((H, 2, 2)), S((H, 2, 2)), S((H, 2, 2)),
        S((H, NY - 1)), S((H, NY - 1)), S((H,)),
        S((H, 2, NY - 1)), S((H, 2, NY - 1)), S((H, 2)),
        V((4, H, 2, T // 2, GW), BF16),
        S((4, H, 2)), S((4, H, 2)), S((4, H, 2)), S((4, H, 2)),
    ]
    any_spec = pl.BlockSpec(memory_space=pl.ANY)
    smem = pl.BlockSpec(memory_space=pltpu.SMEM)
    loss, *grads = pl.pallas_call(
        functools.partial(kernel, nb, T),
        out_shape=(
            jax.ShapeDtypeStruct((1, 1), F32),
            jax.ShapeDtypeStruct((T, D), BF16),
            jax.ShapeDtypeStruct((T, D), BF16),
            jax.ShapeDtypeStruct(key_proj.shape, BF16),
            jax.ShapeDtypeStruct(key_proj.shape, BF16),
        ),
        in_specs=[smem, smem, any_spec, any_spec, any_spec, any_spec, pl.BlockSpec(memory_space=pltpu.VMEM)],
        out_specs=(smem, any_spec, any_spec, any_spec, any_spec),
        scratch_shapes=scratch,
        compiler_params=pltpu.CompilerParams(
            collective_id=0, has_side_effects=True, vmem_limit_bytes=56 * 1024 * 1024
        ),
        cost_estimate=pl.CostEstimate(flops=13 * 10**9, bytes_accessed=6 * 2**20, transcendentals=2**23),
        name="attention_backward",
    )(lengths, positives, residual, query_proj, key_proj, value_proj, norm_gain.reshape(NY, NG, HD))
    return loss.reshape(()), *own_buffers(grads)


def solution(mesh):
    rows = P(("batch", "seq"), None)
    return jax.shard_map(
        functools.partial(on_device, mesh.shape["batch"]),
        mesh=mesh,
        in_specs=(rows, rows, rows, rows, P(), P("batch"), P()),
        out_specs=(P(), rows, rows, rows, rows),
        check_vma=False,
    )
```

```python
import functools
import math

import jax
import jax.numpy as jnp
from jax import lax
from jax.experimental import pallas as pl
from jax.experimental.pallas import tpu as pltpu
from jax.sharding import PartitionSpec as P

MESH = pl.DeviceIdType.MESH
HD = 128
NY = 4
NZ = 4
H = 2
G = 4
GW = G * HD
EPS = 1e-6
F32 = jnp.float32
BF16 = jnp.bfloat16
FACTOR = 1.0 / math.sqrt(HD)
LOG2E_FACTOR = FACTOR * math.log2(math.e)


def dot(a, b, dims=((1,), (0,))):
    return lax.dot_general(a, b, (dims, ((), ())), preferred_element_type=F32)


def kernel(
    nb, t_rows,
    len_ref, pos_ref, res_hbm, q_hbm, k_hbm, v_hbm, gain_ref,
    loss_ref, out_gr, out_gq, out_gk, out_gv,
    k_buf, v_buf, q_buf, res_buf, kvb, kfx, kzt, vta, qin, qs, qt, est, mb, mrun, linv, acc, rin, smt,
    rsq, rsa, invr, pz, pza, emba, sga, lra, gbt, mrw, msa, mrc, dot_t, gro, dqa, gqo, dka, dva, dkvo, own, rs1, rs2, fin,
    lds, kvs, kvr, kvl, qss, qsr, qsl, rns, rnr, rnl, z1s, z1r, z2s, z2r,
    sqs, sqr, pzs, pzr, ems, emr, sis, sir, los, lor, mns, mnr,
    grs, grr, grl, r1s, r1r, r2s, r2r, gqs, gqr, gql, gks, gkr, gkl,
):
    T = t_rows
    BK = NY * T
    NG = H * G
    b = lax.axis_index("batch")
    s = lax.axis_index("seq")
    y = lax.div(s, NZ)
    zh = lax.rem(s, NZ)
    right = (b, y * NZ + lax.rem(zh + 1, NZ))
    left = (b, y * NZ + lax.rem(zh + NZ - 1, NZ))

    def yo(k):
        return lax.rem(y + k, NY)

    def zo(k):
        return lax.rem(zh + k, NZ)

    def bo(k):
        return lax.rem(b + k, nb)

    def ydev(yy):
        return (b, yy * NZ + zh)

    def zdev(zz):
        return (b, y * NZ + zz)

    def col(index, width):
        return pl.ds(pl.multiple_of(index * width, width), width)

    def rcopy(src, dst, ssem, rsem, dev):
        return pltpu.make_async_remote_copy(
            src_ref=src, dst_ref=dst, send_sem=ssem, recv_sem=rsem, device_id=dev, device_id_type=MESH
        )

    def lcopy(src, dst, sem):
        return pltpu.make_async_copy(src, dst, sem)

    def await_ref(ref, sem):
        pltpu.make_async_copy(ref, ref, sem).wait()

    sends = []

    def send(src, dst, ssem, rsem, dev):
        copy = rcopy(src, dst, ssem, rsem, dev)
        copy.start()
        sends.append(copy)

    length = len_ref[0]
    lenf = length.astype(F32)

    loads = [
        lcopy(src, dst, lds.at[i])
        for i, (src, dst) in enumerate(((k_hbm, k_buf), (v_hbm, v_buf), (q_hbm, q_buf), (res_hbm, res_buf)))
    ]
    for load in loads:
        load.start()

    barrier = pltpu.get_barrier_semaphore()
    for k in range(1, NY):
        pl.semaphore_signal(barrier, inc=1, device_id=ydev(yo(k)), device_id_type=MESH)
    for k in range(1, NZ):
        pl.semaphore_signal(barrier, inc=1, device_id=zdev(zo(k)), device_id_type=MESH)
    for k in range(1, nb):
        pl.semaphore_signal(barrier, inc=1, device_id=(bo(k), s), device_id_type=MESH)
    pl.semaphore_wait(barrier, NY - 1 + NZ - 1 + nb - 1)

    for load in loads:
        load.wait()
    def kv_sends(h):
        for c, src in ((0, k_buf), (1, v_buf)):
            lcopy(src.at[:, col(2 * y + h, HD)], kvb.at[h, 0, c, y], kvl.at[h, c]).start()
            for k in (1, 3, 2):
                yy = yo(k)
                send(src.at[:, col(2 * yy + h, HD)], kvb.at[h, 0, c, y], kvs.at[h, c, k - 1], kvr.at[h, c, k - 1], ydev(yy))

    def q_send(h, k):
        yy = yo(k)
        send(q_buf.at[:, col(2 * yy + h, GW)], qin.at[h, y], qss.at[h, k - 1], qsr.at[h, k - 1], ydev(yy))

    def res_copy(h, k):
        yy = yo(k)
        return rcopy(res_buf.at[:, col(2 * yy + h, GW)], rin.at[h, y], rns.at[h, k - 1], rnr.at[h, k - 1], ydev(yy))

    def hop1(h, k):
        p = yo(NY - k)
        for c, src in ((0, k_buf), (1, v_buf)):
            if k == 0:
                lcopy(src.at[:, col(2 * y + h, HD)], kvb.at[h, 0, c, y], kvl.at[h, c]).wait()
            else:
                await_ref(kvb.at[h, 0, c, p], kvr.at[h, c, k - 1])
        send(kvb.at[h, 0, :, p], kvb.at[h, 1, :, p], z1s.at[h, 0, k], z1r.at[h, 0, k], right)
        send(kvb.at[h, 0, :, p], kvb.at[h, 2, :, p], z1s.at[h, 1, k], z1r.at[h, 1, k], left)

    kv_sends(0)
    kv_sends(1)
    for h in range(H):
        lcopy(q_buf.at[:, col(2 * y + h, GW)], qin.at[h, y], qsl.at[h]).start()
        lcopy(res_buf.at[:, col(2 * y + h, GW)], rin.at[h, y], rnl.at[h]).start()
        hop1(h, 0)
        for k in (1, 3, 2):
            q_send(h, k)
            hop1(h, k)

    def hop2(h, way):
        src, dev, piece = (1, right, 0) if way == 0 else (2, left, 2)
        return rcopy(
            kvb.at[h, src, :, pl.ds(piece, 2)], kvb.at[h, 3, :, pl.ds(piece, 2)], z2s.at[h, way], z2r.at[h, way], dev
        )

    def forward_hops(h):
        for way in range(2):
            for k in range(NY):
                await_ref(kvb.at[h, 1 + way, :, yo(NY - k)], z1r.at[h, way, k])
            hop2(h, way).start()

    def await_columns(h, src, dst, lsem, rsem):
        lcopy(src.at[:, col(2 * y + h, GW)], dst.at[h, y], lsem.at[h]).wait()
        for k in range(1, NY):
            await_ref(dst.at[h, yo(NY - k)], rsem.at[h, k - 1])

    def prep_q(h):
        def body(yy, carry):
            for j in range(G):
                head = qin[h, yy, :, j * HD : (j + 1) * HD]
                qs[h, yy, j * T : (j + 1) * T, :] = head
                qt[h, yy, :, j * T : (j + 1) * T] = head.T
            mrun[h, yy] = jnp.full((1, G * T), -3e38, F32)
            acc[h, yy] = jnp.zeros((HD + 16, G * T), F32)
            return carry

        lax.fori_loop(0, NY, body, 0)

    def prep_res(h):
        def body(yy, carry):
            for j in range(G):
                smt[h, yy, :, j * T : (j + 1) * T] = rin[h, yy, :, j * HD : (j + 1) * HD].T.astype(F32)
            return carry

        lax.fori_loop(0, NY, body, 0)

    def prep_kv(h, rel, zb):
        first_key = kvb[h, rel, 0, 0, 0:1, :].astype(F32)
        for yy in range(NY):
            base = (yy * NZ + zb) * T
            rows = slice(yy * T, (yy + 1) * T)
            kp = kvb[h, rel, 0, yy]
            valid = lax.broadcasted_iota(jnp.int32, (T, HD), 0) + base < length
            kfx[h, rel, rows, :] = jnp.where(valid, kp.astype(F32), first_key).astype(BF16)
            lanes = lax.broadcasted_iota(jnp.int32, (16, T), 1) + base < length
            ones = jnp.where(lanes, 1.0, 0.0).astype(BF16)
            vta[h, rel, HD : HD + 16, rows] = ones
            kzt[h, rel, :, rows] = kp.T * ones[0:1, :]
            vta[h, rel, 0:HD, rows] = kvb[h, rel, 1, yy].T * ones[0:1, :]

    halves = [slice(part * (G * T // 2), (part + 1) * (G * T // 2)) for part in range(2)]

    def attend(h, rel, yy):
        for lanes in halves:
            sc = dot(kfx[h, rel], qt[h, yy, :, lanes])
            m = jnp.max(sc, axis=0, keepdims=True)
            e = jnp.exp2((sc - m) * LOG2E_FACTOR).astype(BF16)
            est[h, rel, yy, :, lanes] = e
            mb[h, rel, yy, :, lanes] = m
            o = dot(vta[h, rel], e)
            mo = mrun[h, yy, :, lanes]
            mn = jnp.maximum(mo, m)
            keep = jnp.exp2((mo - mn) * LOG2E_FACTOR)
            add = jnp.exp2((m - mn) * LOG2E_FACTOR)
            acc[h, yy, :, lanes] = acc[h, yy, :, lanes] * keep + o * add
            mrun[h, yy, :, lanes] = mn

    def over_chunks(body):
        def step(yy, carry):
            body(yy)
            return carry

        lax.fori_loop(0, NY, step, 0, unroll=NY)

    def own_step(h, carry):
        @pl.when(h == 1)
        def _():
            forward_hops(0)
            for k in (1, 3, 2):
                res_copy(0, k).start()

        await_columns(h, q_buf, qin, qsl, qsr)
        prep_q(h)
        prep_kv(h, 0, zh)
        over_chunks(lambda yy: attend(h, 0, yy))
        return carry

    def near_step(m, carry):
        h = lax.div(m, 2)
        rel = 1 + lax.rem(m, 2)

        @pl.when(m == 2)
        def _():
            forward_hops(1)
            for k in (1, 3, 2):
                res_copy(1, k).start()

        prep_kv(h, rel, zo(5 - 2 * rel))
        over_chunks(lambda yy: attend(h, rel, yy))
        return carry

    def far_step(h, carry):
        await_columns(h, res_buf, rin, rnl, rnr)
        prep_res(h)
        for way in range(2):
            await_ref(kvb.at[h, 3, :, pl.ds(2 * way, 2)], z2r.at[h, way])
        prep_kv(h, 3, zo(2))

        def chunk(yy):
            attend(h, 3, yy)
            li = 1.0 / acc[h, yy, HD : HD + 1, :]
            linv[h, yy] = li
            o = acc[h, yy, 0:HD, :] * li
            acc[h, yy, 0:HD, :] = o
            x = smt[h, yy] + o.astype(BF16).astype(F32)
            smt[h, yy] = x
            sq = jnp.sum(x * x, axis=0, keepdims=True)
            rsq[yy] = rsq[yy] + sum(sq[:, j * T : (j + 1) * T] for j in range(G))

        over_chunks(chunk)
        return carry

    rsq[...] = jnp.zeros((NY, 1, T), F32)
    lax.fori_loop(0, H, own_step, 0)
    lax.fori_loop(0, 2 * H, near_step, 0)
    lax.fori_loop(0, H, far_step, 0)

    def sum_along_y(src, gathered, ssem, rsem):
        for k in (2, 1, 3):
            send(src, gathered.at[y], ssem.at[k - 1], rsem.at[k - 1], ydev(yo(k)))
        gathered[y] = src[...]
        for k in (1, 3, 2):
            await_ref(gathered.at[yo(NY - k)], rsem.at[k - 1])
        return (gathered[0] + gathered[1]) + (gathered[2] + gathered[3])

    mean_square = sum_along_y(rsq, rsa, sqs, sqr) * (1.0 / (NY * NG * HD))
    inv = lax.rsqrt(mean_square + EPS)
    lane = lax.broadcasted_iota(jnp.int32, (NY, 1, T), 2)
    chunk_id = lax.broadcasted_iota(jnp.int32, (NY, 1, T), 0)
    live = (chunk_id * NZ + zh) * T + lane < length
    inv = jnp.where(live, inv, 0.0)
    invr[...] = inv

    for h in range(H):
        for j in range(G):
            part = smt[h, 0, :, j * T : (j + 1) * T] * inv[0]
            for yy in range(1, NY):
                part = part + smt[h, yy, :, j * T : (j + 1) * T] * inv[yy]
            pz[h * G + j : h * G + j + 1, :] = jnp.sum(part.T, axis=0, keepdims=True)
    gain = gain_ref[y]
    pz[...] = pz[...] * gain / lenf
    for k in (2, 1, 3):
        send(pz, pza.at[zh], pzs.at[k - 1], pzr.at[k - 1], zdev(zo(k)))
    pza[zh] = pz[...]
    for k in (1, 3, 2):
        await_ref(pza.at[zo(NZ - k)], pzr.at[k - 1])
    mine = (pza[0] + pza[1]) + (pza[2] + pza[3])
    emba[b] = mine
    for k in range(1, nb):
        send(emba.at[b], emba.at[b], ems.at[k - 1], emr.at[k - 1], (bo(k), s))
    for k in range(1, nb):
        await_ref(emba.at[bo(nb - k)], emr.at[k - 1])

    doc_ids = lax.broadcasted_iota(jnp.int32, (nb, HD), 0)
    lane_ids = lax.broadcasted_iota(jnp.int32, (nb, HD), 1)
    dots = jnp.zeros((nb, HD), F32)
    squares = jnp.zeros((nb, HD), F32)
    for j in range(nb):
        row = emba[j]
        dots = jnp.where(doc_ids == j, jnp.sum(row * mine, axis=0, keepdims=True), dots)
        squares = jnp.where(doc_ids == j, jnp.sum(row * row, axis=0, keepdims=True), squares)
    dots = jnp.broadcast_to(jnp.sum(dots, axis=1, keepdims=True), (nb, HD))
    squares = jnp.broadcast_to(jnp.sum(squares, axis=1, keepdims=True), (nb, HD))
    sga[NY] = jnp.where(lane_ids < HD // 2, dots, squares)
    both = sum_along_y(sga.at[NY], sga, sis, sir)
    dots = jnp.broadcast_to(both[:, 0:1], (nb, HD))
    rho = lax.rsqrt(jnp.broadcast_to(both[:, HD // 2 : HD // 2 + 1], (nb, HD)) + EPS)
    row_rho = jnp.broadcast_to(jnp.sum(jnp.where(doc_ids == b, rho, 0.0), axis=0, keepdims=True), (nb, HD))
    sims = dots * rho * row_rho
    logits = 10.0 * sims - 2.0
    posv = jnp.zeros((nb, HD), jnp.int32)
    for j in range(nb):
        posv = jnp.where(doc_ids == j, pos_ref[j], posv)
    sign = jnp.where(doc_ids == pos_ref[b], 1.0, -1.0)

    def pull(label):
        return -10.0 / nb * label / (1.0 + jnp.exp(label * logits))

    pair = pull(sign) + pull(jnp.where(posv == b, 1.0, -1.0))
    pair = jnp.where(doc_ids == b, 0.0, pair) * (16.0 * NY * NZ * T)
    coef = pair * rho * row_rho
    self_coef = row_rho * row_rho * jnp.broadcast_to(jnp.sum(pair * sims, axis=0, keepdims=True), (nb, HD))
    grad = -self_coef[0:1, :] * mine
    for j in range(nb):
        grad = grad + coef[j : j + 1, :] * emba[j]
    gained = grad / lenf * gain

    for i in range(NG):
        gbt[i] = jnp.broadcast_to(gained[i : i + 1, :], (T, HD)).T
    for yy in range(NY):
        part = gbt[0] * smt[0, yy, :, 0:T]
        for i in range(1, NG):
            j = i % G
            part = part + gbt[i] * smt[i // G, yy, :, j * T : (j + 1) * T]
        mrw[yy] = jnp.sum(part, axis=0, keepdims=True)
    mean = sum_along_y(mrw, msa, mns, mnr) * invr[...] * (1.0 / (NY * NG * HD))
    mrw_scale = invr[...] * invr[...] * mean

    def r1(h, way, c):
        dev, piece = (right, 0) if way == 0 else (left, 2)
        return rcopy(
            dkvo.at[h, 2, c, pl.ds(piece, 2)], rs1.at[h, way, c], r1s.at[h, way, c], r1r.at[h, way, c], dev
        )

    def r2(h, way, c):
        dev = right if way == 0 else left
        return rcopy(dkvo.at[h, 1 - way, c], rs2.at[h, way, c], r2s.at[h, way, c], r2r.at[h, way, c], dev)

    def gq_send(h, kk):
        yy = yo(kk)
        return rcopy(gqo.at[h, yy], out_gq.at[:, col(2 * y + h, GW)], gqs.at[h, kk - 1], gqr.at[h, kk - 1], ydev(yy))

    def gq_local(h):
        return lcopy(gqo.at[h, y], out_gq.at[:, col(2 * y + h, GW)], gql.at[h])

    def gr_send(h, kk):
        yy = yo(kk)
        return rcopy(gro.at[h, yy], out_gr.at[:, col(2 * y + h, GW)], grs.at[h, kk - 1], grr.at[h, kk - 1], ydev(yy))

    def gr_local(h):
        return lcopy(gro.at[h, y], out_gr.at[:, col(2 * y + h, GW)], grl.at[h])

    def scaled_grads(h, rel, yy, lanes):
        r = jnp.exp2((mb[h, rel, yy, :, lanes] - mrun[h, yy, :, lanes]) * LOG2E_FACTOR) * linv[h, yy, :, lanes]
        return (dot_t[h, yy, :, lanes].astype(F32) * r).astype(BF16)

    def values_back(h, rel, yy, dos=None):
        if dos is None:
            dos = [scaled_grads(h, rel, yy, lanes) for lanes in halves]
        dva[...] += dot(est[h, rel, yy], jnp.concatenate(dos, axis=1), ((1,), (1,)))

    def keys_back(h, rel, yy):
        vals = kvb[h, rel, 1].reshape(BK, HD)
        dos, scores = [], []
        for lanes in halves:
            do = scaled_grads(h, rel, yy, lanes)
            delta = jnp.sum(do.astype(F32) * acc[h, yy, 0:HD, lanes], axis=0, keepdims=True)
            dp = dot(vals, do)
            ds = est[h, rel, yy, :, lanes] * (dp - delta).astype(BF16)
            dqa[h, yy, :, lanes] += dot(kzt[h, rel], ds)
            dos.append(do)
            scores.append(ds)
        dka[...] += dot(jnp.concatenate(scores, axis=1), qs[h, yy])
        return dos

    def pull_back(h, rel, yy):
        values_back(h, rel, yy, keys_back(h, rel, yy))

    def clear():
        dka[...] = jnp.zeros((BK, HD), F32)
        dva[...] = jnp.zeros((BK, HD), F32)

    def store(h, slot, c, added):
        for p in range(NY):
            x = dva[p * T : (p + 1) * T, :] if c == 1 else dka[p * T : (p + 1) * T, :] * FACTOR
            if added is not None and p // 2 == added:
                x = x + rs1[h, added, c, p % 2].astype(F32)
            dkvo[h, slot, c, p] = x.astype(BF16)

    def far_back(h, carry):
        for yy in range(NY):
            a = jnp.concatenate([invr[yy]] * G, axis=1)
            c = jnp.concatenate([mrc[yy]] * G, axis=1)
            g = jnp.concatenate([gbt[h * G + j] for j in range(G)], axis=1)
            dot_t[h, yy] = (g * a - smt[h, yy] * c).astype(BF16)
            dqa[h, yy] = jnp.zeros((HD, G * T), F32)
        clear()
        over_chunks(lambda yy: values_back(h, 3, yy))
        store(h, 2, 1, None)
        r1(h, 0, 1).start()
        r1(h, 1, 1).start()
        over_chunks(lambda yy: keys_back(h, 3, yy))
        store(h, 2, 0, None)
        r1(h, 0, 0).start()
        r1(h, 1, 0).start()

        def give(t, carry):
            kk = lax.rem(t + 1, NY)
            yy = yo(kk)
            for j in range(G):
                gro[h, yy, :, j * HD : (j + 1) * HD] = dot_t[h, yy, :, j * T : (j + 1) * T].T

            @pl.when(kk > 0)
            def _():
                gr_send(h, kk).start()

            @pl.when(kk == 0)
            def _():
                gr_local(h).start()

            return carry

        lax.fori_loop(0, NY, give, 0)
        return carry

    def near_back(m, carry):
        h = lax.div(m, 2)
        way = lax.rem(m, 2)
        rel = 2 - way
        clear()
        over_chunks(lambda yy: pull_back(h, rel, yy))
        for w in range(2):

            @pl.when(way == w)
            def _(w=w):
                for c in (1, 0):
                    await_ref(rs1.at[h, w, c], r1r.at[h, w, c])
                    store(h, 1 - w, c, w)
                    r2(h, w, c).start()

        return carry

    def own_back(h, carry):
        clear()

        for kk in (2, 1, 3, 0):
            yy = yo(kk)
            pull_back(h, 0, yy)
            for j in range(G):
                part = dqa[h, yy, :, j * T : (j + 1) * T] * FACTOR
                gqo[h, yy, :, j * HD : (j + 1) * HD] = part.astype(BF16).T
            if kk > 0:
                gq_send(h, kk).start()
            else:
                gq_local(h).start()

        own[h, 0] = dka[...] * FACTOR
        own[h, 1] = dva[...]
        return carry

    mrc[...] = mrw_scale
    lax.fori_loop(0, H, far_back, 0)

    x = -sign * logits
    term = jnp.maximum(x, 0.0) + jnp.log(1.0 + jnp.exp(-jnp.abs(x)))
    term = jnp.sum(jnp.where(doc_ids == b, 0.0, term), axis=0, keepdims=True)
    lra[b] = jnp.broadcast_to(term, (8, HD))
    for k in range(1, nb):
        send(lra.at[b], lra.at[b], los.at[k - 1], lor.at[k - 1], (bo(k), s))

    def finish_head(h, carry):
        lax.fori_loop(2 * h, 2 * h + 2, near_back, 0)
        return own_back(h, carry)

    lax.fori_loop(0, H, finish_head, 0)

    for k in range(1, nb):
        await_ref(lra.at[bo(nb - k)], lor.at[k - 1])
    loss = lra[0]
    for j in range(1, nb):
        loss = loss + lra[j]
    loss_ref[0, 0] = jnp.sum(loss) * (1.0 / (8 * HD * nb))

    for h in range(H):
        for c, out in ((1, out_gv), (0, out_gk)):
            await_ref(rs2.at[h, 0, c], r2r.at[h, 0, c])
            await_ref(rs2.at[h, 1, c], r2r.at[h, 1, c])
            for p in range(NY):
                valid = lax.broadcasted_iota(jnp.int32, (T, HD), 0) + (p * NZ + zh) * T < length
                x = own[h, c, p * T : (p + 1) * T, :] + rs2[h, 0, c, p].astype(F32) + rs2[h, 1, c, p].astype(F32)
                fin[h, c, p] = jnp.where(valid, x, 0.0).astype(BF16)
            for k in (2, 1, 3):
                yy = yo(k)
                send(fin.at[h, c, yy], out.at[:, col(2 * y + h, HD)], gks.at[h, c, k - 1], gkr.at[h, c, k - 1], ydev(yy))
            lcopy(fin.at[h, c, y], out.at[:, col(2 * y + h, HD)], gkl.at[h, c]).start()

    for h in range(H):
        gq_local(h).wait()
        gr_local(h).wait()
        for k in range(1, NY):
            await_ref(out_gr.at[:, col(2 * yo(NY - k) + h, GW)], grr.at[h, k - 1])
            await_ref(out_gq.at[:, col(2 * yo(NY - k) + h, GW)], gqr.at[h, k - 1])
        for c, out in ((0, out_gk), (1, out_gv)):
            lcopy(fin.at[h, c, y], out.at[:, col(2 * y + h, HD)], gkl.at[h, c]).wait()
            for k in range(1, NY):
                await_ref(out.at[:, col(2 * yo(NY - k) + h, HD)], gkr.at[h, c, k - 1])
    for copy in sends:
        copy.wait_send()
    for h in range(H):
        for way in range(2):
            hop2(h, way).wait_send()
            for c in range(2):
                r1(h, way, c).wait_send()
                r2(h, way, c).wait_send()
        for k in range(1, NY):
            res_copy(h, k).wait_send()
            gr_send(h, k).wait_send()
            gq_send(h, k).wait_send()


def copy_kernel(parts, n, *refs):
    srcs, dsts, bufs, sems = refs[:n], refs[n : 2 * n], refs[2 * n : 3 * n], refs[-1]
    pairs = []
    for i in range(n):
        rows = srcs[i].shape[0] // parts
        for p in range(parts):
            span = pl.ds(p * rows, rows)
            pairs.append(
                (
                    pltpu.make_async_copy(srcs[i].at[span], bufs[i].at[span], sems.at[0, i, p]),
                    pltpu.make_async_copy(bufs[i].at[span], dsts[i].at[span], sems.at[1, i, p]),
                )
            )
    for load, _ in pairs:
        load.start()
    for load, give in pairs:
        load.wait()
        give.start()
    for _, give in pairs:
        give.wait()


def own_buffers(arrays):
    parts = 2
    any_spec = pl.BlockSpec(memory_space=pl.ANY)
    return pl.pallas_call(
        functools.partial(copy_kernel, parts, len(arrays)),
        out_shape=tuple(jax.ShapeDtypeStruct(x.shape, x.dtype) for x in arrays),
        in_specs=[any_spec] * len(arrays),
        out_specs=(any_spec,) * len(arrays),
        scratch_shapes=[pltpu.VMEM(x.shape, x.dtype) for x in arrays]
        + [pltpu.SemaphoreType.DMA((2, len(arrays), parts))],
        compiler_params=pltpu.CompilerParams(vmem_limit_bytes=56 * 1024 * 1024),
        cost_estimate=pl.CostEstimate(flops=0, bytes_accessed=5 * 2**20, transcendentals=0),
        name="copy_out",
    )(*arrays)


def on_device(nb, residual, query_proj, key_proj, value_proj, norm_gain, lengths, positives):
    T, D = residual.shape
    BK, QC, NG = NY * T, G * T, H * G
    V = pltpu.VMEM
    S = pltpu.SemaphoreType.DMA
    columns = V((H, NY, T, GW), BF16)
    scratch = [
        V(key_proj.shape, BF16), V(key_proj.shape, BF16), V((T, D), BF16), V((T, D), BF16),
        V((H, NZ, 2, NY, T, HD), BF16),
        V((H, NZ, BK, HD), BF16),
        V((H, NZ, HD, BK), BF16),
        V((H, NZ, HD + 16, BK), BF16),
        columns,
        V((H, NY, QC, HD), BF16),
        V((H, NY, HD, QC), BF16),
        V((H, NZ, NY, BK, QC), BF16),
        V((H, NZ, NY, 1, QC), F32),
        V((H, NY, 1, QC), F32),
        V((H, NY, 1, QC), F32),
        V((H, NY, HD + 16, QC), F32),
        columns,
        V((H, NY, HD, QC), F32),
        V((NY, 1, T), F32), V((NY, NY, 1, T), F32), V((NY, 1, T), F32),
        V((NG, HD), F32), V((NZ, NG, HD), F32),
        V((nb, NG, HD), F32),
        V((NY + 1, nb, HD), F32),
        V((nb, 8, HD), F32),
        V((NG, HD, T), F32),
        V((NY, 1, T), F32), V((NY, NY, 1, T), F32), V((NY, 1, T), F32),
        V((H, NY, HD, QC), BF16),
        columns,
        V((H, NY, HD, QC), F32),
        columns,
        V((BK, HD), F32),
        V((BK, HD), F32),
        V((H, 3, 2, NY, T, HD), BF16),
        V((H, 2, BK, HD), F32),
        V((H, 2, 2, 2, T, HD), BF16),
        V((H, 2, 2, NY, T, HD), BF16),
        V((H, 2, NY, T, HD), BF16),
        S((4,)), S((H, 2, NY - 1)), S((H, 2, NY - 1)), S((H, 2)),
        S((H, NY - 1)), S((H, NY - 1)), S((H,)),
        S((H, NY - 1)), S((H, NY - 1)), S((H,)),
        S((H, 2, NY)), S((H, 2, NY)), S((H, 2)), S((H, 2)),
        S((NY - 1,)), S((NY - 1,)), S((NZ - 1,)), S((NZ - 1,)),
        S((nb - 1,)), S((nb - 1,)), S((NY - 1,)), S((NY - 1,)),
        S((nb - 1,)), S((nb - 1,)), S((NY - 1,)), S((NY - 1,)),
        S((H, NY - 1)), S((H, NY - 1)), S((H,)),
        S((H, 2, 2)), S((H, 2, 2)), S((H, 2, 2)), S((H, 2, 2)),
        S((H, NY - 1)), S((H, NY - 1)), S((H,)),
        S((H, 2, NY - 1)), S((H, 2, NY - 1)), S((H, 2)),
    ]
    any_spec = pl.BlockSpec(memory_space=pl.ANY)
    smem = pl.BlockSpec(memory_space=pltpu.SMEM)
    loss, *grads = pl.pallas_call(
        functools.partial(kernel, nb, T),
        out_shape=(
            jax.ShapeDtypeStruct((1, 1), F32),
            jax.ShapeDtypeStruct((T, D), BF16),
            jax.ShapeDtypeStruct((T, D), BF16),
            jax.ShapeDtypeStruct(key_proj.shape, BF16),
            jax.ShapeDtypeStruct(key_proj.shape, BF16),
        ),
        in_specs=[smem, smem, any_spec, any_spec, any_spec, any_spec, pl.BlockSpec(memory_space=pltpu.VMEM)],
        out_specs=(smem, any_spec, any_spec, any_spec, any_spec),
        scratch_shapes=scratch,
        compiler_params=pltpu.CompilerParams(
            collective_id=0, has_side_effects=True, vmem_limit_bytes=56 * 1024 * 1024
        ),
        cost_estimate=pl.CostEstimate(flops=13 * 10**9, bytes_accessed=6 * 2**20, transcendentals=2**23),
        name="attention_backward",
    )(lengths, positives, residual, query_proj, key_proj, value_proj, norm_gain.reshape(NY, NG, HD))
    return loss.reshape(()), *own_buffers(grads)


def solution(mesh):
    rows = P(("batch", "seq"), None)
    return jax.shard_map(
        functools.partial(on_device, mesh.shape["batch"]),
        mesh=mesh,
        in_specs=(rows, rows, rows, rows, P(), P("batch"), P()),
        out_specs=(P(), rows, rows, rows, rows),
        check_vma=False,
    )
```
